32 devices in a mesh: section: 2 (over core), tm: 16 (over z, y, x).
Axes of the slice: x: 2, y: 2, z: 4, core: 2. Of those that a mesh axis runs over, the one named last changes fastest.
Arguments:
- samples: bfloat16 [8, 8192, 512], P(None, 'tm'), may hold values from -6 to 6
- mel: bfloat16 [8, 8192, 80], P(None, 'tm'), may hold values from -6 to 6
- clip_ids: int32 [8, 8192], replicated, may hold values from 0 to 7, never falling along the last dimension, each value on 1 to 4096 neighbouring positions
- valid: int32 [8, 8192], P(None, 'tm'), may hold values 0 or 1
- w_conv: bfloat16 [2, 2, 512, 1024], P('section'), may hold values from -0.1875 to 0.1875
- w_cond: bfloat16 [2, 80, 1024], P('section'), may hold values from -0.625 to 0.625
- b_conv: float32 [2, 1024], P('section'), may hold values from -3 to 3
- w_res: bfloat16 [2, 512, 512], P('section'), may hold values from -0.5 to 0.5
- b_res: float32 [2, 512], P('section'), may hold values from -3 to 3
- w_skip: bfloat16 [2, 512, 512], P('section'), may hold values from -0.5 to 0.5
- b_skip: float32 [2, 512], P('section'), may hold values from -3 to 3
- cot_out: bfloat16 [8, 8192, 512], P(None, 'tm'), may hold values from -6 to 6
- cot_skip: bfloat16 [8, 8192, 512], P(None, 'tm'), may hold values from -6 to 6
Outputs:
- activations: float32 [2, 8, 8192, 512], P('section', None, 'tm')
- skips: float32 [2, 8, 8192, 512], P('section', None, 'tm')
- input_grads: float32 [2, 8, 8192, 512], P('section', None, 'tm')
- grad_w_conv: float32 [2, 2, 512, 1024], P('section', None, None, 'tm')
- grad_w_cond: float32 [2, 80, 1024], P('section', None, 'tm')
- grad_b_conv: float32 [2, 1024], P('section', 'tm')
- grad_w_res: float32 [2, 512, 512], P('section', None, 'tm')
- grad_b_res: float32 [2, 512], P('section', 'tm')
- grad_w_skip: float32 [2, 512, 512], P('section', None, 'tm')
- grad_b_skip: float32 [2, 512], P('section', 'tm')
The draws below stay inside these ranges and needn't reach their ends.
Inputs may be any that keep to these rules, and one draw needn't show every extreme that they name: `clip_ids`: within each micro-batch the clip number never falls; each clip covers 1 to 4096 samples and one covers exactly 4096.
All inputs are finite; a program needn't handle non-finite values. No bound on the sum of `valid` on one device may be relied on, other than what follows from the above.
Results may differ from the reference program's by a relative error of at most 0.007.
Values may be sent and summed in bfloat16 or wider, within the bound.
No kernel may reach another device: no remote copies, remote signals or barrier semaphores. Data moves between devices by JAX's collectives and lax.ppermute only.
A program may use at most 256 MiB of HBM per device.

```python
import math
import jax
import jax.numpy as jnp
import numpy as np
from jax import lax

C = 512
MEL = 80
FIRST_DILATION = 512
MB = 8
CLIPS = 8
TOKENS = 8192
CLIP_MOST = 4096


def plant(drawn, rng, smallest, high):
    longest = drawn.shape.index(max(drawn.shape))
    spots = []
    for shift in (0, 1):
        where = [jax.random.randint(jax.random.fold_in(rng, axis), (), 0, length) for axis, length in enumerate(drawn.shape)]
        where[longest] = (where[longest] + shift) % drawn.shape[longest]
        spots.append(tuple(where))
    return drawn.at[spots[0]].set(smallest).at[spots[1]].set(high)


def block_levels(key, extent, split, low, largest):
    loudness, own = 1.0, jax.random.fold_in(key, 6)
    for dim, parts in split:
        heights = jnp.exp(jax.random.uniform(jax.random.fold_in(own, dim), (parts,), jnp.float32, low / len(split), largest / len(split)))
        loudness = loudness * jnp.repeat(heights, extent[dim] // parts).reshape([-1 if axis == dim else 1 for axis in range(len(extent))])
    return loudness


def length_profile(count, total, limit, skew):
    loads = [(1 << 20) // math.isqrt(grade ** skew) + 1 for grade in range(2, count + 1)]
    rest, counts = total - limit - (count - 1), [1] * (count - 1)
    while rest > 0:
        movable = [i for i in range(count - 1) if counts[i] < limit]
        pool, budget = sum([loads[i] for i in movable]), rest
        for i in movable:
            extra = min(limit - counts[i], max(1, budget * loads[i] // pool), rest)
            counts[i] = counts[i] + extra
            rest = rest - extra
    return np.array([limit] + counts)


def ragged_sizes(rng, amount, total, most, skew):
    if amount == 2:
        one = jax.random.randint(rng, (), max(1, total - most), min(most, total - 1) + 1)
        return jnp.stack([one, total - one])
    lengths = jnp.asarray(length_profile(amount, total, most, skew), jnp.int32)
    couples = (amount - 1) // 2
    giver, taker = lengths[1:1 + 2 * couples:2], lengths[2:2 + 2 * couples:2]
    room = jnp.minimum(giver - 1, most - taker)
    moved = jax.random.randint(jax.random.fold_in(rng, 1), (couples,), 0, 1 << 20) % (room + 1)
    lengths = lengths.at[1:1 + 2 * couples:2].set(giver - moved).at[2:2 + 2 * couples:2].set(taker + moved)
    return lengths[jax.random.permutation(jax.random.fold_in(rng, 2), amount)]


def bell_draw(rng, dims, width, most, pieces=(), dtype=jnp.bfloat16):
    loudness = block_levels(rng, dims, pieces, -0.22, 0.18) if pieces else 1.0
    values = jax.random.normal(rng, dims, jnp.float32) * width * loudness
    return jnp.minimum(jnp.maximum(values, -most), most).astype(dtype)


def setup_inputs(seed: int = 0) -> dict:
    arg_keys = jax.random.split(jax.random.key(seed), 14)
    samples = bell_draw(arg_keys[0], (MB, TOKENS, C), 1.0, 6.0, ((1, 16),))
    mel = bell_draw(arg_keys[1], (MB, TOKENS, MEL), 1.0, 6.0, ((1, 16),))
    clip_ids = jax.vmap(lambda own: jnp.searchsorted(jnp.cumsum(ragged_sizes(own, CLIPS, TOKENS, CLIP_MOST, 1)), jnp.arange(TOKENS), side="right"))(jax.random.split(arg_keys[2], MB)).reshape((MB, TOKENS)).astype(jnp.int32)
    valid = plant((jax.random.randint(arg_keys[3], (MB, TOKENS), 0, 8) < 7).astype(jnp.int32), jax.random.fold_in(arg_keys[3], 1), 0, 1)
    w_conv = bell_draw(arg_keys[4], (2, 2, C, 2 * C), (2 * C) ** -0.5, 0.1875, ((0, 2),))
    w_cond = bell_draw(arg_keys[5], (2, MEL, 2 * C), MEL ** -0.5, 0.625, ((0, 2),))
    b_conv = bell_draw(arg_keys[6], (2, 2 * C), 0.5, 3.0, ((0, 2),), jnp.float32)
    w_res = bell_draw(arg_keys[7], (2, C, C), (C // 4) ** -0.5, 0.5, ((0, 2),))
    b_res = bell_draw(arg_keys[8], (2, C), 0.5, 3.0, ((0, 2),), jnp.float32)
    w_skip = bell_draw(arg_keys[9], (2, C, C), (C // 4) ** -0.5, 0.5, ((0, 2),))
    b_skip = bell_draw(arg_keys[10], (2, C), 0.5, 3.0, ((0, 2),), jnp.float32)
    cot_out = bell_draw(arg_keys[11], (MB, TOKENS, C), 1.0, 6.0, ((1, 16),))
    cot_skip = bell_draw(arg_keys[12], (MB, TOKENS, C), 1.0, 6.0, ((1, 16),))
    return dict(samples=samples, mel=mel, clip_ids=clip_ids, valid=valid, w_conv=w_conv, w_cond=w_cond, b_conv=b_conv, w_res=w_res, b_res=b_res, w_skip=w_skip, b_skip=b_skip, cot_out=cot_out, cot_skip=cot_skip)


@jax.custom_vjp
def low(v):
    return lax.optimization_barrier(v.astype(jnp.bfloat16)).astype(jnp.float32)

@jax.custom_vjp
def low_back(v):
    return v

def low_keep(v):
    return (low(v), None)

def low_pass(kept, grad):
    return (grad,)

def back_keep(v):
    return (v, None)

def back_low(kept, grad):
    return (low(grad),)
low.defvjp(low_keep, low_pass)
low_back.defvjp(back_keep, back_low)

def matmul(left, right):
    return jnp.dot(left, right, precision=lax.Precision.HIGHEST, preferred_element_type=jnp.float32)

def layer_params(stream, spectrum_rows, packed_clips, row_mask, conv_w, cond_w, conv_b, res_w, res_b, skip_w, skip_b, reach):
    kernel_width = stream.shape[1]
    low_stream = low(stream)
    shifted = jnp.concatenate([jnp.zeros((reach, kernel_width), jnp.float32), low_stream[:-reach]], 0)
    backward_pass = jnp.concatenate([jnp.full((reach,), -1, jnp.int32), packed_clips[:-reach]], 0)
    delayed_input = jnp.where((backward_pass == packed_clips)[:, None], shifted, jnp.float32(0.0))
    joined = jnp.concatenate([delayed_input, low_stream], 1)
    pre = matmul(joined, conv_w.reshape(2 * kernel_width, 2 * kernel_width)) + matmul(spectrum_rows, cond_w)
    gate = low_back(pre) + conv_b
    hidden = low(jnp.tanh(gate[:, :kernel_width]) * jax.nn.sigmoid(gate[:, kernel_width:]) * row_mask[:, None])
    res = low_back(matmul(hidden, res_w)) + res_b
    skip = low_back(matmul(hidden, skip_w)) + skip_b
    return (stream + res, skip)

def reference(samples, mel, clip_ids, valid, w_conv, w_cond, b_conv, w_res, b_res, w_skip, b_skip, cot_out, cot_skip):
    params = tuple((p.astype(jnp.float32) for p in (w_conv, w_cond, b_conv, w_res, b_res, w_skip, b_skip)))

    def one(totals, inputs):
        stream, spectrum_rows, packed_clips, row_mask, grad_out, grad_skip = inputs
        stream = stream.astype(jnp.float32)
        spectrum_rows = spectrum_rows.astype(jnp.float32)
        row_mask = row_mask.astype(jnp.float32)
        grad_out = grad_out.astype(jnp.float32)
        grad_skip = grad_skip.astype(jnp.float32)
        first_layer = tuple((p[0] for p in params))
        second = tuple((p[1] for p in params))

        def run_first(layer_input, *packed_params):
            return layer_params(layer_input, spectrum_rows, packed_clips, row_mask, *packed_params, FIRST_DILATION)

        def run_second(layer_input, *packed_params):
            return layer_params(layer_input, spectrum_rows, packed_clips, row_mask, *packed_params, 1)
        (middle, skip_first), back_first = jax.vjp(run_first, stream, *first_layer)
        (final, skip_second), back_second = jax.vjp(run_second, middle, *second)
        grads_second = back_second((grad_out, grad_skip))
        grads_first = back_first((grads_second[0], grad_skip))
        totals = tuple((t + jnp.stack([a, b]) for t, a, b in zip(totals, grads_first[1:], grads_second[1:])))
        outs = (jnp.stack([middle, final]), jnp.stack([skip_first, skip_first + skip_second]), jnp.stack([grads_first[0], grads_second[0]]))
        return (totals, outs)
    zero_padding = tuple((jnp.zeros(p.shape, jnp.float32) for p in params))
    totals, outs = lax.scan(one, zero_padding, (samples, mel, clip_ids, valid, cot_out, cot_skip))
    activations = jnp.transpose(outs[0], (1, 0, 2, 3))
    skips = jnp.transpose(outs[1], (1, 0, 2, 3))
    input_grads = jnp.transpose(outs[2], (1, 0, 2, 3))
    return (activations, skips, input_grads, totals[0], totals[1], totals[2], totals[3], totals[4], totals[5], totals[6])
```

```python
import functools

import jax
import jax.numpy as jnp
from jax import lax
from jax.experimental import pallas as pl
from jax.experimental.pallas import tpu as pltpu
from jax.sharding import PartitionSpec as P

BF16 = jnp.bfloat16
F32 = jnp.float32
EDGE = 16
SIDE = 128
BIAS_ROWS = 16
VMEM_LIMIT = 56 * 1024 * 1024


def shift(axis, by, turns=1):
    devices = lax.axis_size(axis)
    return [(i, i + by) for i in range(devices) if 0 <= i + by < devices]


def nn(left, right):
    return lax.dot_general(left, right, (((1,), (0,)), ((), ())), preferred_element_type=F32)


def nt(left, right):
    return lax.dot_general(left, right, (((1,), (1,)), ((), ())), preferred_element_type=F32)


def tn(left, right):
    return lax.dot_general(left, right, (((0,), (0,)), ((), ())), preferred_element_type=F32)


def sigmoid(v):
    return 0.5 * jnp.tanh(0.5 * v) + 0.5


def tiles(width, step=256):
    return [slice(n, n + step) for n in range(0, width, step)]


def chain_kernel(
    chunk, per, mel_width, section_ref, x_hbm, halo_hbm, side_hbm, edge_hbm, out_cot_hbm, skip_cot_hbm,
    conv_own, conv_other, small_own, small_other, bias_ref, act_in, skip_in,
    act_hbm, skip_hbm, send_hbm, keep_hbm, back_hbm, delayed0_hbm, joined1_hbm, hidden0_hbm, hidden1_hbm,
    dgate0_hbm, dgate1_hbm, grad0_hbm, sums_ref,
    conv, small, arrived, joined0, joined1, grads1, grads0, side, edge, tanh0, sig0, tanh1, sig1, hidden0, hidden1,
    act_f, skip_f, act_b, skip_b, dgate0, dgate1, grad_f, lower, back, sems, out_sems,
):
    del act_in, skip_in
    section = section_ref[0]
    other = 1 - section
    micro = section * per + chunk
    rows, width = arrived.shape
    total = rows + EDGE
    main = slice(0, rows)
    rim = slice(rows, total)
    cond_rows = SIDE

    loads = [
        pltpu.make_async_copy(x_hbm.at[micro], joined0.at[main, width:], sems.at[0]),
        pltpu.make_async_copy(halo_hbm, arrived, sems.at[1]),
        pltpu.make_async_copy(side_hbm.at[chunk], side, sems.at[2]),
        pltpu.make_async_copy(edge_hbm.at[chunk], edge, sems.at[3]),
        pltpu.make_async_copy(conv_own, conv.at[section], sems.at[4]),
        pltpu.make_async_copy(conv_other, conv.at[other], sems.at[5]),
        pltpu.make_async_copy(small_own, small.at[section], sems.at[6]),
        pltpu.make_async_copy(small_other, small.at[other], sems.at[7]),
        pltpu.make_async_copy(out_cot_hbm.at[micro], grads1.at[main, :width], sems.at[8]),
        pltpu.make_async_copy(skip_cot_hbm.at[micro], grads1.at[main, width:], sems.at[9]),
        pltpu.make_async_copy(skip_cot_hbm.at[micro], grads0.at[:, width:], sems.at[10]),
    ]
    for load in loads:
        load.start()
    for load in loads[:4]:
        load.wait()

    stores = []

    def put(source, target):
        copy = pltpu.make_async_copy(source, target, out_sems.at[len(stores)])
        copy.start()
        stores.append(copy)

    place = lax.broadcasted_iota(jnp.int32, (EDGE, width), 0)
    keep0 = side[:, mel_width + 1 : mel_width + 2]
    keep1 = side[:, mel_width + 2 : mel_width + 3]
    valid = side[:, mel_width : mel_width + 1].astype(F32)
    joined0[main, :width] = arrived[...] * keep0[main]
    first = joined0[0:EDGE, width:].astype(F32)
    last = arrived[rows - EDGE : rows, :].astype(F32)
    joined0[rim, :width] = (
        jnp.where(place == 0, first, edge[:, width : 2 * width].astype(F32)).astype(BF16) * keep0[rim]
    )
    joined0[rim, width:] = jnp.where(place == EDGE - 1, last, edge[:, :width].astype(F32)).astype(BF16)
    grads1[rim, :] = edge[:, 2 * width : 4 * width]
    put(joined0.at[main, :width], delayed0_hbm)
    keep1 = keep1.astype(F32)
    keep0 = keep0.astype(F32)

    for load in loads[4:8]:
        load.wait()

    def gates(layer, joined, tanh, sig, hidden, kept):
        for part in tiles(width):
            late = slice(part.start + width, part.stop + width)
            left = (
                nn(joined[...], conv[layer, :, part])
                + nn(side[...], small[layer, :cond_rows, part])
                + bias_ref[layer, 0:1, part]
            )
            right = (
                nn(joined[...], conv[layer, :, late])
                + nn(side[...], small[layer, :cond_rows, late])
                + bias_ref[layer, 0:1, late]
            )
            th = jnp.tanh(left)
            sg = sigmoid(right)
            tanh[:, part] = th[kept]
            sig[:, part] = sg[kept]
            hidden[:, part] = (th * sg * valid).astype(BF16)

    gates(0, joined0, tanh0, sig0, hidden0, main)
    put(hidden0.at[main], hidden0_hbm)
    for part in tiles(width):
        late = slice(part.start + width, part.stop + width)
        stream = (
            joined0[:, late].astype(F32)
            + nn(hidden0[...], small[0, cond_rows:, part])
            + bias_ref[0, 1:2, part]
        )
        low = stream.astype(BF16)
        act_f[0, :, part] = stream[main]
        act_b[0, :, part] = low[main]
        joined1[:, late] = low
        joined1[:, part] = (pltpu.roll(stream, 1, 0) * keep1).astype(BF16)
        skip = nn(hidden0[main], small[0, cond_rows:, late]) + bias_ref[0, 1:2, late]
        skip_f[0, :, part] = skip
        skip_b[0, :, part] = skip.astype(BF16)
    put(joined1.at[main], joined1_hbm)

    gates(1, joined1, tanh1, sig1, hidden1, slice(0, total))
    put(hidden1.at[main], hidden1_hbm)
    for part in tiles(width):
        late = slice(part.start + width, part.stop + width)
        stream = act_f[0, :, part] + (
            nn(hidden1[main], small[1, cond_rows:, part]) + bias_ref[1, 1:2, part]
        )
        act_f[1, :, part] = stream
        act_b[1, :, part] = stream.astype(BF16)
        skip = skip_f[0, :, part] + (
            nn(hidden1[main], small[1, cond_rows:, late]) + bias_ref[1, 1:2, late]
        )
        skip_f[1, :, part] = skip
        skip_b[1, :, part] = skip.astype(BF16)
    put(act_f.at[section], act_hbm.at[micro])
    put(skip_f.at[section], skip_hbm.at[micro])
    put(act_b.at[other], send_hbm.at[0])
    put(skip_b.at[other], send_hbm.at[1])

    for load in loads[8:]:
        load.wait()

    def gate_grads(layer, grads, tanh, sig, dgate, mask):
        for part in tiles(width):
            late = slice(part.start + width, part.stop + width)
            scaled = nt(grads[...], small[layer, cond_rows + part.start : cond_rows + part.stop, :]) * mask
            th = tanh[:, part]
            sg = sig[:, part]
            both = scaled * sg
            left = both * (1.0 - th * th)
            right = both * th * (1.0 - sg)
            sums_ref[layer, 0:1, part] = jnp.sum(left[main], 0, keepdims=True)
            sums_ref[layer, 0:1, late] = jnp.sum(right[main], 0, keepdims=True)
            dgate[:, part] = left.astype(BF16)
            dgate[:, late] = right.astype(BF16)

    gate_grads(1, grads1, tanh1, sig1, dgate1, valid)
    put(dgate1.at[main], dgate1_hbm)
    for part in tiles(width):
        late = slice(part.start + width, part.stop + width)
        early = nt(dgate1[...], conv[1, part, :]) * keep1
        here = nt(dgate1[main], conv[1, late, :])
        outer = grads1[main, part].astype(F32)
        gradient = outer + here + pltpu.roll(early, total - 1, 0)[main]
        low = gradient.astype(BF16)
        grad_f[:, part] = gradient
        grads0[:, part] = low
        lower[1, :, part] = low
        sums_ref[1, 1:2, part] = jnp.sum(outer, 0, keepdims=True)
        sums_ref[0, 1:2, part] = jnp.sum(gradient, 0, keepdims=True)
        skip_sum = jnp.sum(grads0[:, late].astype(F32), 0, keepdims=True)
        sums_ref[1, 1:2, late] = skip_sum
        sums_ref[0, 1:2, late] = skip_sum
    put(grads0.at[:, :width], grad0_hbm)

    gate_grads(0, grads0, tanh0, sig0, dgate0, valid[main])
    put(dgate0, dgate0_hbm)
    for part in tiles(width):
        late = slice(part.start + width, part.stop + width)
        back[:, part] = (nt(dgate0[...], conv[0, part, :]) * keep0[main]).astype(BF16)
        lower[0, :, part] = (grad_f[:, part] + nt(dgate0[...], conv[0, late, :])).astype(BF16)
    put(back, back_hbm)
    put(lower.at[section], keep_hbm)
    put(lower.at[other], send_hbm.at[2])
    for store in stores:
        store.wait()


def chain(chunk, per, mel_width, section, x, halo, side, edge, out_cot, skip_cot, weights, bias, act, skip):
    count, rows, width = x.shape
    total = rows + EDGE
    any_space = pl.BlockSpec(memory_space=pl.ANY)
    vmem = pl.BlockSpec(memory_space=pltpu.VMEM)
    smem = pl.BlockSpec(memory_space=pltpu.SMEM)
    out = lambda *shape: jax.ShapeDtypeStruct(shape, BF16)
    full = jax.ShapeDtypeStruct((count, rows, width), F32)
    reused = [] if act is None else [act, skip]
    aliases = {} if act is None else {12: 0, 13: 1}
    kernel = functools.partial(chain_kernel, chunk, per, mel_width)
    if act is None:
        inner = kernel
        kernel = lambda *refs: inner(*refs[:12], None, None, *refs[12:])
    cond = weights[2].shape[0]
    return pl.pallas_call(
        kernel,
        out_shape=[
            full, full, out(3, rows, width), out(rows, width), out(rows, width),
            out(rows, width), out(rows, 2 * width), out(rows, width), out(rows, width),
            out(rows, 2 * width), out(rows, 2 * width), out(rows, width),
            jax.ShapeDtypeStruct((2, 8, 2 * width), F32),
        ],
        in_specs=[smem] + [any_space] * 10 + [vmem] + [any_space] * len(reused),
        out_specs=[any_space] * 12 + [vmem],
        input_output_aliases=aliases,
        scratch_shapes=[
            pltpu.VMEM((2, 2 * width, 2 * width), BF16),
            pltpu.VMEM((2, cond, 2 * width), BF16),
            pltpu.VMEM((rows, width), BF16),
            pltpu.VMEM((total, 2 * width), BF16),
            pltpu.VMEM((total, 2 * width), BF16),
            pltpu.VMEM((total, 2 * width), BF16),
            pltpu.VMEM((rows, 2 * width), BF16),
            pltpu.VMEM((total, SIDE), BF16),
            pltpu.VMEM((EDGE, 4 * width), BF16),
            pltpu.VMEM((rows, width), F32),
            pltpu.VMEM((rows, width), F32),
            pltpu.VMEM((total, width), F32),
            pltpu.VMEM((total, width), F32),
            pltpu.VMEM((total, width), BF16),
            pltpu.VMEM((total, width), BF16),
            pltpu.VMEM((2, rows, width), F32),
            pltpu.VMEM((2, rows, width), F32),
            pltpu.VMEM((2, rows, width), BF16),
            pltpu.VMEM((2, rows, width), BF16),
            pltpu.VMEM((rows, 2 * width), BF16),
            pltpu.VMEM((total, 2 * width), BF16),
            pltpu.VMEM((rows, width), F32),
            pltpu.VMEM((2, rows, width), BF16),
            pltpu.VMEM((rows, width), BF16),
            pltpu.SemaphoreType.DMA((11,)),
            pltpu.SemaphoreType.DMA((14,)),
        ],
        compiler_params=pltpu.CompilerParams(vmem_limit_bytes=VMEM_LIMIT),
        cost_estimate=pl.CostEstimate(
            flops=26 * total * width * width * 2, bytes_accessed=20 << 20, transcendentals=0
        ),
        name="chain",
    )(section, x, halo, side, edge, out_cot, skip_cot, *weights, bias, *reused)


def weight_kernel(
    per, section_ref, x_hbm, side_hbm, out_cot_hbm, skip_cot_hbm, *refs
):
    delayed0, joined1, hidden0, hidden1, dgate0, dgate1, grad0 = (
        refs[per * i : per * (i + 1)] for i in range(7)
    )
    sums_refs = refs[7 * per : 8 * per]
    keep_hbm, send_hbm = refs[8 * per : 8 * per + 2]
    joined, dgate, hidden, grads, side, acc, blocks, sems, out_sems = refs[8 * per + 2 :]
    section = section_ref[0]
    rows, width = x_hbm.shape[1:]
    half = per * rows // 2
    lanes = blocks.shape[-1]
    turn = lanes // 2
    cond_rows = SIDE

    def loads(layer):
        groups = []
        for chunk in range(per):
            micro = section * per + chunk
            at = slice(chunk * rows, (chunk + 1) * rows)
            sem = sems.at[layer, chunk]
            if layer == 1:
                sources = [
                    (joined1[chunk], joined.at[1, at, :]),
                    (dgate1[chunk], dgate.at[1, at, :]),
                    (hidden1[chunk], hidden.at[1, at, :]),
                    (out_cot_hbm.at[micro], grads.at[1, at, :width]),
                ]
            else:
                sources = [
                    (delayed0[chunk], joined.at[0, at, :width]),
                    (x_hbm.at[micro], joined.at[0, at, width:]),
                    (dgate0[chunk], dgate.at[0, at, :]),
                    (hidden0[chunk], hidden.at[0, at, :]),
                    (grad0[chunk], grads.at[0, at, :width]),
                ]
            sources.append((skip_cot_hbm.at[micro], grads.at[layer, at, width:]))
            if layer == 1:
                sources.append((side_hbm.at[chunk, pl.ds(0, rows)], side.at[at, :]))
            group = [pltpu.make_async_copy(s, d, sem.at[i]) for i, (s, d) in enumerate(sources)]
            groups.append(group)
        return groups

    pending = {1: loads(1), 0: loads(0)}
    for layer in (1, 0):
        for group in pending[layer]:
            for copy in group:
                copy.start()

    place = lax.broadcasted_iota(jnp.int32, (width, lanes), 1)
    outs = []
    for layer in (1, 0):
        for part in range(2):
            span = slice(part * half, (part + 1) * half)
            for group in pending[layer][part * per // 2 : (part + 1) * per // 2]:
                for copy in group:
                    copy.wait()
            for tile in tiles(2 * width):
                conv = tn(joined[layer, span, :], dgate[layer, span, tile])
                cond = tn(side[span, :], dgate[layer, span, tile])
                if part == 0:
                    acc[0 : 2 * width, tile] = conv
                    acc[2 * width : 2 * width + cond_rows, tile] = cond
                else:
                    conv = (conv + acc[0 : 2 * width, tile]).astype(BF16)
                    cond = (cond + acc[2 * width : 2 * width + cond_rows, tile]).astype(BF16)
                    for n in range(tile.start // lanes, tile.stop // lanes):
                        at = slice(n * lanes - tile.start, (n + 1) * lanes - tile.start)
                        blocks[layer, n, 0 : 2 * width, :] = conv[:, at]
                        blocks[layer, n, 2 * width : 2 * width + cond_rows, :] = cond[:, at]
            top = 2 * width + cond_rows
            for tile in tiles(width):
                late = slice(tile.start + width, tile.stop + width)
                res = tn(hidden[layer, span, :], grads[layer, span, tile])
                skip = tn(hidden[layer, span, :], grads[layer, span, late])
                if part == 0:
                    acc[top : top + width, tile] = res
                    acc[top : top + width, late] = skip
                else:
                    res = res + acc[top : top + width, tile]
                    skip = skip + acc[top : top + width, late]
                    for n in range(2 * tile.start // lanes, 2 * tile.stop // lanes):
                        at = slice((n // 2) * lanes - tile.start, (n // 2 + 1) * lanes - tile.start)
                        a, b = res[:, at], skip[:, at]
                        if n % 2:
                            a = pltpu.roll(a, turn, 1)
                        else:
                            b = pltpu.roll(b, turn, 1)
                        blocks[layer, n, top : top + width, :] = jnp.where(place < turn, a, b).astype(BF16)
        sums = sums_refs[0][layer]
        for ref in sums_refs[1:]:
            sums = sums + ref[layer]
        spot = lax.broadcasted_iota(jnp.int32, (8, lanes), 1)
        line = lax.broadcasted_iota(jnp.int32, (8, lanes), 0)
        for n in range(2 * width // lanes):
            bias = sums[:, n * lanes : (n + 1) * lanes]
            a = sums[:, (n // 2) * lanes : (n // 2 + 1) * lanes]
            b = sums[:, width + (n // 2) * lanes : width + (n // 2 + 1) * lanes]
            if n % 2:
                a = pltpu.roll(a, turn, 1)
            else:
                b = pltpu.roll(b, turn, 1)
            both = jnp.where(spot < turn, a, b)
            both = jnp.where(line == 0, bias, jnp.where(line == 1, both, 0.0))
            filled = jnp.concatenate([both, jnp.zeros_like(both)], 0).astype(BF16)
            blocks[layer, n, top + width : top + width + BIAS_ROWS, :] = filled
        mine = section == layer
        copy = pltpu.make_async_copy(blocks.at[layer], keep_hbm, out_sems.at[layer])
        away = pltpu.make_async_copy(blocks.at[layer], send_hbm, out_sems.at[layer])

        @pl.when(mine)
        def _():
            copy.start()

        @pl.when(jnp.logical_not(mine))
        def _():
            away.start()

        outs.append(copy)
    for copy in outs:
        copy.wait()


def weight_sums(per, section, x, side, out_cot, skip_cot, results):
    rows, width = x.shape[1:]
    any_space = pl.BlockSpec(memory_space=pl.ANY)
    vmem = pl.BlockSpec(memory_space=pltpu.VMEM)
    smem = pl.BlockSpec(memory_space=pltpu.SMEM)
    samples = per * rows
    lanes = 128
    height = 3 * width + SIDE + BIAS_ROWS
    shape = jax.ShapeDtypeStruct((2 * width // lanes, height, lanes), BF16)
    operands = [r[i] for i in range(7) for r in results] + [r[7] for r in results]
    return pl.pallas_call(
        functools.partial(weight_kernel, per),
        out_shape=[shape, shape],
        in_specs=[smem] + [any_space] * (4 + 7 * per) + [vmem] * per,
        out_specs=[any_space] * 2,
        scratch_shapes=[
            pltpu.VMEM((2, samples, 2 * width), BF16),
            pltpu.VMEM((2, samples, 2 * width), BF16),
            pltpu.VMEM((2, samples, width), BF16),
            pltpu.VMEM((2, samples, 2 * width), BF16),
            pltpu.VMEM((samples, SIDE), BF16),
            pltpu.VMEM((3 * width + SIDE, 2 * width), F32),
            pltpu.VMEM((2, 2 * width // lanes, height, lanes), BF16),
            pltpu.SemaphoreType.DMA((2, per, 7)),
            pltpu.SemaphoreType.DMA((2,)),
        ],
        compiler_params=pltpu.CompilerParams(vmem_limit_bytes=VMEM_LIMIT),
        cost_estimate=pl.CostEstimate(
            flops=14 * samples * width * width * 2, bytes_accessed=36 << 20, transcendentals=0
        ),
        name="weight_sums",
    )(section, x, side, out_cot, skip_cot, *operands)


def widen_kernel(section_ref, recv_ref, act_in, skip_in, act_ref, skip_ref):
    del section_ref, act_in, skip_in
    act_ref[0] = recv_ref[0].astype(F32)
    skip_ref[0] = recv_ref[1].astype(F32)


def widen(chunk, per, section, received, act, skip):
    count, rows, width = act.shape
    step = rows // 2
    index = lambda i, s: ((1 - s[0]) * per + chunk, i, 0)
    return pl.pallas_call(
        widen_kernel,
        grid_spec=pltpu.PrefetchScalarGridSpec(
            num_scalar_prefetch=1,
            grid=(rows // step,),
            in_specs=[
                pl.BlockSpec((2, step, width), lambda i, s: (0, i, 0)),
                pl.BlockSpec(memory_space=pl.ANY),
                pl.BlockSpec(memory_space=pl.ANY),
            ],
            out_specs=[pl.BlockSpec((1, step, width), index)] * 2,
        ),
        out_shape=[jax.ShapeDtypeStruct(act.shape, F32)] * 2,
        input_output_aliases={2: 0, 3: 1},
        compiler_params=pltpu.CompilerParams(vmem_limit_bytes=VMEM_LIMIT),
        cost_estimate=pl.CostEstimate(flops=0, bytes_accessed=3 << 20, transcendentals=0),
        name="widen",
    )(section, received, act, skip)


def finish_kernel(section_ref, keep_ref, recv_ref, near_ref, far_ref, *refs):
    out_ref = refs[-1]
    which = pl.program_id(0)

    @pl.when(which == 0)
    def _():
        out_ref[0] = keep_ref[...].astype(F32) + near_ref[...].astype(F32)

    @pl.when(which == 1)
    def _():
        out_ref[0] = recv_ref[0].astype(F32) + far_ref[...].astype(F32)


def finish(chunk, per, section, kept, received, near, far, grads, count):
    rows, width = kept.shape
    step = rows // 2
    steps = rows // step
    index = lambda w, i, s: (jnp.where(w == 0, s[0], 1 - s[0]) * per + chunk, i, 0)
    early = lambda w, i, s: (jnp.where(w == 0, i, steps - 1), 0)
    late = lambda w, i, s: (jnp.where(w == 1, i, 0), 0)
    reused = [] if grads is None else [grads]
    return pl.pallas_call(
        finish_kernel,
        grid_spec=pltpu.PrefetchScalarGridSpec(
            num_scalar_prefetch=1,
            grid=(2, steps),
            in_specs=[
                pl.BlockSpec((step, width), early),
                pl.BlockSpec((1, step, width), lambda w, i, s: (2,) + late(w, i, s)),
                pl.BlockSpec((step, width), early),
                pl.BlockSpec((step, width), late),
            ]
            + [pl.BlockSpec(memory_space=pl.ANY)] * len(reused),
            out_specs=pl.BlockSpec((1, step, width), index),
        ),
        out_shape=jax.ShapeDtypeStruct((count, rows, width), F32),
        input_output_aliases={5: 0} if reused else {},
        compiler_params=pltpu.CompilerParams(vmem_limit_bytes=VMEM_LIMIT),
        cost_estimate=pl.CostEstimate(flops=0, bytes_accessed=4 << 20, transcendentals=0),
        name="finish",
    )(section, kept, received, near, far, *reused)


def halve(blocks, axis_bit, bit, pairs):
    away = lax.dynamic_index_in_dim(blocks, 1 - bit, axis_bit, keepdims=False)
    here = lax.dynamic_index_in_dim(blocks, bit, axis_bit, keepdims=False)
    came = lax.ppermute(away, "tm", pairs)
    return (here.astype(F32) + came.astype(F32)).astype(BF16)


def scatter_sums(blocks, width, mel_width):
    parts = lax.axis_size("tm")
    me = lax.axis_index("tm")
    lanes = blocks.shape[-1]
    top = 2 * width + SIDE
    if 2 * width // parts * 2 == lanes and parts == 16:
        flip = lambda mask: [(i, i ^ mask) for i in range(parts)]
        z_high, z_low, y, x = (me // 8) % 2, (me // 4) % 2, (me // 2) % 2, me % 2
        height = blocks.shape[1]
        left = blocks.reshape(2, 2, 2, height, lanes)
        left = halve(left, 2, y, flip(2))
        left = halve(left, 1, z_low, flip(4))
        left = halve(left, 0, z_high, flip(8))
        came = lax.ppermute(left, "tm", flip(1))
        summed = left.astype(F32) + came.astype(F32)
        share = lanes // 2
        quarter = lanes // 4
        body = lax.dynamic_slice_in_dim(summed, x * share, share, 1)
        res = lax.dynamic_slice_in_dim(summed[top:], x * quarter, quarter, 1)
        skip = lax.dynamic_slice_in_dim(summed[top:], lanes // 2 + x * quarter, quarter, 1)
        conv = body[: 2 * width]
        cond = body[2 * width : 2 * width + mel_width]
        b_conv = body[top + width]
        return conv, cond, b_conv, res[:width], res[width + 1], skip[:width], skip[width + 1]
    count = blocks.shape[0]
    flat = lambda part: jnp.moveaxis(part, 0, 1).reshape(part.shape[1], -1)
    scatter = lambda part: lax.psum_scatter(
        part.astype(F32), "tm", scatter_dimension=1, tiled=True
    )
    conv = scatter(flat(blocks[:, : 2 * width]))
    cond = scatter(flat(blocks[:, 2 * width : 2 * width + mel_width]))
    rest = blocks[:, top:]
    res = scatter(flat(rest[:, :, : lanes // 2]))
    skip = scatter(flat(rest[:, :, lanes // 2 :]))
    b_conv = scatter(flat(rest[:, width : width + 1]))
    return conv, cond, b_conv[0], res[:width], res[width + 1], skip[:width], skip[width + 1]


def on_device(
    samples, mel, clip_ids, valid, w_conv, w_cond, b_conv, w_res, b_res, w_skip, b_skip, cot_out, cot_skip
):
    section = lax.axis_index("section")
    position = lax.axis_index("tm")
    count, rows, width = samples.shape
    mel_width = mel.shape[-1]
    per = count // 2
    base = section * per
    own = lambda a: lax.dynamic_slice_in_dim(a, base, per, 0)
    scalar = jnp.reshape(section, (1,)).astype(jnp.int32)
    forward = shift("tm", 1)
    backward = shift("tm", -1)
    swap = [(0, 1), (1, 0)]

    halos = [
        lax.ppermute(lax.dynamic_index_in_dim(samples, base + c, 0, keepdims=False), "tm", forward)
        for c in range(per)
    ]

    conv_own = w_conv[0].reshape(2 * width, 2 * width)
    small_own = jnp.concatenate(
        [
            jnp.pad(w_cond[0], ((0, SIDE - mel_width), (0, 0))),
            jnp.concatenate([w_res[0], w_skip[0]], 1),
        ],
        0,
    )
    bias_own = jnp.concatenate([b_conv, jnp.concatenate([b_res, b_skip], 1)], 0)
    conv_other = lax.ppermute(conv_own, "section", swap)
    small_other = lax.ppermute(small_own, "section", swap)
    bias_other = lax.ppermute(bias_own, "section", swap)
    first_layer = section == 0
    bias = jnp.stack(
        [
            jnp.where(first_layer, bias_own, bias_other),
            jnp.where(first_layer, bias_other, bias_own),
        ]
    )

    padded = jnp.pad(own(clip_ids), ((0, 0), (rows, 0)), constant_values=-1)
    start = position * rows
    now = lax.dynamic_slice_in_dim(padded, start + rows, rows, 1)
    keep0 = now == lax.dynamic_slice_in_dim(padded, start, rows, 1)
    keep1 = now == lax.dynamic_slice_in_dim(padded, start + rows - 1, rows, 1)
    marks = jnp.stack([own(valid).astype(BF16), keep0.astype(BF16), keep1.astype(BF16)], -1)
    side = jnp.concatenate(
        [own(mel), marks, jnp.zeros((per, rows, SIDE - mel_width - 3), BF16)], -1
    )
    heads = jnp.concatenate(
        [own(a)[:, 0] for a in (samples, cot_out, cot_skip)] + [side[:, 0]], -1
    )
    after = lax.ppermute(heads, "tm", backward)
    before = lax.ppermute(side[:, -1], "tm", forward)
    twice = lax.ppermute(own(samples)[:, -1], "tm", shift("tm", 2))
    blank = jnp.zeros((per, EDGE - 2, 4 * width), BF16)
    nothing = jnp.zeros((per, width), BF16)
    edge = jnp.concatenate(
        [
            jnp.concatenate([after[:, :width], nothing, after[:, width : 3 * width]], -1)[:, None],
            blank,
            jnp.concatenate([nothing, twice, nothing, nothing], -1)[:, None],
        ],
        1,
    )
    side = jnp.concatenate(
        [
            side,
            after[:, None, 3 * width :],
            jnp.zeros((per, EDGE - 2, SIDE), BF16),
            before[:, None],
        ],
        1,
    )

    act = skip = None
    results = []
    received = []
    near, far, kept = [], [], []
    sections = [(i, i) for i in range(2)]
    parts = lax.axis_size("tm")
    for c in range(per):
        act, skip, send, keep, back, *rest = chain(
            c, per, mel_width, scalar, samples, halos[c], side, edge, cot_out, cot_skip,
            (conv_own, conv_other, small_own, small_other), bias, act, skip,
        )
        results.append(rest)
        received.append(lax.ppermute(send, "section", swap))
        kept.append(keep)
        axes = ("section", "tm")
        near.append(lax.ppermute(back, axes, [(j + 1, j) for j in range(parts - 1)]))
        far.append(lax.ppermute(back, axes, [(parts + j + 1, j) for j in range(parts - 1)]))

    keep_sums, send_sums = weight_sums(per, scalar, samples, side, cot_out, cot_skip, results)
    came = lax.ppermute(send_sums, "section", swap)
    summed = (keep_sums.astype(F32) + came.astype(F32)).astype(BF16)
    conv, cond, g_conv, res, g_res, skip_w, g_skip = scatter_sums(summed, width, mel_width)

    grads = None
    for c in range(per):
        act, skip = widen(c, per, scalar, received[c], act, skip)
        grads = finish(c, per, scalar, kept[c], received[c], near[c], far[c], grads, count)
    return (
        act[None],
        skip[None],
        grads[None],
        conv.reshape(1, 2, width, -1),
        cond[None],
        g_conv[None],
        res[None],
        g_res[None],
        skip_w[None],
        g_skip[None],
    )


def solution(mesh):
    placed = (
        P(None, "tm", None),
        P(None, "tm", None),
        P(),
        P(None, "tm"),
        P("section", None, None, None),
        P("section", None, None),
        P("section", None),
        P("section", None, None),
        P("section", None),
        P("section", None, None),
        P("section", None),
        P(None, "tm", None),
        P(None, "tm", None),
    )
    return jax.shard_map(
        on_device,
        mesh=mesh,
        in_specs=placed,
        out_specs=(
            P("section", None, "tm", None),
            P("section", None, "tm", None),
            P("section", None, "tm", None),
            P("section", None, None, "tm"),
            P("section", None, "tm"),
            P("section", "tm"),
            P("section", None, "tm"),
            P("section", "tm"),
            P("section", None, "tm"),
            P("section", "tm"),
        ),
        check_vma=False,
    )
```

```python
import functools

import jax
import jax.numpy as jnp
from jax import lax
from jax.experimental import pallas as pl
from jax.experimental.pallas import tpu as pltpu
from jax.sharding import PartitionSpec as P

BF16 = jnp.bfloat16
F32 = jnp.float32
EDGE = 16
SIDE = 128
BIAS_ROWS = 64
CHAIN_SMALL = 16
VMEM_LIMIT = 56 * 1024 * 1024
LONG = pl.CostEstimate(flops=10**12, bytes_accessed=10**9, transcendentals=0)


def shift(axis, by):
    devices = lax.axis_size(axis)
    return [(i, i + by) for i in range(devices) if 0 <= i + by < devices]


def nn(left, right):
    return lax.dot_general(left, right, (((1,), (0,)), ((), ())), preferred_element_type=F32)


def nt(left, right):
    return lax.dot_general(left, right, (((1,), (1,)), ((), ())), preferred_element_type=F32)


def tn(left, right):
    return lax.dot_general(left, right, (((0,), (0,)), ((), ())), preferred_element_type=F32)


def sigmoid(v):
    return 0.5 * jnp.tanh(0.5 * v) + 0.5


def tiles(width, step=256):
    return [slice(n, n + step) for n in range(0, width, step)]


def prep_kernel(
    per, mel_width, place_ref, mel_ref, valid_ref, ids_ref, before_ref, earlier_ref, cond_ref, res_ref, skip_ref,
    b_conv_ref, b_res_ref, b_skip_ref, x_hbm, out_cot_hbm, skip_cot_hbm, conv_hbm, *refs,
):
    pairs = per // 2
    sources = refs[:pairs]
    heads_ref, twice_ref, side_ref, pack_hbm = refs[pairs : pairs + 4]
    stage, tail, tops, ends, pack, marks, sems = refs[pairs + 4 :]
    section, position = place_ref[0], place_ref[1]
    base = section * per
    rows, width = x_hbm.shape[1:]
    cond_rows = SIDE

    copies = []
    loads = [pltpu.make_async_copy(x_hbm.at[base + c], stage.at[c], sems.at[0, c]) for c in range(per)]
    conv_load = pltpu.make_async_copy(conv_hbm, pack.at[pl.ds(0, 2 * width)], sems.at[1, 0])
    pieces = []
    for c in range(per):
        micro = base + c
        top = pl.ds(0, EDGE)
        for i, array in enumerate((x_hbm, out_cot_hbm, skip_cot_hbm)):
            target = tops.at[c, :, pl.ds(i * width, width)]
            pieces.append(pltpu.make_async_copy(array.at[micro, top], target, sems.at[2 + i, c]))
        end = pl.ds(rows - EDGE, EDGE)
        pieces.append(pltpu.make_async_copy(x_hbm.at[micro, end], ends.at[c], sems.at[5, c]))
    for copy in loads + [conv_load] + pieces:
        copy.start()

    cond_at = 2 * width
    outer_at = cond_at + cond_rows
    pack[cond_at : cond_at + mel_width, :] = cond_ref[0]
    pack[cond_at + mel_width : outer_at, :] = jnp.zeros((cond_rows - mel_width, 2 * width), BF16)
    pack[outer_at : outer_at + width, :width] = res_ref[0]
    pack[outer_at : outer_at + width, width:] = skip_ref[0]
    line = lax.broadcasted_iota(jnp.int32, (CHAIN_SMALL, width), 0)
    for half, lower in ((0, b_res_ref), (1, b_skip_ref)):
        span = slice(half * width, (half + 1) * width)
        first, second = b_conv_ref[0:1, span], lower[0:1, :]
        first_high = first.astype(BF16).astype(F32)
        second_high = second.astype(BF16).astype(F32)
        packed = jnp.where(
            line == 0,
            first_high,
            jnp.where(
                line == 1,
                first - first_high,
                jnp.where(line == 2, second_high, jnp.where(line == 3, second - second_high, 0.0)),
            ),
        )
        pack[outer_at + width :, span] = packed.astype(BF16)
    def store(source, target, sem):
        copy = pltpu.make_async_copy(source, target, sem)
        copy.start()
        copies.append(copy)

    for c, copy in enumerate(loads):
        copy.wait()
        store(stage.at[c], sources[c // 2].at[pl.ds((c % 2) * rows, rows)], sems.at[6, c])
    conv_load.wait()
    store(pack, pack_hbm, sems.at[1, 1])

    ids, before, earlier = ids_ref[...], before_ref[...], earlier_ref[...]
    spot = lax.broadcasted_iota(jnp.int32, ids.shape, 1)
    shifted = jnp.where(spot == 0, pltpu.roll(before, 1, 1), pltpu.roll(ids, 1, 1))
    started = position >= 1
    keep0 = jnp.where((ids == before) & started, 1.0, 0.0)
    keep1 = jnp.where((ids == shifted) & (started | (spot > 0)), 1.0, 0.0)
    keep_before = jnp.where((before == earlier) & (position >= 2), 1.0, 0.0)
    valid = valid_ref[...].astype(F32)
    row = lax.broadcasted_iota(jnp.int32, (EDGE, SIDE), 0)
    lane = lax.broadcasted_iota(jnp.int32, (EDGE, SIDE), 1)
    level = lax.broadcasted_iota(jnp.int32, (SIDE - mel_width, rows), 0)

    def pick(values, c):
        low, high = values[c : c + 1], values[per + c : per + c + 1]
        return jnp.where(section == 0, low, high)

    for c in range(per):
        marks[mel_width:, :] = jnp.where(
            level == 0,
            pick(valid, c),
            jnp.where(level == 1, pick(keep0, c), jnp.where(level == 2, pick(keep1, c), 0.0)),
        )
        marks[0:mel_width, :] = mel_ref[c].astype(F32)
        side_ref[c, 0:rows, :] = marks[...].T.astype(BF16)
        kept = jnp.broadcast_to(pick(keep_before, c)[:, rows - 1 : rows], (EDGE, SIDE))
        rim = jnp.where((row == EDGE - 1) & (lane == mel_width + 1), kept, 0.0)
        side_ref[c, rows : rows + EDGE, :] = rim.astype(BF16)
        last = side_ref[c, rows - EDGE : rows, :].astype(F32)
        tail[:, c * SIDE : (c + 1) * SIDE] = jnp.where(
            (row == EDGE - 1) & (lane <= mel_width), last, 0.0
        ).astype(BF16)
    store(tail, sources[0].at[pl.ds(2 * rows, EDGE)], sems.at[1, 2])
    for copy in pieces:
        copy.wait()
    head_line = lax.broadcasted_iota(jnp.int32, (EDGE, 3 * width), 0)
    end_line = lax.broadcasted_iota(jnp.int32, (EDGE, width), 0)
    heads = jnp.zeros((EDGE, 3 * width), F32)
    ended = jnp.zeros((EDGE, width), F32)
    sides = jnp.zeros((EDGE, SIDE), F32)
    for c in range(per):
        heads = jnp.where(head_line == c, tops[c].astype(F32)[0:1], heads)
        ended = jnp.where(end_line == c, ends[c].astype(F32)[EDGE - 1 : EDGE], ended)
        sides = jnp.where(row == c, side_ref[c, 0:EDGE, :].astype(F32)[0:1], sides)
    heads_ref[:, : 3 * width] = heads.astype(BF16)
    heads_ref[:, 3 * width :] = sides.astype(BF16)
    twice_ref[...] = ended.astype(BF16)
    for copy in copies:
        copy.wait()


def prep(per, place, samples, mel, clip_ids, valid, weights, out_cot, skip_cot):
    w_conv, w_cond, b_conv, w_res, b_res, w_skip, b_skip = weights
    count, rows, width = samples.shape
    mel_width = mel.shape[-1]
    any_space = pl.BlockSpec(memory_space=pl.ANY)
    packed = 3 * width + SIDE + CHAIN_SMALL
    whole = lambda a: pl.BlockSpec(a.shape, lambda i, s: (0,) * a.ndim)
    out = lambda *shape: jax.ShapeDtypeStruct(shape, BF16)
    ids = lambda back: pl.BlockSpec((count, rows), lambda i, s: (0, jnp.maximum(s[1] - back, 0)))
    return pl.pallas_call(
        functools.partial(prep_kernel, per, mel_width),
        grid_spec=pltpu.PrefetchScalarGridSpec(
            num_scalar_prefetch=1,
            grid=(1,),
            in_specs=[
                pl.BlockSpec((per, mel_width, rows), lambda i, s: (s[0], 0, 0)),
                whole(valid), ids(0), ids(1), ids(2),
                whole(w_cond), whole(w_res), whole(w_skip), whole(b_conv), whole(b_res), whole(b_skip),
            ]
            + [any_space] * 4,
            out_specs=[any_space] * (per // 2)
            + [
                pl.BlockSpec((EDGE, 3 * width + SIDE), lambda i, s: (0, 0)),
                pl.BlockSpec((EDGE, width), lambda i, s: (0, 0)),
                pl.BlockSpec((per, rows + EDGE, SIDE), lambda i, s: (0, 0, 0)),
                any_space,
            ],
            scratch_shapes=[
                pltpu.VMEM((per, rows, width), BF16),
                pltpu.VMEM((EDGE, width), BF16),
                pltpu.VMEM((per, EDGE, 3 * width), BF16),
                pltpu.VMEM((per, EDGE, width), BF16),
                pltpu.VMEM((packed, 2 * width), BF16),
                pltpu.VMEM((SIDE, rows), F32),
                pltpu.SemaphoreType.DMA((7, per)),
            ],
        ),
        out_shape=[out(2 * rows + (0 if c else EDGE), width) for c in range(per // 2)]
        + [
            out(EDGE, 3 * width + SIDE), out(EDGE, width), out(per, rows + EDGE, SIDE),
            out(packed, 2 * width),
        ],
        compiler_params=pltpu.CompilerParams(vmem_limit_bytes=VMEM_LIMIT),
        cost_estimate=LONG,
        name="prep",
    )(
        place, jnp.swapaxes(mel, 1, 2), valid, clip_ids, clip_ids, clip_ids, w_cond, w_res, w_skip, b_conv, b_res, b_skip,
        samples, out_cot, skip_cot, w_conv,
    )


def layers_kernel(pair, per, mel_width, waits, reused, place_ref, *refs):
    (
        x_hbm, halo_hbm, tail_hbm, side_hbm, after_hbm, twice_hbm, out_cot_hbm, skip_cot_hbm, pack_own, pack_other,
    ) = refs[:10]
    refs = refs[10 + waits + reused :]
    (
        act_hbm, skip_hbm, send_hbm, delayed0_hbm, joined1_hbm, hidden0_hbm, hidden1_hbm, dgate1_hbm,
        dgate0_hbm, grad0_hbm, keep_hbm, back_hbm, sums0_ref, sums1_ref,
    ) = refs[:14]
    (
        pack, arrived2, joined02, joined12, grads12, side2, after, twice, tail, tanh0, sig0, tanh1, sig1,
        hidden02, hidden12, act_f2, skip_f2, act_b2, skip_b2, dgate12, dgate02, grad_f, grads0, lower2, back2,
        sems, out_sems,
    ) = refs[14:]
    section = place_ref[0]
    other = 1 - section
    rows, width = arrived2.shape[1:]
    total = rows + EDGE
    main = slice(0, rows)
    rim = slice(rows, total)
    cond = slice(2 * width, 2 * width + SIDE)
    outer_rows = 2 * width + SIDE
    outer = slice(outer_rows, outer_rows + width)
    bias_row = outer_rows + width

    def load(source, target, *sem):
        return pltpu.make_async_copy(source, target, sems.at[sem])

    first_loads, late_loads = [], []
    for i in range(2):
        chunk = 2 * pair + i
        micro = section * per + chunk
        first_loads.append(
            [
                load(x_hbm.at[micro], joined02.at[i, main, width:], i, 0),
                load(halo_hbm.at[pl.ds(i * rows, rows)], arrived2.at[i], i, 1),
                load(side_hbm.at[chunk], side2.at[i], i, 2),
            ]
        )
        late_loads.append(
            [
                load(out_cot_hbm.at[micro], grads12.at[i, main, :width], i, 3),
                load(skip_cot_hbm.at[micro], grads12.at[i, main, width:], i, 4),
            ]
        )
    first_loads[0] += [
        load(after_hbm, after, 2, 0),
        load(twice_hbm, twice, 2, 1),
        load(
            tail_hbm.at[pl.ds(2 * rows, EDGE), pl.ds(2 * pair * SIDE, 2 * SIDE)], tail, 2, 2
        ),
    ]
    for copy in first_loads[0]:
        copy.start()

    @pl.when(section == 0)
    def _():
        load(pack_own, pack.at[0], 2, 3).start()
        load(pack_other, pack.at[1], 2, 4).start()

    @pl.when(section == 1)
    def _():
        load(pack_other, pack.at[0], 2, 3).start()
        load(pack_own, pack.at[1], 2, 4).start()

    for copy in late_loads[0] + first_loads[1] + late_loads[1]:
        copy.start()

    stores = []

    def put(source, target):
        copy = pltpu.make_async_copy(source, target, out_sems.at[len(stores)])
        copy.start()
        stores.append(copy)

    spot = lax.broadcasted_iota(jnp.int32, (EDGE, width), 0)
    narrow = lax.broadcasted_iota(jnp.int32, (EDGE, SIDE), 0)
    zero = jnp.zeros((EDGE, width), F32)
    sums0_ref[...] = jnp.zeros_like(sums0_ref)
    sums1_ref[...] = jnp.zeros_like(sums1_ref)

    def bias(layer, which, span):
        both = pack[layer, bias_row : bias_row + CHAIN_SMALL, span].astype(F32)
        return both[2 * which : 2 * which + 1] + both[2 * which + 1 : 2 * which + 2]

    for i in range(2):
        chunk = 2 * pair + i
        arrived, joined0, joined1, grads1, side = (
            ref.at[i] for ref in (arrived2, joined02, joined12, grads12, side2)
        )
        hidden0, hidden1 = (ref.at[i] for ref in (hidden02, hidden12))
        act_f, skip_f, act_b, skip_b = (ref.at[i] for ref in (act_f2, skip_f2, act_b2, skip_b2))
        dgate1, dgate0, lower, back = (ref.at[i] for ref in (dgate12, dgate02, lower2, back2))
        for copy in first_loads[i]:
            copy.wait()
        next_row = after[...].astype(F32)[chunk : chunk + 1]
        next_side = jnp.where(narrow == 0, next_row[:, 3 * width :], 0.0)
        side[rim, :] = side[rim, :] + tail[:, i * SIDE : (i + 1) * SIDE] + next_side.astype(BF16)
        keep0 = side[:, mel_width + 1 : mel_width + 2]
        joined0[main, :width] = arrived[...] * keep0[main]
        first = joined0[0:EDGE, width:].astype(F32)
        last = arrived[rows - EDGE : rows, :].astype(F32)
        two_back = twice[...].astype(F32)[chunk : chunk + 1]
        early = jnp.where(spot == 0, first, jnp.where(spot == EDGE - 1, two_back, zero))
        joined0[rim, :width] = early.astype(BF16) * keep0[rim]
        here = jnp.where(spot == 0, next_row[:, :width], jnp.where(spot == EDGE - 1, last, zero))
        joined0[rim, width:] = here.astype(BF16)
        for n in range(2):
            value = jnp.where(spot == 0, next_row[:, (n + 1) * width : (n + 2) * width], zero)
            grads1[rim, n * width : (n + 1) * width] = value.astype(BF16)
        put(joined0.at[main, :width], delayed0_hbm.at[i])
        keep1 = side[:, mel_width + 2 : mel_width + 3].astype(F32)
        valid = side[:, mel_width : mel_width + 1].astype(F32)

        def gates(layer, joined, tanh, sig, hidden, kept):
            if i == 0:
                load(pack_own, pack.at[layer], 2, 3 + layer).wait()
            for part in tiles(width):
                late = slice(part.start + width, part.stop + width)
                left = (
                    nn(joined[...], pack[layer, : 2 * width, part])
                    + nn(side[...], pack[layer, cond, part])
                    + bias(layer, 0, part)
                )
                right = (
                    nn(joined[...], pack[layer, : 2 * width, late])
                    + nn(side[...], pack[layer, cond, late])
                    + bias(layer, 0, late)
                )
                th = jnp.tanh(left)
                sg = sigmoid(right)
                tanh[:, part] = th[kept]
                sig[:, part] = sg[kept]
                hidden[:, part] = (th * sg * valid).astype(BF16)

        gates(0, joined0, tanh0, sig0, hidden0, main)
        put(hidden0.at[main], hidden0_hbm.at[i])
        for part in tiles(width):
            late = slice(part.start + width, part.stop + width)
            stream = (
                joined0[:, late].astype(F32) + nn(hidden0[...], pack[0, outer, part]) + bias(0, 1, part)
            )
            low = stream.astype(BF16)
            act_f[0, :, part] = stream[main]
            act_b[0, :, part] = low[main]
            joined1[:, late] = low
            joined1[:, part] = (pltpu.roll(stream, 1, 0) * keep1).astype(BF16)
            skip = nn(hidden0[main], pack[0, outer, late]) + bias(0, 1, late)
            skip_f[0, :, part] = skip
            skip_b[0, :, part] = skip.astype(BF16)
        put(joined1.at[main], joined1_hbm.at[i])

        gates(1, joined1, tanh1, sig1, hidden1, slice(0, total))
        put(hidden1.at[main], hidden1_hbm.at[i])
        for part in tiles(width):
            late = slice(part.start + width, part.stop + width)
            stream = act_f[0, :, part] + (nn(hidden1[main], pack[1, outer, part]) + bias(1, 1, part))
            act_f[1, :, part] = stream
            act_b[1, :, part] = stream.astype(BF16)
            skip = skip_f[0, :, part] + (nn(hidden1[main], pack[1, outer, late]) + bias(1, 1, late))
            skip_f[1, :, part] = skip
            skip_b[1, :, part] = skip.astype(BF16)
        put(act_b.at[other], send_hbm.at[i, 0])
        put(skip_b.at[other], send_hbm.at[i, 1])
        put(act_f.at[section], act_hbm.at[section, chunk])
        put(skip_f.at[section], skip_hbm.at[section, chunk])

        for copy in late_loads[i]:
            copy.wait()
        for part in tiles(width):
            late = slice(part.start + width, part.stop + width)
            weight = pack[1, outer_rows + part.start : outer_rows + part.stop, :]
            left, right = gate_grads(nt(grads1[...], weight) * valid, tanh1[:, part], sig1[:, part])
            sums1_ref[0:1, part] += jnp.sum(left[main], 0, keepdims=True)
            sums1_ref[0:1, late] += jnp.sum(right[main], 0, keepdims=True)
            dgate1[:, part] = left.astype(BF16)
            dgate1[:, late] = right.astype(BF16)
        put(dgate1.at[main], dgate1_hbm.at[i])
        for part in tiles(width):
            late = slice(part.start + width, part.stop + width)
            early = nt(dgate1[...], pack[1, part, :]) * keep1
            here = nt(dgate1[main], pack[1, late, :])
            above = grads1[main, part].astype(F32)
            gradient = above + here + pltpu.roll(early, total - 1, 0)[main]
            low = gradient.astype(BF16)
            grad_f[:, part] = gradient
            grads0[:, part] = low
            grads0[:, late] = grads1[main, late]
            lower[1, :, part] = low
            sums1_ref[1:2, part] += jnp.sum(above, 0, keepdims=True)
            sums0_ref[1:2, part] += jnp.sum(gradient, 0, keepdims=True)
            skip_sum = jnp.sum(grads1[main, late].astype(F32), 0, keepdims=True)
            sums1_ref[1:2, late] += skip_sum
            sums0_ref[1:2, late] += skip_sum
        put(lower.at[1], grad0_hbm.at[i])

        for part in tiles(width):
            late = slice(part.start + width, part.stop + width)
            weight = pack[0, outer_rows + part.start : outer_rows + part.stop, :]
            left, right = gate_grads(nt(grads0[...], weight) * valid[main], tanh0[:, part], sig0[:, part])
            sums0_ref[0:1, part] += jnp.sum(left, 0, keepdims=True)
            sums0_ref[0:1, late] += jnp.sum(right, 0, keepdims=True)
            dgate0[:, part] = left.astype(BF16)
            dgate0[:, late] = right.astype(BF16)
        put(dgate0, dgate0_hbm.at[i])
        for part in tiles(width):
            late = slice(part.start + width, part.stop + width)
            early = nt(dgate0[...], pack[0, part, :]) * keep0[main].astype(F32)
            back[:, part] = early.astype(BF16)
            put(back.at[:, part], back_hbm.at[i, :, part])
            lower[0, :, part] = (grad_f[:, part] + nt(dgate0[...], pack[0, late, :])).astype(BF16)
            put(lower.at[section, :, part], keep_hbm.at[i, :, part])
            put(lower.at[other, :, part], send_hbm.at[i, 2, :, part])
    for store in stores:
        store.wait()


def gate_grads(scaled, th, sg):
    both = scaled * sg
    return both * (1.0 - th * th), both * th * (1.0 - sg)


def layers(pair, per, mel_width, place, x, halo, tail, side, after, twice, out_cot, skip_cot, packs, reused, waits):
    count, rows, width = x.shape
    total = rows + EDGE
    any_space = pl.BlockSpec(memory_space=pl.ANY)
    vmem = pl.BlockSpec(memory_space=pltpu.VMEM)
    smem = pl.BlockSpec(memory_space=pltpu.SMEM)
    low = lambda *shape: jax.ShapeDtypeStruct(shape, BF16)
    wide = lambda *shape: jax.ShapeDtypeStruct(shape, F32)
    first = 11 + len(waits)
    return pl.pallas_call(
        functools.partial(layers_kernel, pair, per, mel_width, len(waits), len(reused)),
        out_shape=[
            wide(2, per, rows, width), wide(2, per, rows, width), low(2, 3, rows, width), low(2, rows, width),
            low(2, rows, 2 * width), low(2, rows, width), low(2, rows, width), low(2, rows, 2 * width),
            low(2, rows, 2 * width), low(2, rows, width), low(2, rows, width), low(2, rows, width),
            wide(8, 2 * width), wide(8, 2 * width),
        ],
        in_specs=[smem] + [any_space] * (10 + len(waits) + len(reused)),
        out_specs=[any_space] * 12 + [vmem] * 2,
        input_output_aliases={first + i: i for i in range(len(reused))},
        scratch_shapes=[
            pltpu.VMEM((2,) + packs[0].shape, BF16),
            pltpu.VMEM((2, rows, width), BF16),
            pltpu.VMEM((2, total, 2 * width), BF16),
            pltpu.VMEM((2, total, 2 * width), BF16),
            pltpu.VMEM((2, total, 2 * width), BF16),
            pltpu.VMEM((2, total, SIDE), BF16),
            pltpu.VMEM(after.shape, BF16),
            pltpu.VMEM(twice.shape, BF16),
            pltpu.VMEM((EDGE, 2 * SIDE), BF16),
            pltpu.VMEM((rows, width), F32),
            pltpu.VMEM((rows, width), F32),
            pltpu.VMEM((total, width), F32),
            pltpu.VMEM((total, width), F32),
            pltpu.VMEM((2, total, width), BF16),
            pltpu.VMEM((2, total, width), BF16),
            pltpu.VMEM((2, 2, rows, width), F32),
            pltpu.VMEM((2, 2, rows, width), F32),
            pltpu.VMEM((2, 2, rows, width), BF16),
            pltpu.VMEM((2, 2, rows, width), BF16),
            pltpu.VMEM((2, total, 2 * width), BF16),
            pltpu.VMEM((2, rows, 2 * width), BF16),
            pltpu.VMEM((rows, width), F32),
            pltpu.VMEM((rows, 2 * width), BF16),
            pltpu.VMEM((2, 2, rows, width), BF16),
            pltpu.VMEM((2, rows, width), BF16),
            pltpu.SemaphoreType.DMA((3, 5)),
            pltpu.SemaphoreType.DMA((34,)),
        ],
        compiler_params=pltpu.CompilerParams(vmem_limit_bytes=VMEM_LIMIT),
        cost_estimate=LONG,
        name="layers",
    )(place, x, halo, tail, side, after, twice, out_cot, skip_cot, *packs, *waits, *reused)


def weight_kernel(layer, per, sums_count, waits, place_ref, x_hbm, side_hbm, out_cot_hbm, skip_cot_hbm, *refs):
    pairs = per // 2
    joined_refs, hidden_refs, dgate_refs, grad_refs = (refs[pairs * i : pairs * (i + 1)] for i in range(4))
    sums_refs = refs[4 * pairs : 4 * pairs + sums_count]
    refs = refs[4 * pairs + sums_count + waits :]
    keep_hbm, send_hbm, joined, dgate, hidden, grads, side, acc, blocks, sems, out_sems = refs
    section = place_ref[0]
    rows, width = x_hbm.shape[1:]
    quarter, lanes = blocks.shape[-2:]
    turn = lanes // 2
    top = 2 * width + SIDE

    groups = []
    for chunk in range(per):
        micro = section * per + chunk
        at = slice(chunk * rows, (chunk + 1) * rows)
        if layer == 1:
            sources = [(joined_refs[chunk // 2].at[chunk % 2], joined.at[at, :])]
            outer = out_cot_hbm.at[micro]
        else:
            sources = [
                (joined_refs[chunk // 2].at[chunk % 2], joined.at[at, :width]),
                (x_hbm.at[micro], joined.at[at, width:]),
            ]
            outer = grad_refs[chunk // 2].at[chunk % 2]
        sources += [
            (dgate_refs[chunk // 2].at[chunk % 2], dgate.at[at, :]),
            (side_hbm.at[chunk, pl.ds(0, rows)], side.at[at, :]),
            (hidden_refs[chunk // 2].at[chunk % 2], hidden.at[at, :]),
            (outer, grads.at[at, :width]),
            (skip_cot_hbm.at[micro], grads.at[at, width:]),
        ]
        groups.append(
            [pltpu.make_async_copy(s, d, sems.at[chunk, i]) for i, (s, d) in enumerate(sources)]
        )
    for group in groups:
        for copy in group:
            copy.start()

    def fill(zy, start, value):
        turned = pltpu.roll(value, turn, 1).astype(BF16)
        value = value.astype(BF16)
        stop = start + value.shape[0]
        for q in range(4):
            low, high = max(start, q * quarter), min(stop, (q + 1) * quarter)
            if low < high:
                to = slice(low - q * quarter, high - q * quarter)
                at = slice(low - start, high - start)
                half, odd = q // 2, q % 2
                span = slice(turn, lanes) if odd else slice(0, turn)
                blocks[half, 2 * zy + odd, to, span] = value[at, span]
                blocks[half, 2 * zy + 1 - odd, to, span] = turned[at, span]

    def send(half):
        @pl.when(section == half)
        def _():
            pltpu.make_async_copy(blocks.at[half], keep_hbm, out_sems.at[half]).start()

        @pl.when(section != half)
        def _():
            pltpu.make_async_copy(blocks.at[half], send_hbm, out_sems.at[half]).start()

    def weave(res, skip, odd):
        place = lax.broadcasted_iota(jnp.int32, res.shape, 1)
        if odd:
            res = pltpu.roll(res, turn, 1)
        else:
            skip = pltpu.roll(skip, turn, 1)
        both = jnp.where(place < turn, res, skip)
        inner = jnp.where(
            place < turn, pltpu.roll(both, lanes - turn // 2, 1), pltpu.roll(both, turn // 2, 1)
        )
        outside = (place < turn // 2) | (place >= lanes - turn // 2)
        return jnp.where(outside, both, inner)

    splits = [slice(0, rows), slice(rows, per * rows)]
    for part, span in enumerate(splits):
        for group in groups[span.start // rows : span.stop // rows]:
            for copy in group:
                copy.wait()
        for tile in tiles(2 * width):
            conv = tn(joined[span, :], dgate[span, tile])
            cond = tn(side[span, :], dgate[span, tile])
            if part == 0:
                acc[0 : 2 * width, tile] = conv
                acc[2 * width : top, tile] = cond
            else:
                conv = conv + acc[0 : 2 * width, tile]
                cond = cond + acc[2 * width : top, tile]
                for zy in range(tile.start // lanes, tile.stop // lanes):
                    at = slice(zy * lanes - tile.start, (zy + 1) * lanes - tile.start)
                    fill(zy, 0, conv[:, at])
                    fill(zy, 2 * width, cond[:, at])
        if part == 1:
            send(0)
        for tile in tiles(width):
            late = slice(tile.start + width, tile.stop + width)
            res = tn(hidden[span, :], grads[span, tile])
            skip = tn(hidden[span, :], grads[span, late])
            if part == 0:
                acc[top : top + width, tile] = res
                acc[top : top + width, late] = skip
            else:
                res = res + acc[top : top + width, tile]
                skip = skip + acc[top : top + width, late]
                for zy in range(2 * tile.start // lanes, 2 * tile.stop // lanes):
                    at = slice((zy // 2) * lanes - tile.start, (zy // 2 + 1) * lanes - tile.start)
                    fill(zy, top, weave(res[:, at], skip[:, at], zy % 2))
    sums = sums_refs[0][...]
    for ref in sums_refs[1:]:
        sums = sums + ref[...]
    line = lax.broadcasted_iota(jnp.int32, (8, lanes), 0)
    for zy in range(2 * width // lanes):
        bias = sums[:, zy * lanes : (zy + 1) * lanes]
        res = sums[:, (zy // 2) * lanes : (zy // 2 + 1) * lanes]
        skip = sums[:, width + (zy // 2) * lanes : width + (zy // 2 + 1) * lanes]
        both = jnp.where(line == 0, bias, jnp.where(line == 1, weave(res, skip, zy % 2), 0.0))
        fill(zy, top + width, jnp.concatenate([both] + [jnp.zeros_like(both)] * (BIAS_ROWS // 8 - 1), 0))
    send(1)
    for half in range(2):
        pltpu.make_async_copy(blocks.at[half], keep_hbm, out_sems.at[half]).wait()


def weight_sums(layer, per, place, x, side, out_cot, skip_cot, joined, hidden, dgate, grad, sums, waits):
    rows, width = x.shape[1:]
    any_space = pl.BlockSpec(memory_space=pl.ANY)
    vmem = pl.BlockSpec(memory_space=pltpu.VMEM)
    smem = pl.BlockSpec(memory_space=pltpu.SMEM)
    samples = per * rows
    lanes = 128
    quarter = (3 * width + SIDE + BIAS_ROWS) // 4
    shape = jax.ShapeDtypeStruct((4 * width // lanes, quarter, lanes), BF16)
    operands = [*joined, *hidden, *dgate, *grad]
    return pl.pallas_call(
        functools.partial(weight_kernel, layer, per, len(sums), len(waits)),
        out_shape=[shape, shape],
        in_specs=[smem]
        + [any_space] * (4 + len(operands))
        + [vmem] * len(sums)
        + [any_space] * len(waits),
        out_specs=[any_space] * 2,
        scratch_shapes=[
            pltpu.VMEM((samples, 2 * width), BF16),
            pltpu.VMEM((samples, 2 * width), BF16),
            pltpu.VMEM((samples, width), BF16),
            pltpu.VMEM((samples, 2 * width), BF16),
            pltpu.VMEM((samples, SIDE), BF16),
            pltpu.VMEM((3 * width + SIDE, 2 * width), F32),
            pltpu.VMEM((2,) + shape.shape, BF16),
            pltpu.SemaphoreType.DMA((per, 7)),
            pltpu.SemaphoreType.DMA((2,)),
        ],
        compiler_params=pltpu.CompilerParams(vmem_limit_bytes=VMEM_LIMIT),
        cost_estimate=LONG,
        name="weight_sums",
    )(place, x, side, out_cot, skip_cot, *operands, *sums, *waits)


def finish_kernel(place_ref, received, kept, near, far, *refs):
    act_ref, skip_ref, grads_ref, token_ref = refs[-4:]
    section = place_ref[0]
    act_ref[0] = received[:, 0].astype(F32)
    skip_ref[0] = received[:, 1].astype(F32)
    grads_ref[section] = kept[...].astype(F32) + near[...].astype(F32)
    grads_ref[1 - section] = received[:, 2].astype(F32) + far[...].astype(F32)
    token_ref[...] = jnp.zeros_like(token_ref)


def finish(pair, place, received, kept, near, far, act, skip, grads, waits):
    per, rows, width = act.shape[1:]
    step = rows // 4
    any_space = pl.BlockSpec(memory_space=pl.ANY)
    part = pl.BlockSpec((2, step, width), lambda i, s: (0, i, 0))
    away = pl.BlockSpec((1, 2, step, width), lambda i, s: (1 - s[0], pair, i, 0))
    reused = [act, skip] + ([] if grads is None else [grads])
    return pl.pallas_call(
        finish_kernel,
        grid_spec=pltpu.PrefetchScalarGridSpec(
            num_scalar_prefetch=1,
            grid=(rows // step,),
            in_specs=[pl.BlockSpec((2, 3, step, width), lambda i, s: (0, 0, i, 0))]
            + [part] * 3
            + [any_space] * (len(waits) + len(reused)),
            out_specs=[
                away,
                away,
                pl.BlockSpec((2, 2, step, width), lambda i, s: (0, pair, i, 0)),
                pl.BlockSpec((8, 128), lambda i, s: (0, 0)),
            ],
        ),
        out_shape=[jax.ShapeDtypeStruct(act.shape, F32)] * 3 + [jax.ShapeDtypeStruct((8, 128), F32)],
        input_output_aliases={5 + len(waits) + i: i for i in range(len(reused))},
        compiler_params=pltpu.CompilerParams(vmem_limit_bytes=VMEM_LIMIT),
        cost_estimate=LONG,
        name="finish",
    )(place, received, kept, near, far, *waits, *reused)


def split_kernel(stride, mask, place_ref, first_ref, second_ref, *refs):
    away_ref, here_ref = refs[-2:]
    bit = lax.rem(place_ref[1] // mask, 2)
    for i in range(away_ref.shape[0]):
        at = (i // stride) * 2 * stride + i % stride
        for which, ref in ((1 - bit, away_ref), (bit, here_ref)):
            n = at + which * stride
            ref[i] = (first_ref[n].astype(F32) + second_ref[n].astype(F32)).astype(BF16)


def split(stride, mask, place, terms, waits):
    n = terms[0].shape[0]
    any_space = pl.BlockSpec(memory_space=pl.ANY)
    vmem = pl.BlockSpec(memory_space=pltpu.VMEM)
    shape = jax.ShapeDtypeStruct((n // 2,) + terms[0].shape[1:], BF16)
    return pl.pallas_call(
        functools.partial(split_kernel, stride, mask),
        out_shape=[shape, shape],
        in_specs=[pl.BlockSpec(memory_space=pltpu.SMEM), vmem, vmem] + [any_space] * len(waits),
        out_specs=[vmem, vmem],
        compiler_params=pltpu.CompilerParams(vmem_limit_bytes=VMEM_LIMIT),
        cost_estimate=LONG,
        name="split",
    )(place, *terms, *waits)


def sort_kernel(place_ref, first0, second0, first1, second1, mine_ref, theirs_ref):
    own = [
        (a[0].astype(F32) + b[0].astype(F32)).astype(BF16) for a, b in ((first0, second0), (first1, second1))
    ]
    is_first = place_ref[0] == 0
    mine_ref[...] = jnp.where(is_first, own[0], own[1])
    theirs_ref[...] = jnp.where(is_first, own[1], own[0])


def sort(place, terms0, terms1):
    vmem = pl.BlockSpec(memory_space=pltpu.VMEM)
    shape = jax.ShapeDtypeStruct(terms0[0].shape[1:], BF16)
    return pl.pallas_call(
        sort_kernel,
        out_shape=[shape, shape],
        in_specs=[pl.BlockSpec(memory_space=pltpu.SMEM)] + [vmem] * 4,
        out_specs=[vmem, vmem],
        cost_estimate=LONG,
        name="sort",
    )(place, *terms0, *terms1)


def unfold(halves, width, mel_width):
    _, devices, quarter, lanes = halves.shape
    share = lanes // 2
    full = halves.reshape(2, devices, quarter, 2, share).transpose(0, 3, 2, 1, 4)
    full = full.reshape(4 * quarter, devices, share).astype(F32)
    top = 2 * width + SIDE
    flat = lambda part: part.reshape(part.shape[0], -1)
    rest = full[top:]
    conv, cond, b_conv = flat(full[: 2 * width]), flat(full[2 * width : 2 * width + mel_width]), flat(rest[width : width + 1])
    res, skip = flat(rest[:, :, : share // 2]), flat(rest[:, :, share // 2 :])
    return conv, cond, b_conv, res[:width], res[width + 1 : width + 2], skip[:width], skip[width + 1 : width + 2]


def on_device(
    samples, mel, clip_ids, valid, w_conv, w_cond, b_conv, w_res, b_res, w_skip, b_skip, cot_out, cot_skip
):
    section = lax.axis_index("section")
    position = lax.axis_index("tm")
    parts = lax.axis_size("tm")
    count, rows, width = samples.shape
    mel_width = mel.shape[-1]
    per = count // 2
    place = jnp.stack([section, position]).astype(jnp.int32)
    swap = [(0, 1), (1, 0)]
    swapped = lambda a: lax.ppermute(a, "section", swap)

    *blocks, heads, ends, side, pack = prep(
        per, place, samples, mel, clip_ids, valid,
        (w_conv[0].reshape(2 * width, 2 * width), w_cond, b_conv, w_res, b_res, w_skip, b_skip),
        cot_out, cot_skip,
    )
    halos = []
    for block in blocks:
        if halos:
            block = lax.optimization_barrier((block, halos[-1]))[0]
        halos.append(lax.ppermute(block, "tm", shift("tm", 1)))
    after = lax.ppermute(heads, "tm", shift("tm", -1))
    twice = lax.ppermute(ends, "tm", shift("tm", 2))
    packs = (pack, swapped(pack))

    near_pairs = [(j + 1, j) for j in range(parts - 1)]
    far_pairs = [(parts + j + 1, j) for j in range(parts - 1)]
    axes = ("section", "tm")
    pairs = range(per // 2)
    outs, received, near, far = [], [], [], []
    for pair in pairs:
        out = layers(
            pair, per, mel_width, place, samples, halos[pair], halos[0], side, after, twice, cot_out, cot_skip,
            packs, outs[-1][:2] if outs else [], [],
        )
        outs.append(out)
        received.append(swapped(out[2]))
        near.append(lax.ppermute(out[11], axes, near_pairs))
        far.append(lax.ppermute(out[11], axes, far_pairs))
    act, skip = outs[-1][:2]
    each = lambda n: [out[n] for out in outs]

    def weights(layer, waits):
        picks = (4, 6, 7, 9, 13) if layer else (3, 5, 8, 9, 12)
        operands = [each(n) for n in picks]
        return weight_sums(layer, per, place, samples, side, cot_out, cot_skip, *operands, waits)

    def finished(pair, act, skip, grads, waits):
        return finish(pair, place, received[pair], outs[pair][10], near[pair], far[pair], act, skip, grads, waits)

    keep1, send1 = weights(1, [received[0], near[0], far[0]])
    came1 = swapped(send1)
    act, skip, grads, done = finished(0, act, skip, None, [send1])

    halving = parts == 16 and 2 * width // parts == send1.shape[-1] // 2
    if halving:
        flipped = lambda a, mask: lax.ppermute(a, "tm", [(i, i ^ mask) for i in range(parts)])

        def halved(terms, stride, mask, waits):
            away, here = split(stride, mask, place, terms, waits)
            return [here, flipped(away, mask)], away

        terms1, token = halved([keep1, came1], 2, 2, [done])
        keep0, send0 = weights(0, [token])
        came0 = swapped(send0)
        terms1, token = halved(terms1, 1, 1, [send0])
        terms0, token = halved([keep0, came0], 4, 4, [token])
        terms1, token = halved(terms1, 1, 4, [token])
        terms0, token = halved(terms0, 2, 2, [token])
        act, skip, grads, done = finished(1, act, skip, grads, [token])
        terms1, token = halved(terms1, 1, 8, [done])
        terms0, token = halved(terms0, 1, 1, [token])
        terms0, token = halved(terms0, 1, 8, [token])
        mine, theirs = sort(place, terms0, terms1)
        got = swapped(theirs)
        low = jnp.where(section == 0, mine, got)
        high = jnp.where(section == 0, got, mine)
        shares = unfold(jnp.stack([low, high])[:, None], width, mel_width)
    else:
        keep0, send0 = weights(0, [])
        came0 = swapped(send0)
        act, skip, grads, _ = finished(1, act, skip, grads, [])
        whole = lambda a, b: (a.astype(F32) + b.astype(F32)).astype(BF16)
        total0, total1 = whole(keep0, came0), whole(keep1, came1)
        mine = jnp.where(section == 0, total0, total1)
        got = swapped(jnp.where(section == 0, total1, total0))
        low = jnp.where(section == 0, mine, got)
        high = jnp.where(section == 0, got, mine)
        shares = [
            lax.psum_scatter(part, "tm", scatter_dimension=1, tiled=True)
            for part in unfold(jnp.stack([low, high]), width, mel_width)
        ]
    conv, cond, g_conv, res, g_res, skip_w, g_skip = shares
    flat = lambda a: a.reshape(1, count, rows, width)
    return (
        flat(act),
        flat(skip),
        flat(grads),
        conv.reshape(1, 2, width, -1),
        cond[None],
        g_conv,
        res[None],
        g_res,
        skip_w[None],
        g_skip,
    )


def solution(mesh):
    placed = (
        P(None, "tm", None),
        P(None, "tm", None),
        P(),
        P(None, "tm"),
        P("section", None, None, None),
        P("section", None, None),
        P("section", None),
        P("section", None, None),
        P("section", None),
        P("section", None, None),
        P("section", None),
        P(None, "tm", None),
        P(None, "tm", None),
    )
    return jax.shard_map(
        on_device,
        mesh=mesh,
        in_specs=placed,
        out_specs=(
            P("section", None, "tm", None),
            P("section", None, "tm", None),
            P("section", None, "tm", None),
            P("section", None, None, "tm"),
            P("section", None, "tm"),
            P("section", "tm"),
            P("section", None, "tm"),
            P("section", "tm"),
            P("section", None, "tm"),
            P("section", "tm"),
        ),
        check_vma=False,
    )
```

```python
import functools

import jax
import jax.numpy as jnp
from jax import lax
from jax.experimental import pallas as pl
from jax.experimental.pallas import tpu as pltpu
from jax.sharding import PartitionSpec as P

BF16 = jnp.bfloat16
F32 = jnp.float32
EDGE = 16
SIDE = 128
BIAS_ROWS = 64
CHAIN_SMALL = 16
VMEM_LIMIT = 60 * 1024 * 1024
LONG = pl.CostEstimate(flops=10**12, bytes_accessed=10**9, transcendentals=0)


def shift(axis, by):
    devices = lax.axis_size(axis)
    return [(i, i + by) for i in range(devices) if 0 <= i + by < devices]


def nn(left, right):
    return lax.dot_general(left, right, (((1,), (0,)), ((), ())), preferred_element_type=F32)


def nt(left, right):
    return lax.dot_general(left, right, (((1,), (1,)), ((), ())), preferred_element_type=F32)


def tn(left, right):
    return lax.dot_general(left, right, (((0,), (0,)), ((), ())), preferred_element_type=F32)


def sigmoid(v):
    return 0.5 * jnp.tanh(0.5 * v) + 0.5


def tiles(width, step=256):
    return [slice(n, n + step) for n in range(0, width, step)]


def first_halo_kernel(
    per, mel_width, place_ref, mel_ref, valid_ref, x_hbm, halo_hbm, ends_ref, stage, tail, ends, marks, sems
):
    section = place_ref[0]
    rows, width = stage.shape[1:]
    loads = [
        pltpu.make_async_copy(x_hbm.at[section * per + c], stage.at[c], sems.at[c]) for c in range(2)
    ]
    end = pl.ds(rows - EDGE, EDGE)
    end_loads = [
        pltpu.make_async_copy(x_hbm.at[section * per + c, end], ends.at[c], sems.at[5 + c]) for c in range(per)
    ]
    for copy in end_loads + loads:
        copy.start()
    row = lax.broadcasted_iota(jnp.int32, (EDGE, SIDE), 0)
    level = lax.broadcasted_iota(jnp.int32, (SIDE - mel_width, SIDE), 0)
    valid = valid_ref[...].astype(F32)
    for c in range(per):
        own = jnp.where(section == 0, valid[c : c + 1], valid[per + c : per + c + 1])
        marks[:mel_width, :] = mel_ref[c].astype(F32)
        marks[mel_width:, :] = jnp.where(level == 0, own, 0.0)
        last = marks[...].T[SIDE - EDGE :, :]
        tail[:, c * SIDE : (c + 1) * SIDE] = jnp.where(row == EDGE - 1, last, 0.0).astype(BF16)
    stores = [pltpu.make_async_copy(tail, halo_hbm.at[pl.ds(2 * rows, EDGE)], sems.at[4])]
    stores[0].start()
    for c, copy in enumerate(loads):
        copy.wait()
        stores.append(
            pltpu.make_async_copy(stage.at[c], halo_hbm.at[pl.ds(c * rows, rows)], sems.at[2 + c])
        )
        stores[-1].start()
    for copy in end_loads:
        copy.wait()
    line = lax.broadcasted_iota(jnp.int32, (EDGE, width), 0)
    ended = jnp.zeros((EDGE, width), F32)
    for c in range(per):
        ended = jnp.where(line == c, ends[c].astype(F32)[EDGE - 1 : EDGE], ended)
    ends_ref[...] = ended.astype(BF16)
    for copy in stores:
        copy.wait()


def first_halo(per, place, samples, mel, valid):
    count, rows, width = samples.shape
    mel_width = mel.shape[1]
    last = rows // SIDE - 1
    return pl.pallas_call(
        functools.partial(first_halo_kernel, per, mel_width),
        grid_spec=pltpu.PrefetchScalarGridSpec(
            num_scalar_prefetch=1,
            grid=(1,),
            in_specs=[
                pl.BlockSpec((per, mel_width, SIDE), lambda i, s: (s[0], 0, last)),
                pl.BlockSpec((count, SIDE), lambda i, s: (0, last)),
                pl.BlockSpec(memory_space=pl.ANY),
            ],
            out_specs=[
                pl.BlockSpec(memory_space=pl.ANY),
                pl.BlockSpec((EDGE, width), lambda i, s: (0, 0)),
            ],
            scratch_shapes=[
                pltpu.VMEM((2, rows, width), BF16),
                pltpu.VMEM((EDGE, width), BF16),
                pltpu.VMEM((per, EDGE, width), BF16),
                pltpu.VMEM((SIDE, SIDE), F32),
                pltpu.SemaphoreType.DMA((5 + per,)),
            ],
        ),
        out_shape=[
            jax.ShapeDtypeStruct((2 * rows + EDGE, width), BF16),
            jax.ShapeDtypeStruct((EDGE, width), BF16),
        ],
        compiler_params=pltpu.CompilerParams(vmem_limit_bytes=VMEM_LIMIT),
        cost_estimate=LONG,
        name="first_halo",
    )(place, mel, valid, samples)


def pack_kernel(conv_hbm, cond_ref, res_ref, skip_ref, b_conv_ref, b_res_ref, b_skip_ref, pack_hbm, pack, sems):
    _, mel_width, wide = cond_ref.shape
    width = wide // 2
    cond_rows = SIDE
    conv_load = pltpu.make_async_copy(conv_hbm, pack.at[pl.ds(0, wide)], sems.at[0])
    conv_load.start()
    cond_at = wide
    outer_at = cond_at + cond_rows
    pack[cond_at : cond_at + mel_width, :] = cond_ref[0]
    pack[cond_at + mel_width : outer_at, :] = jnp.zeros((cond_rows - mel_width, 2 * width), BF16)
    pack[outer_at : outer_at + width, :width] = res_ref[0]
    pack[outer_at : outer_at + width, width:] = skip_ref[0]
    line = lax.broadcasted_iota(jnp.int32, (CHAIN_SMALL, width), 0)
    for half, lower in ((0, b_res_ref), (1, b_skip_ref)):
        span = slice(half * width, (half + 1) * width)
        first, second = b_conv_ref[0:1, span], lower[0:1, :]
        first_high = first.astype(BF16).astype(F32)
        second_high = second.astype(BF16).astype(F32)
        packed = jnp.where(
            line == 0,
            first_high,
            jnp.where(
                line == 1,
                first - first_high,
                jnp.where(line == 2, second_high, jnp.where(line == 3, second - second_high, 0.0)),
            ),
        )
        pack[outer_at + width :, span] = packed.astype(BF16)
    below = pl.ds(wide, pack.shape[0] - wide)
    stores = [pltpu.make_async_copy(pack.at[below], pack_hbm.at[below], sems.at[1])]
    stores[0].start()
    conv_load.wait()
    above = pl.ds(0, wide)
    stores.append(pltpu.make_async_copy(pack.at[above], pack_hbm.at[above], sems.at[2]))
    stores[1].start()
    for copy in stores:
        copy.wait()


def pack_weights(w_conv, w_cond, b_conv, w_res, b_res, w_skip, b_skip):
    wide = w_conv.shape[-1]
    packed = wide + SIDE + wide // 2 + CHAIN_SMALL
    vmem = pl.BlockSpec(memory_space=pltpu.VMEM)
    any_space = pl.BlockSpec(memory_space=pl.ANY)
    return pl.pallas_call(
        pack_kernel,
        out_shape=jax.ShapeDtypeStruct((packed, wide), BF16),
        in_specs=[any_space] + [vmem] * 6,
        out_specs=any_space,
        scratch_shapes=[pltpu.VMEM((packed, wide), BF16), pltpu.SemaphoreType.DMA((3,))],
        compiler_params=pltpu.CompilerParams(vmem_limit_bytes=VMEM_LIMIT),
        cost_estimate=LONG,
        name="pack_weights",
    )(w_conv, w_cond, w_res, w_skip, b_conv, b_res, b_skip)


def prep_kernel(
    per, mel_width, place_ref, mel_ref, valid_ref, ids_ref, before_ref, earlier_ref, x_hbm, out_cot_hbm,
    skip_cot_hbm, _, *refs,
):
    sources = refs[: per // 2 - 1]
    heads_ref, side_ref = refs[per // 2 - 1 : per // 2 + 1]
    stage, tops, marks, sems = refs[per // 2 + 1 :]
    section, position = place_ref[0], place_ref[1]
    base = section * per
    rows, width = x_hbm.shape[1:]

    copies = []
    loads = [pltpu.make_async_copy(x_hbm.at[base + c], stage.at[c], sems.at[0, c]) for c in range(2, per)]
    pieces = []
    for c in range(per):
        micro = base + c
        top = pl.ds(0, EDGE)
        for i, array in enumerate((x_hbm, out_cot_hbm, skip_cot_hbm)):
            target = tops.at[c, :, pl.ds(i * width, width)]
            pieces.append(pltpu.make_async_copy(array.at[micro, top], target, sems.at[2 + i, c]))
    for copy in loads + pieces:
        copy.start()

    def store(source, target, sem):
        copy = pltpu.make_async_copy(source, target, sem)
        copy.start()
        copies.append(copy)

    for c, copy in enumerate(loads, 2):
        copy.wait()
        store(stage.at[c], sources[c // 2 - 1].at[pl.ds((c % 2) * rows, rows)], sems.at[6, c])

    ids, before, earlier = ids_ref[...], before_ref[...], earlier_ref[...]
    spot = lax.broadcasted_iota(jnp.int32, ids.shape, 1)
    shifted = jnp.where(spot == 0, pltpu.roll(before, 1, 1), pltpu.roll(ids, 1, 1))
    started = position >= 1
    keep0 = jnp.where((ids == before) & started, 1.0, 0.0)
    keep1 = jnp.where((ids == shifted) & (started | (spot > 0)), 1.0, 0.0)
    keep_before = jnp.where((before == earlier) & (position >= 2), 1.0, 0.0)
    valid = valid_ref[...].astype(F32)
    row = lax.broadcasted_iota(jnp.int32, (EDGE, SIDE), 0)
    lane = lax.broadcasted_iota(jnp.int32, (EDGE, SIDE), 1)
    level = lax.broadcasted_iota(jnp.int32, (SIDE - mel_width, rows), 0)

    def pick(values, c):
        low, high = values[c : c + 1], values[per + c : per + c + 1]
        return jnp.where(section == 0, low, high)

    for c in range(per):
        marks[mel_width:, :] = jnp.where(
            level == 0,
            pick(valid, c),
            jnp.where(level == 1, pick(keep0, c), jnp.where(level == 2, pick(keep1, c), 0.0)),
        )
        marks[0:mel_width, :] = mel_ref[c].astype(F32)
        side_ref[c, 0:rows, :] = marks[...].T.astype(BF16)
        kept = jnp.broadcast_to(pick(keep_before, c)[:, rows - 1 : rows], (EDGE, SIDE))
        rim = jnp.where((row == EDGE - 1) & (lane == mel_width + 1), kept, 0.0)
        side_ref[c, rows : rows + EDGE, :] = rim.astype(BF16)
    for copy in pieces:
        copy.wait()
    head_line = lax.broadcasted_iota(jnp.int32, (EDGE, 3 * width), 0)
    heads = jnp.zeros((EDGE, 3 * width), F32)
    sides = jnp.zeros((EDGE, SIDE), F32)
    for c in range(per):
        heads = jnp.where(head_line == c, tops[c].astype(F32)[0:1], heads)
        sides = jnp.where(row == c, side_ref[c, 0:EDGE, :].astype(F32)[0:1], sides)
    heads_ref[:, : 3 * width] = heads.astype(BF16)
    heads_ref[:, 3 * width :] = sides.astype(BF16)
    for copy in copies:
        copy.wait()


def prep(per, place, samples, mel, clip_ids, valid, out_cot, skip_cot, wait):
    count, rows, width = samples.shape
    mel_width = mel.shape[1]
    any_space = pl.BlockSpec(memory_space=pl.ANY)
    whole = lambda a: pl.BlockSpec(a.shape, lambda i, s: (0,) * a.ndim)
    out = lambda *shape: jax.ShapeDtypeStruct(shape, BF16)
    ids = lambda back: pl.BlockSpec((count, rows), lambda i, s: (0, jnp.maximum(s[1] - back, 0)))
    return pl.pallas_call(
        functools.partial(prep_kernel, per, mel_width),
        grid_spec=pltpu.PrefetchScalarGridSpec(
            num_scalar_prefetch=1,
            grid=(1,),
            in_specs=[
                pl.BlockSpec((per, mel_width, rows), lambda i, s: (s[0], 0, 0)),
                whole(valid), ids(0), ids(1), ids(2),
            ]
            + [any_space] * 4,
            out_specs=[any_space] * (per // 2 - 1)
            + [
                pl.BlockSpec((EDGE, 3 * width + SIDE), lambda i, s: (0, 0)),
                pl.BlockSpec((per, rows + EDGE, SIDE), lambda i, s: (0, 0, 0)),
            ],
            scratch_shapes=[
                pltpu.VMEM((per, rows, width), BF16),
                pltpu.VMEM((per, EDGE, 3 * width), BF16),
                pltpu.VMEM((SIDE, rows), F32),
                pltpu.SemaphoreType.DMA((7, per)),
            ],
        ),
        out_shape=[out(2 * rows, width) for _ in range(per // 2 - 1)]
        + [
            out(EDGE, 3 * width + SIDE), out(per, rows + EDGE, SIDE),
        ],
        compiler_params=pltpu.CompilerParams(vmem_limit_bytes=VMEM_LIMIT),
        cost_estimate=LONG,
        name="prep",
    )(
        place, mel, valid, clip_ids, clip_ids, clip_ids, samples, out_cot, skip_cot, wait,
    )


def gate_grads(scaled, th, sg):
    both = scaled * sg
    return both * (1.0 - th * th), both * th * (1.0 - sg)


def fold(blocks, pair, start, top, bottom, group):
    lanes = top.shape[1]
    place = lax.broadcasted_iota(jnp.int32, top.shape, 1)
    low = lax.rem(place, 2 * group) < group
    stop = start + top.shape[0]
    blocks[2 * pair, start:stop, :] = jnp.where(low, top, pltpu.roll(bottom, group, 1))
    blocks[2 * pair + 1, start:stop, :] = jnp.where(low, pltpu.roll(top, lanes - group, 1), bottom)


def beside(res, skip, odd):
    lanes = res.shape[1]
    place = lax.broadcasted_iota(jnp.int32, res.shape, 1)
    if odd:
        return jnp.where(place < lanes // 2, pltpu.roll(res, lanes // 2, 1), skip)
    return jnp.where(place < lanes // 2, res, pltpu.roll(skip, lanes // 2, 1))


def layers_kernel(pair, per, mel_width, waits, reused, place_ref, *refs):
    first_pair = pair == 0
    last_pair = pair == per // 2 - 1
    (
        x_hbm, halo_hbm, tail_hbm, side_hbm, after_hbm, twice_hbm, out_cot_hbm, skip_cot_hbm, pack_own, pack_other,
    ) = refs[:10]
    refs = refs[10 + waits :]
    if not first_pair:
        sums_in, acc_in = refs[:2]
        refs = refs[2:]
    refs = refs[reused:]
    act_hbm, skip_hbm, send_hbm, keep_hbm, back_hbm = refs[:5]
    if last_pair:
        keep_sums_hbm, send_sums_hbm = refs[5:7]
    else:
        sums_ref, acc_hbm = refs[5:7]
    (
        pack, arrived2, joined02, joined12, grads12, grads02, side2, after, twice, tail, tanh0, sig0, tanh1, sig1,
        hidden02, hidden12, act_f, skip_f, act_b, skip_b, dgate12, dgate02, grad_f, lower2, back2, acc, sums, blocks,
        sems, out_sems,
    ) = refs[7:]
    section = place_ref[0]
    other = 1 - section
    rows, width = arrived2.shape[1:]
    wide = 2 * width
    both_rows = slice(0, 2 * rows)
    cond = slice(wide, wide + SIDE)
    outer_rows = wide + SIDE
    outer = slice(outer_rows, outer_rows + width)
    bias_row = outer_rows + width

    def load(source, target, *sem):
        return pltpu.make_async_copy(source, target, sems.at[sem])

    def main(i):
        return slice(i * rows, (i + 1) * rows)

    def rim(i):
        return slice(2 * rows + i * EDGE, 2 * rows + (i + 1) * EDGE)

    def whole(ref, i, span=slice(None)):
        return jnp.concatenate([ref[main(i), span], ref[rim(i), span]], 0)

    def put_whole(ref, i, span, value):
        ref[main(i), span] = value[:rows]
        ref[rim(i), span] = value[rows:]

    first_loads, late_loads = [], []
    for i in range(2):
        chunk = 2 * pair + i
        micro = section * per + chunk
        first_loads.append(
            [
                load(x_hbm.at[micro], joined02.at[main(i), width:], i, 0),
                load(halo_hbm.at[pl.ds(i * rows, rows)], arrived2.at[i], i, 1),
                load(side_hbm.at[chunk, pl.ds(0, rows)], side2.at[main(i)], i, 2),
                load(side_hbm.at[chunk, pl.ds(rows, EDGE)], side2.at[rim(i)], i, 3),
            ]
        )
        late_loads.append(
            [
                load(out_cot_hbm.at[micro], grads12.at[main(i), :width], i, 4),
                load(skip_cot_hbm.at[micro], grads12.at[main(i), width:], i, 5),
            ]
        )
    first_loads[0] += [
        load(after_hbm, after, 2, 0),
        load(twice_hbm, twice, 2, 1),
        load(
            tail_hbm.at[pl.ds(2 * rows, EDGE), pl.ds(2 * pair * SIDE, 2 * SIDE)], tail, 2, 2
        ),
    ]
    def start_pack(layer):
        for which, pack_hbm in ((layer, pack_own), (1 - layer, pack_other)):

            @pl.when(section == which)
            def _():
                load(pack_hbm, pack.at[layer], 2, 3 + layer).start()

    for copy in first_loads[0]:
        copy.start()
    start_pack(0)

    stores = []

    def put(source, target):
        copy = pltpu.make_async_copy(source, target, out_sems.at[len(stores)])
        copy.start()
        stores.append(copy)
        return copy

    columns = tiles(wide)
    spot = lax.broadcasted_iota(jnp.int32, (EDGE, width), 0)
    narrow = lax.broadcasted_iota(jnp.int32, (EDGE, SIDE), 0)
    zero = jnp.zeros((EDGE, width), F32)
    sums[...] = jnp.zeros_like(sums) if first_pair else sums_in[...]

    def bias(layer, which, span):
        both = pack[layer, bias_row : bias_row + CHAIN_SMALL, span].astype(F32)
        return both[2 * which : 2 * which + 1] + both[2 * which + 1 : 2 * which + 2]

    output_stores, finished_stores = [], []
    for i in range(2):
        chunk = 2 * pair + i
        for copy in first_loads[i]:
            copy.wait()
        next_row = after[...].astype(F32)[chunk : chunk + 1]
        next_side = jnp.where(narrow == 0, next_row[:, 3 * width :], 0.0)
        side2[rim(i), :] = side2[rim(i), :] + tail[:, i * SIDE : (i + 1) * SIDE] + next_side.astype(BF16)
        side = whole(side2, i)
        keep0 = side[:, mel_width + 1 : mel_width + 2]
        joined02[main(i), :width] = arrived2[i] * keep0[:rows]
        first = joined02[i * rows : i * rows + EDGE, width:].astype(F32)
        last = arrived2[i, rows - EDGE : rows, :].astype(F32)
        two_back = twice[...].astype(F32)[chunk : chunk + 1]
        early = jnp.where(spot == 0, first, jnp.where(spot == EDGE - 1, two_back, zero))
        joined02[rim(i), :width] = early.astype(BF16) * keep0[rows:]
        here = jnp.where(spot == 0, next_row[:, :width], jnp.where(spot == EDGE - 1, last, zero))
        joined02[rim(i), width:] = here.astype(BF16)
        for n in range(2):
            value = jnp.where(spot == 0, next_row[:, (n + 1) * width : (n + 2) * width], zero)
            grads12[rim(i), n * width : (n + 1) * width] = value.astype(BF16)
        keep0 = keep0[:rows].astype(F32)
        keep1 = side[:, mel_width + 2 : mel_width + 3].astype(F32)
        valid = side[:, mel_width : mel_width + 1].astype(F32)

        def gates(layer, joined, tanh, sig, hidden, kept):
            if i == 0:
                load(pack_own, pack.at[layer], 2, 3 + layer).wait()
                if layer == 0:
                    start_pack(1)
                    for copy in late_loads[0] + first_loads[1] + late_loads[1]:
                        copy.start()
            rows_in = whole(joined, i)
            for part in tiles(width):
                late = slice(part.start + width, part.stop + width)
                left = nn(rows_in, pack[layer, :wide, part]) + nn(side, pack[layer, cond, part])
                right = nn(rows_in, pack[layer, :wide, late]) + nn(side, pack[layer, cond, late])
                th = jnp.tanh(left + bias(layer, 0, part))
                sg = sigmoid(right + bias(layer, 0, late))
                tanh[:, part] = th[:kept]
                sig[:, part] = sg[:kept]
                put_whole(hidden, i, part, (th * sg * valid).astype(BF16))

        gates(0, joined02, tanh0, sig0, hidden02, rows)
        if i == 1 and not first_pair:
            acc_load = load(acc_in, acc, 2, 5)
            acc_load.start()
        for copy in output_stores:
            copy.wait()
            finished_stores.append(copy)
        hidden = whole(hidden02, i)
        for part in tiles(width):
            late = slice(part.start + width, part.stop + width)
            stream = (
                whole(joined02, i, late).astype(F32) + nn(hidden, pack[0, outer, part]) + bias(0, 1, part)
            )
            low = stream.astype(BF16)
            act_f[0, :, part] = stream[:rows]
            act_b[0, :, part] = low[:rows]
            put_whole(joined12, i, late, low)
            put_whole(joined12, i, part, (pltpu.roll(stream, 1, 0) * keep1).astype(BF16))
            skip = nn(hidden[:rows], pack[0, outer, late]) + bias(0, 1, late)
            skip_f[0, :, part] = skip
            skip_b[0, :, part] = skip.astype(BF16)

        gates(1, joined12, tanh1, sig1, hidden12, rows + EDGE)
        hidden = hidden12[main(i), :]
        for part in tiles(width):
            late = slice(part.start + width, part.stop + width)
            stream = act_f[0, :, part] + (nn(hidden, pack[1, outer, part]) + bias(1, 1, part))
            act_f[1, :, part] = stream
            act_b[1, :, part] = stream.astype(BF16)
            skip = skip_f[0, :, part] + (nn(hidden, pack[1, outer, late]) + bias(1, 1, late))
            skip_f[1, :, part] = skip
            skip_b[1, :, part] = skip.astype(BF16)
        output_stores = [
            put(act_b.at[other], send_hbm.at[i, 0]),
            put(skip_b.at[other], send_hbm.at[i, 1]),
            put(act_f.at[section], act_hbm.at[section, chunk]),
            put(skip_f.at[section], skip_hbm.at[section, chunk]),
        ]

        for copy in late_loads[i]:
            copy.wait()
        grads = whole(grads12, i)
        for part in tiles(width):
            late = slice(part.start + width, part.stop + width)
            weight = pack[1, outer_rows + part.start : outer_rows + part.stop, :]
            left, right = gate_grads(nt(grads, weight) * valid, tanh1[:, part], sig1[:, part])
            sums[1, 0:1, part] += jnp.sum(left[:rows], 0, keepdims=True)
            sums[1, 0:1, late] += jnp.sum(right[:rows], 0, keepdims=True)
            put_whole(dgate12, i, part, left.astype(BF16))
            put_whole(dgate12, i, late, right.astype(BF16))
        dgate = whole(dgate12, i)
        for part in tiles(width):
            late = slice(part.start + width, part.stop + width)
            early = nt(dgate, pack[1, part, :]) * keep1
            here = nt(dgate[:rows], pack[1, late, :])
            above = grads12[main(i), part].astype(F32)
            gradient = above + here + pltpu.roll(early, rows + EDGE - 1, 0)[:rows]
            low = gradient.astype(BF16)
            grad_f[:, part] = gradient
            grads02[main(i), part] = low
            grads02[main(i), late] = grads12[main(i), late]
            lower2[i, 1, :, part] = low
            sums[1, 1:2, part] += jnp.sum(above, 0, keepdims=True)
            sums[0, 1:2, part] += jnp.sum(gradient, 0, keepdims=True)
            skip_sum = jnp.sum(grads12[main(i), late].astype(F32), 0, keepdims=True)
            sums[1, 1:2, late] += skip_sum
            sums[0, 1:2, late] += skip_sum

        grads = grads02[main(i), :]
        for part in tiles(width):
            late = slice(part.start + width, part.stop + width)
            weight = pack[0, outer_rows + part.start : outer_rows + part.stop, :]
            left, right = gate_grads(nt(grads, weight) * valid[:rows], tanh0[:, part], sig0[:, part])
            sums[0, 0:1, part] += jnp.sum(left, 0, keepdims=True)
            sums[0, 0:1, late] += jnp.sum(right, 0, keepdims=True)
            dgate02[main(i), part] = left.astype(BF16)
            dgate02[main(i), late] = right.astype(BF16)
        dgate = dgate02[main(i), :]
        for part in tiles(width):
            late = slice(part.start + width, part.stop + width)
            back2[i, :, part] = (nt(dgate, pack[0, part, :]) * keep0).astype(BF16)
            lower2[i, 0, :, part] = (grad_f[:, part] + nt(dgate, pack[0, late, :])).astype(BF16)
        put(back2.at[i], back_hbm.at[i])
        put(lower2.at[i, section], keep_hbm.at[i])
        put(lower2.at[i, other], send_hbm.at[i, 2])

    operands = {
        1: (joined12, dgate12, hidden12, grads12),
        0: (joined02, dgate02, hidden02, grads02),
    }
    def put_half(layer, half):
        copies = [
            pltpu.make_async_copy(blocks.at[layer, half], there.at[layer], out_sems.at[len(stores)])
            for there in (keep_sums_hbm, send_sums_hbm)
        ]
        for mine, copy in zip((section == half, section != half), copies):
            pl.when(mine)(copy.start)
        stores.append(copies[0])

    if not first_pair:
        acc_load.wait()
    quarter, lanes = blocks.shape[-2:]
    turn = lanes // 2
    for layer in (1, 0):
        joined, dgate, hidden, grads = operands[layer]
        outer_sums = []
        for tile in columns:
            conv = tn(joined[both_rows, :], dgate[both_rows, tile])
            conds = tn(side2[both_rows, :], dgate[both_rows, tile])
            if not first_pair:
                conv = conv + acc[layer, :wide, tile].astype(F32)
                conds = conds + acc[layer, wide:outer_rows, tile].astype(F32)
            conv, conds = conv.astype(BF16), conds.astype(BF16)
            if not last_pair:
                acc[layer, :wide, tile] = conv
                acc[layer, wide:outer_rows, tile] = conds
                continue
            for at in range(tile.start, tile.stop, lanes):
                span = slice(at - tile.start, at - tile.start + lanes)
                halves = [blocks.at[layer, half] for half in range(2)]
                value = conv[:, span]
                fold(halves[0], at // lanes, 0, value[:quarter], value[quarter : 2 * quarter], turn)
                value = value[2 * quarter :]
                middle = value.shape[0] // 2
                fold(halves[1], at // lanes, 0, value[:middle], value[middle:], turn)
                value = conds[:, span]
                fold(halves[1], at // lanes, middle, value[: SIDE // 2], value[SIDE // 2 :], turn)
        if last_pair:
            put_half(layer, 0)
        else:
            put(acc.at[layer, :outer_rows], acc_hbm.at[layer, pl.ds(0, outer_rows)])
        for tile in columns:
            outer_sum = tn(hidden[both_rows, :], grads[both_rows, tile])
            if not first_pair:
                outer_sum = outer_sum + acc[layer, outer, tile].astype(F32)
            outer_sum = outer_sum.astype(BF16)
            outer_sums.append(outer_sum)
            if not last_pair:
                acc[layer, outer, tile] = outer_sum
        if not last_pair:
            put(acc.at[layer, outer], acc_hbm.at[layer, pl.ds(outer_rows, width)])
        if last_pair:
            line = lax.broadcasted_iota(jnp.int32, (BIAS_ROWS // 2, lanes), 0)
            total = sums[layer]
            middle = (wide - 2 * quarter + SIDE) // 2
            for zy in range(wide // lanes):
                at = zy // 2 * lanes
                n, span = at // 256, slice(at % 256, at % 256 + lanes)
                value = beside(outer_sums[n][:, span], outer_sums[n + width // 256][:, span], zy % 2)
                fold(blocks.at[layer, 1], zy, middle, value[: width // 2], value[width // 2 :], turn // 2)
                biases = total[0:1, zy * lanes : (zy + 1) * lanes]
                pair_biases = beside(total[:, at : at + lanes], total[:, width + at : width + at + lanes], zy % 2)
                start = middle + width // 2
                for x, (first, second) in enumerate(
                    ((biases, pair_biases[1:2]), (pltpu.roll(total[:, zy * lanes : (zy + 1) * lanes], turn, 1)[0:1], pltpu.roll(pair_biases, lanes - turn // 2, 1)[1:2]))
                ):
                    rows_in = jnp.where(line == 0, first, jnp.where(line == 1, second, 0.0))
                    blocks[layer, 1, 2 * zy + x, start : start + BIAS_ROWS // 2, :] = rows_in.astype(BF16)
            put_half(layer, 1)
    if not last_pair:
        sums_ref[...] = sums[...]
    for store in stores:
        if not any(store is done for done in finished_stores):
            store.wait()


def layers(pair, per, mel_width, place, x, halo, tail, side, after, twice, out_cot, skip_cot, packs, sums, reused, waits):
    count, rows, width = x.shape
    total = rows + EDGE
    wide = 2 * width
    lanes = 128
    any_space = pl.BlockSpec(memory_space=pl.ANY)
    vmem = pl.BlockSpec(memory_space=pltpu.VMEM)
    smem = pl.BlockSpec(memory_space=pltpu.SMEM)
    low = lambda *shape: jax.ShapeDtypeStruct(shape, BF16)
    full = lambda *shape: jax.ShapeDtypeStruct(shape, F32)
    last_pair = pair == per // 2 - 1
    blocks = (wide // (lanes // 2), (3 * width + SIDE + BIAS_ROWS) // 4, lanes)
    first = 11 + len(waits) + len(sums)
    return pl.pallas_call(
        functools.partial(layers_kernel, pair, per, mel_width, len(waits), len(reused)),
        out_shape=[full(2, per, rows, width)] * 2
        + [low(2, 3, rows, width), low(2, rows, width), low(2, rows, width)]
        + ([low(2, *blocks)] * 2 if last_pair else [full(2, 8, wide), low(2, 3 * width + SIDE, wide)]),
        in_specs=[smem]
        + [any_space] * (10 + len(waits))
        + [vmem, any_space][: len(sums)]
        + [any_space] * len(reused),
        out_specs=[any_space] * 5 + ([any_space] * 2 if last_pair else [vmem, any_space]),
        input_output_aliases={first + i: i for i in range(len(reused))},
        scratch_shapes=[
            pltpu.VMEM((2,) + packs[0].shape, BF16),
            pltpu.VMEM((2, rows, width), BF16),
            pltpu.VMEM((2 * total, wide), BF16),
            pltpu.VMEM((2 * total, wide), BF16),
            pltpu.VMEM((2 * total, wide), BF16),
            pltpu.VMEM((2 * rows, wide), BF16),
            pltpu.VMEM((2 * total, SIDE), BF16),
            pltpu.VMEM(after.shape, BF16),
            pltpu.VMEM(twice.shape, BF16),
            pltpu.VMEM((EDGE, 2 * SIDE), BF16),
            pltpu.VMEM((rows, width), F32),
            pltpu.VMEM((rows, width), F32),
            pltpu.VMEM((total, width), F32),
            pltpu.VMEM((total, width), F32),
            pltpu.VMEM((2 * total, width), BF16),
            pltpu.VMEM((2 * total, width), BF16),
            pltpu.VMEM((2, rows, width), F32),
            pltpu.VMEM((2, rows, width), F32),
            pltpu.VMEM((2, rows, width), BF16),
            pltpu.VMEM((2, rows, width), BF16),
            pltpu.VMEM((2 * total, wide), BF16),
            pltpu.VMEM((2 * rows, wide), BF16),
            pltpu.VMEM((rows, width), F32),
            pltpu.VMEM((2, 2, rows, width), BF16),
            pltpu.VMEM((2, rows, width), BF16),
            pltpu.VMEM((2, 3 * width + SIDE, wide), BF16),
            pltpu.VMEM((2, 8, wide), F32),
            pltpu.VMEM((2, 2) + (blocks if last_pair else (1, 16, lanes)), BF16),
            pltpu.SemaphoreType.DMA((3, 6)),
            pltpu.SemaphoreType.DMA((18,)),
        ],
        compiler_params=pltpu.CompilerParams(vmem_limit_bytes=VMEM_LIMIT),
        cost_estimate=LONG,
        name="layers",
    )(place, x, halo, tail, side, after, twice, out_cot, skip_cot, *packs, *waits, *sums, *reused)


def finish_kernel(place_ref, received, kept, near, far, *refs):
    act_ref, skip_ref, grads_ref, token_ref = refs[-4:]
    section = place_ref[0]
    act_ref[0] = received[:, 0].astype(F32)
    skip_ref[0] = received[:, 1].astype(F32)
    first_layer = section == 0
    grads_ref[section] = kept[...].astype(F32) + jnp.where(first_layer, near[...].astype(F32), 0.0)
    grads_ref[1 - section] = received[:, 2].astype(F32) + jnp.where(first_layer, far[...].astype(F32), 0.0)
    token_ref[...] = jnp.zeros_like(token_ref)


def finish(pair, place, received, kept, near, far, act, skip, grads, waits):
    per, rows, width = act.shape[1:]
    step = rows // 4
    any_space = pl.BlockSpec(memory_space=pl.ANY)
    part = pl.BlockSpec((2, step, width), lambda i, s: (0, i, 0))
    away = pl.BlockSpec((1, 2, step, width), lambda i, s: (1 - s[0], pair, i, 0))
    reused = [act, skip] + ([] if grads is None else [grads])
    return pl.pallas_call(
        finish_kernel,
        grid_spec=pltpu.PrefetchScalarGridSpec(
            num_scalar_prefetch=1,
            grid=(rows // step,),
            in_specs=[pl.BlockSpec((2, 3, step, width), lambda i, s: (0, 0, i, 0))]
            + [part] * 3
            + [any_space] * (len(waits) + len(reused)),
            out_specs=[
                away,
                away,
                pl.BlockSpec((2, 2, step, width), lambda i, s: (0, pair, i, 0)),
                pl.BlockSpec((8, 128), lambda i, s: (0, 0)),
            ],
        ),
        out_shape=[jax.ShapeDtypeStruct(act.shape, F32)] * 3 + [jax.ShapeDtypeStruct((8, 128), F32)],
        input_output_aliases={5 + len(waits) + i: i for i in range(len(reused))},
        compiler_params=pltpu.CompilerParams(vmem_limit_bytes=VMEM_LIMIT),
        cost_estimate=LONG,
        name="finish",
    )(place, received, kept, near, far, *waits, *reused)


AXES = {"h": 8, "l": 4, "y": 2, "x": 1}


def bits_of(position):
    return {axis: lax.rem(position // mask, 2) for axis, mask in AXES.items()}


def step_kernel(step, pieces, waits, place_ref, *refs):
    count = 2 + step
    terms = [refs[2 + p * step : 2 + (p + 1) * step] for p in range(len(pieces))]
    aways = refs[2 + len(pieces) * step + waits :][: len(pieces)]
    buffers = refs[2 + len(pieces) * step + waits + len(pieces) :]
    sems = buffers[-1]
    bits = bits_of(place_ref[1])
    copies = []
    for p, (start, rows, order) in enumerate(pieces):
        for k, source in enumerate(refs[:2] + terms[p]):
            gone = order[: max(k - 1, 0)]
            index = []
            for axis in AXES:
                if axis in gone:
                    continue
                if axis == order[step]:
                    index.append(1 - bits[axis])
                elif axis in order[:step]:
                    index.append(bits[axis])
                else:
                    index.append(slice(None))
            at = pl.ds(start, rows) if k < 2 else slice(None)
            copy = pltpu.make_async_copy(
                source.at[(slice(None), *index, at)], buffers[p].at[k], sems.at[p, k]
            )
            copy.start()
            copies.append(copy)
    for p in range(len(pieces)):
        for k in range(count):
            copies[p * count + k].wait()
        total = buffers[p][0].astype(F32)
        for k in range(1, count):
            total = total + buffers[p][k].astype(F32)
        aways[p][...] = total.astype(BF16)


def halving_step(step, pieces, place, sums, terms, waits):
    any_space = pl.BlockSpec(memory_space=pl.ANY)
    lanes = sums[0].shape[-1]
    shapes = [(2,) + (2,) * (len(AXES) - 1 - step) + (rows, lanes) for _, rows, _ in pieces]
    flat = [term for of_piece in terms for term in of_piece]
    return pl.pallas_call(
        functools.partial(step_kernel, step, pieces, len(waits)),
        out_shape=[jax.ShapeDtypeStruct(shape, BF16) for shape in shapes],
        in_specs=[pl.BlockSpec(memory_space=pltpu.SMEM)] + [any_space] * (2 + len(flat) + len(waits)),
        out_specs=[pl.BlockSpec(memory_space=pltpu.VMEM)] * len(pieces),
        scratch_shapes=[pltpu.VMEM((2 + step,) + shape, BF16) for shape in shapes]
        + [pltpu.SemaphoreType.DMA((len(pieces), 2 + step))],
        compiler_params=pltpu.CompilerParams(vmem_limit_bytes=VMEM_LIMIT),
        cost_estimate=LONG,
        name="halving_step",
    )(place, *sums, *flat, *waits)


def last_kernel(pieces, place_ref, *refs):
    steps = len(AXES) - 1
    count = 2 + steps
    terms = [refs[2 + p * steps : 2 + (p + 1) * steps] for p in range(len(pieces))]
    near_ref, cross_ref, swap_ref, mine_ref, buffer, sems = refs[2 + len(pieces) * steps :]
    section = place_ref[0]
    bits = bits_of(place_ref[1])
    copies = []
    for p, (start, rows, order) in enumerate(pieces):
        for k, source in enumerate(refs[:2] + terms[p]):
            gone = order[: max(k - 1, 0)]
            for side in range(2):
                index = []
                for axis in AXES:
                    if axis not in gone:
                        index.append(bits[axis] if axis in order[:steps] or side else 1 - bits[axis])
                at = pl.ds(start, rows) if k < 2 else slice(None)
                copy = pltpu.make_async_copy(
                    source.at[(slice(None), *index, at)],
                    buffer.at[k, side, :, pl.ds(start, rows)],
                    sems.at[p, k, side],
                )
                copy.start()
                copies.append(copy)
    for copy in copies:
        copy.wait()

    def total(layer, side):
        return sum(buffer[k, side, layer].astype(F32) for k in range(count))

    near_ref[...] = total(section, 0).astype(BF16)
    cross_ref[...] = total(1 - section, 0).astype(BF16)
    swap_ref[...] = total(1 - section, 1).astype(BF16)
    mine_ref[...] = total(section, 1)


def last_step(pieces, place, sums, terms):
    any_space = pl.BlockSpec(memory_space=pl.ANY)
    vmem = pl.BlockSpec(memory_space=pltpu.VMEM)
    shape = sums[0].shape[-2:]
    flat = [term for of_piece in terms for term in of_piece]
    count = len(AXES) + 1
    return pl.pallas_call(
        functools.partial(last_kernel, pieces),
        out_shape=[jax.ShapeDtypeStruct(shape, BF16)] * 3 + [jax.ShapeDtypeStruct(shape, F32)],
        in_specs=[pl.BlockSpec(memory_space=pltpu.SMEM)] + [any_space] * (2 + len(flat)),
        out_specs=[vmem] * 4,
        scratch_shapes=[
            pltpu.VMEM((count, 2, 2) + shape, BF16),
            pltpu.SemaphoreType.DMA((len(pieces), count, 2)),
        ],
        compiler_params=pltpu.CompilerParams(vmem_limit_bytes=VMEM_LIMIT),
        cost_estimate=LONG,
        name="last_step",
    )(place, *sums, *flat)


def shares_kernel(
    width, mel_width, place_ref, mine, near, cross, swap, conv, cond, b_conv, res, b_res, skip, b_skip, tall
):
    quarter, lanes = mine.shape
    share = lanes // 2
    own = mine[...] + near[...].astype(F32)
    got = cross[...].astype(F32) + swap[...].astype(F32)
    is_first = place_ref[0] == 0
    low, high = jnp.where(is_first, own, got), jnp.where(is_first, got, own)
    rest = width - quarter
    tall[0:quarter, :] = low
    tall[quarter : 2 * quarter, :] = pltpu.roll(low, share, 1)
    tall[2 * quarter : 2 * quarter + rest, :] = high[:rest]
    tall[2 * quarter + rest : 2 * width, :] = pltpu.roll(high[:rest], share, 1)
    for tap in range(2):
        conv[tap] = tall[tap * width : (tap + 1) * width, :].T[:share]
    value = high[rest : rest + SIDE // 2]
    cond[...] = jnp.concatenate([value, pltpu.roll(value, share, 1)], 0).T[:share, :mel_width]
    start = rest + SIDE // 2
    value = high[start : start + width // 2]
    value = jnp.concatenate([value, pltpu.roll(value, lanes - share // 2, 1)], 0).T
    res[...] = value[: share // 2]
    skip[...] = value[share : share + share // 2]
    biases = high[start + width // 2 : start + width // 2 + 8]
    b_conv[...] = biases[0:1, :share]
    b_res[...] = biases[1:2, : share // 2]
    b_skip[...] = biases[1:2, share : share + share // 2]


def own_shares(place, width, mel_width, mine, near, cross, swap):
    vmem = pl.BlockSpec(memory_space=pltpu.VMEM)
    share = mine.shape[1] // 2
    full = lambda *shape: jax.ShapeDtypeStruct(shape, F32)
    conv, cond, b_conv, res, b_res, skip, b_skip = pl.pallas_call(
        functools.partial(shares_kernel, width, mel_width),
        out_shape=[
            full(2, share, width), full(share, mel_width), full(1, share), full(share // 2, width),
            full(1, share // 2), full(share // 2, width), full(1, share // 2),
        ],
        in_specs=[pl.BlockSpec(memory_space=pltpu.SMEM)] + [vmem] * 4,
        out_specs=[vmem] * 7,
        scratch_shapes=[pltpu.VMEM((2 * width, mine.shape[1]), F32)],
        compiler_params=pltpu.CompilerParams(vmem_limit_bytes=VMEM_LIMIT),
        cost_estimate=LONG,
        name="own_shares",
    )(place, mine, near, cross, swap)
    return jnp.swapaxes(conv, 1, 2), cond.T, b_conv, res.T, b_res, skip.T, b_skip


def unfold(halves, width, mel_width):
    _, devices, quarter, lanes = halves.shape
    share = lanes // 2
    halves = halves.astype(F32)
    rest = width - quarter

    def stacked(block, group):
        split_lanes = block.reshape(block.shape[:2] + (lanes // (2 * group), 2, group))
        return jnp.moveaxis(split_lanes, 3, 1).reshape(devices, -1, lanes // 2)

    flat = lambda block: jnp.moveaxis(block, 0, 1).reshape(block.shape[1], -1)
    low, high = halves
    conv = jnp.concatenate([stacked(low, share), stacked(high[:, :rest], share)], 1)
    cond = stacked(high[:, rest : rest + SIDE // 2], share)[:, :mel_width]
    start = rest + SIDE // 2
    both = stacked(high[:, start : start + width // 2], share // 2)
    start = start + width // 2
    b_conv = high[:, start : start + 1, :share]
    b_res = high[:, start + 1 : start + 2, : share // 2]
    b_skip = high[:, start + 1 : start + 2, share : share + share // 2]
    parts = (conv, cond, b_conv, both[:, :, : share // 2], b_res, both[:, :, share // 2 :], b_skip)
    return [flat(part) for part in parts]


def on_device(
    samples, mel, clip_ids, valid, w_conv, w_cond, b_conv, w_res, b_res, w_skip, b_skip, cot_out, cot_skip
):
    section = lax.axis_index("section")
    position = lax.axis_index("tm")
    parts = lax.axis_size("tm")
    count, rows, width = samples.shape
    mel_width = mel.shape[-1]
    per = count // 2
    place = jnp.stack([section, position]).astype(jnp.int32)
    swap = [(0, 1), (1, 0)]
    swapped = lambda a: lax.ppermute(a, "section", swap)

    mel = jnp.swapaxes(mel, 1, 2)
    block, ends = first_halo(per, place, samples, mel, valid)
    forward = shift("tm", 1)
    halos = [lax.ppermute(block, "tm", forward)]
    twice = lax.ppermute(ends, "tm", shift("tm", 2))
    pack = pack_weights(w_conv[0].reshape(2 * width, 2 * width), w_cond, b_conv, w_res, b_res, w_skip, b_skip)
    packs = (pack, swapped(pack))
    *later, heads, side = prep(per, place, samples, mel, clip_ids, valid, cot_out, cot_skip, block)
    for block in later:
        block = lax.optimization_barrier((block, halos[-1]))[0]
        halos.append(lax.ppermute(block, "tm", forward))
    after = lax.ppermute(heads, "tm", shift("tm", -1))

    near_pairs = [(j + 1, j) for j in range(parts - 1)]
    far_pairs = [(parts + j + 1, j) for j in range(parts - 1)]
    axes = ("section", "tm")
    pairs = range(per // 2)
    outs, received, near, far = [], [], [], []
    for pair in pairs:
        out = layers(
            pair, per, mel_width, place, samples, halos[pair], halos[0], side, after, twice, cot_out, cot_skip,
            packs, outs[-1][5:] if outs else [], outs[-1][:2] if outs else [], [],
        )
        outs.append(out)
        if pair == pairs[-1]:
            came = swapped(out[6])
        else:
            received.append(swapped(out[2]))
        if pair == pairs[-1]:
            near.append(lax.ppermute(out[4], "tm", shift("tm", -1)))
            far.append(swapped(near[-1]))
        else:
            near.append(lax.ppermute(out[4], axes, near_pairs))
            far.append(lax.ppermute(out[4], axes, far_pairs))
    act, skip = outs[-1][:2]
    kept, sent = outs[-1][5:]

    def finished(pair, act, skip, grads, waits):
        return finish(pair, place, received[pair], outs[pair][3], near[pair], far[pair], act, skip, grads, waits)

    if parts == 16 and 2 * width // parts == sent.shape[-1] // 2:
        quarter, lanes = sent.shape[-2:]
        pieces = ((0, 176, "yxlh"), (176, 176, "lyxh"), (352, quarter - 352, "xlyh"))
        flips = lambda mask: [(i, i ^ mask) for i in range(parts)]
        sums = [array.reshape((2,) + (2,) * len(AXES) + (quarter, lanes)) for array in (kept, came)]
        terms = [[] for _ in pieces]
        act, skip, grads, token = finished(0, act, skip, None, [sent])
        for step in range(len(AXES) - 1):
            aways = halving_step(step, pieces, place, sums, terms, [token])
            token = aways[0]
            for (_, _, order), away, of_piece in zip(pieces, aways, terms):
                of_piece.append(lax.ppermute(away, "tm", flips(AXES[order[step]])))
            if step == 0:
                last = lax.optimization_barrier((outs[-1][2], terms[0][0]))[0]
                received.append(swapped(last))
            if step == 1:
                act, skip, grads, token = finished(1, act, skip, grads, [token])
        near_sum, cross_sum, swap_sum, mine = last_step(pieces, place, sums, terms)
        mask = AXES["h"]
        crossed = [(s * parts + i, (1 - s) * parts + (i ^ mask)) for s in range(2) for i in range(parts)]
        shares = own_shares(
            place, width, mel_width, mine, lax.ppermute(near_sum, "tm", flips(mask)),
            lax.ppermute(cross_sum, axes, crossed), swapped(swap_sum),
        )
    else:
        received.append(swapped(outs[-1][2]))
        act, skip, grads, _ = finished(0, act, skip, None, [])
        act, skip, grads, _ = finished(1, act, skip, grads, [])
        total = (kept.astype(F32) + came.astype(F32)).astype(BF16)
        mine = jnp.where(section == 0, total[0], total[1])
        got = swapped(jnp.where(section == 0, total[1], total[0]))
        low = jnp.where(section == 0, mine, got)
        high = jnp.where(section == 0, got, mine)
        shares = [
            lax.psum_scatter(part, "tm", scatter_dimension=1, tiled=True)
            for part in unfold(jnp.stack([low, high]), width, mel_width)
        ]
    conv, cond, g_conv, res, g_res, skip_w, g_skip = shares
    flat = lambda a: a.reshape(1, count, rows, width)
    return (
        flat(act),
        flat(skip),
        flat(grads),
        conv.reshape(1, 2, width, -1),
        cond[None],
        g_conv,
        res[None],
        g_res,
        skip_w[None],
        g_skip,
    )


def solution(mesh):
    placed = (
        P(None, "tm", None),
        P(None, "tm", None),
        P(),
        P(None, "tm"),
        P("section", None, None, None),
        P("section", None, None),
        P("section", None),
        P("section", None, None),
        P("section", None),
        P("section", None, None),
        P("section", None),
        P(None, "tm", None),
        P(None, "tm", None),
    )
    return jax.shard_map(
        on_device,
        mesh=mesh,
        in_specs=placed,
        out_specs=(
            P("section", None, "tm", None),
            P("section", None, "tm", None),
            P("section", None, "tm", None),
            P("section", None, None, "tm"),
            P("section", None, "tm"),
            P("section", "tm"),
            P("section", None, "tm"),
            P("section", "tm"),
            P("section", None, "tm"),
            P("section", "tm"),
        ),
        check_vma=False,
    )
```

```python
import functools

import jax
import jax.numpy as jnp
from jax import lax
from jax.experimental import pallas as pl
from jax.experimental.pallas import tpu as pltpu
from jax.sharding import PartitionSpec as P

BF16 = jnp.bfloat16
F32 = jnp.float32
EDGE = 16
SIDE = 128
BIAS_ROWS = 64
CHAIN_SMALL = 16
VMEM_LIMIT = 60 * 1024 * 1024
SMALL_VMEM_LIMIT = 48 * 1024 * 1024
LONG = pl.CostEstimate(flops=10**12, bytes_accessed=10**9, transcendentals=0)


def shift(axis, by):
    devices = lax.axis_size(axis)
    return [(i, i + by) for i in range(devices) if 0 <= i + by < devices]


def nn(left, right):
    return lax.dot_general(left, right, (((1,), (0,)), ((), ())), preferred_element_type=F32)


def nt(left, right):
    return lax.dot_general(left, right, (((1,), (1,)), ((), ())), preferred_element_type=F32)


def tn(left, right):
    return lax.dot_general(left, right, (((0,), (0,)), ((), ())), preferred_element_type=F32)


def sigmoid(v):
    return 0.5 * jnp.tanh(0.5 * v) + 0.5


def tiles(width, step=256):
    return [slice(n, n + step) for n in range(0, width, step)]


def first_halo_kernel(
    per, mel_width, place_ref, mel_ref, valid_ref, x_hbm, halo_hbm, ends_ref, stage, tail, ends, marks, sems
):
    section = place_ref[0]
    rows, width = stage.shape[1:]
    loads = [
        pltpu.make_async_copy(x_hbm.at[section * per + c], stage.at[c], sems.at[c]) for c in range(2)
    ]
    end = pl.ds(rows - EDGE, EDGE)
    end_loads = [
        pltpu.make_async_copy(x_hbm.at[section * per + c, end], ends.at[c], sems.at[5 + c]) for c in range(per)
    ]
    for copy in end_loads + loads:
        copy.start()
    row = lax.broadcasted_iota(jnp.int32, (EDGE, SIDE), 0)
    level = lax.broadcasted_iota(jnp.int32, (SIDE - mel_width, SIDE), 0)
    valid = valid_ref[...].astype(F32)
    for c in range(per):
        own = jnp.where(section == 0, valid[c : c + 1], valid[per + c : per + c + 1])
        marks[:mel_width, :] = mel_ref[c].astype(F32)
        marks[mel_width:, :] = jnp.where(level == 0, own, 0.0)
        last = marks[...].T[SIDE - EDGE :, :]
        tail[:, c * SIDE : (c + 1) * SIDE] = jnp.where(row == EDGE - 1, last, 0.0).astype(BF16)
    stores = [pltpu.make_async_copy(tail, halo_hbm.at[pl.ds(2 * rows, EDGE)], sems.at[4])]
    stores[0].start()
    for c, copy in enumerate(loads):
        copy.wait()
        stores.append(
            pltpu.make_async_copy(stage.at[c], halo_hbm.at[pl.ds(c * rows, rows)], sems.at[2 + c])
        )
        stores[-1].start()
    for copy in end_loads:
        copy.wait()
    line = lax.broadcasted_iota(jnp.int32, (EDGE, width), 0)
    ended = jnp.zeros((EDGE, width), F32)
    for c in range(per):
        ended = jnp.where(line == c, ends[c].astype(F32)[EDGE - 1 : EDGE], ended)
    ends_ref[...] = ended.astype(BF16)
    for copy in stores:
        copy.wait()


def first_halo(per, place, samples, mel, valid):
    count, rows, width = samples.shape
    mel_width = mel.shape[1]
    last = rows // SIDE - 1
    return pl.pallas_call(
        functools.partial(first_halo_kernel, per, mel_width),
        grid_spec=pltpu.PrefetchScalarGridSpec(
            num_scalar_prefetch=1,
            grid=(1,),
            in_specs=[
                pl.BlockSpec((per, mel_width, SIDE), lambda i, s: (s[0], 0, last)),
                pl.BlockSpec((count, SIDE), lambda i, s: (0, last)),
                pl.BlockSpec(memory_space=pl.ANY),
            ],
            out_specs=[
                pl.BlockSpec(memory_space=pl.ANY),
                pl.BlockSpec((EDGE, width), lambda i, s: (0, 0)),
            ],
            scratch_shapes=[
                pltpu.VMEM((2, rows, width), BF16),
                pltpu.VMEM((EDGE, width), BF16),
                pltpu.VMEM((per, EDGE, width), BF16),
                pltpu.VMEM((SIDE, SIDE), F32),
                pltpu.SemaphoreType.DMA((5 + per,)),
            ],
        ),
        out_shape=[
            jax.ShapeDtypeStruct((2 * rows + EDGE, width), BF16),
            jax.ShapeDtypeStruct((EDGE, width), BF16),
        ],
        compiler_params=pltpu.CompilerParams(vmem_limit_bytes=VMEM_LIMIT),
        cost_estimate=LONG,
        name="first_halo",
    )(place, mel, valid, samples)


def pack_kernel(conv_hbm, cond_ref, res_ref, skip_ref, b_conv_ref, b_res_ref, b_skip_ref, pack_hbm, pack, sems):
    _, mel_width, wide = cond_ref.shape
    width = wide // 2
    cond_rows = SIDE
    conv_load = pltpu.make_async_copy(conv_hbm, pack.at[pl.ds(0, wide)], sems.at[0])
    conv_load.start()
    cond_at = wide
    outer_at = cond_at + cond_rows
    pack[cond_at : cond_at + mel_width, :] = cond_ref[0]
    pack[cond_at + mel_width : outer_at, :] = jnp.zeros((cond_rows - mel_width, 2 * width), BF16)
    pack[outer_at : outer_at + width, :width] = res_ref[0]
    pack[outer_at : outer_at + width, width:] = skip_ref[0]
    line = lax.broadcasted_iota(jnp.int32, (CHAIN_SMALL, width), 0)
    for half, lower in ((0, b_res_ref), (1, b_skip_ref)):
        span = slice(half * width, (half + 1) * width)
        first, second = b_conv_ref[0:1, span], lower[0:1, :]
        first_high = first.astype(BF16).astype(F32)
        second_high = second.astype(BF16).astype(F32)
        packed = jnp.where(
            line == 0,
            first_high,
            jnp.where(
                line == 1,
                first - first_high,
                jnp.where(line == 2, second_high, jnp.where(line == 3, second - second_high, 0.0)),
            ),
        )
        pack[outer_at + width :, span] = packed.astype(BF16)
    below = pl.ds(wide, pack.shape[0] - wide)
    stores = [pltpu.make_async_copy(pack.at[below], pack_hbm.at[below], sems.at[1])]
    stores[0].start()
    conv_load.wait()
    above = pl.ds(0, wide)
    stores.append(pltpu.make_async_copy(pack.at[above], pack_hbm.at[above], sems.at[2]))
    stores[1].start()
    for copy in stores:
        copy.wait()


def pack_weights(w_conv, w_cond, b_conv, w_res, b_res, w_skip, b_skip):
    wide = w_conv.shape[-1]
    packed = wide + SIDE + wide // 2 + CHAIN_SMALL
    vmem = pl.BlockSpec(memory_space=pltpu.VMEM)
    any_space = pl.BlockSpec(memory_space=pl.ANY)
    return pl.pallas_call(
        pack_kernel,
        out_shape=jax.ShapeDtypeStruct((packed, wide), BF16),
        in_specs=[any_space] + [vmem] * 6,
        out_specs=any_space,
        scratch_shapes=[pltpu.VMEM((packed, wide), BF16), pltpu.SemaphoreType.DMA((3,))],
        compiler_params=pltpu.CompilerParams(vmem_limit_bytes=VMEM_LIMIT),
        cost_estimate=LONG,
        name="pack_weights",
    )(w_conv, w_cond, w_res, w_skip, b_conv, b_res, b_skip)


def prep_kernel(
    per, mel_width, place_ref, mel_ref, valid_ref, ids_ref, before_ref, earlier_ref, x_hbm, out_cot_hbm,
    skip_cot_hbm, _, *refs,
):
    sources = refs[: per // 2 - 1]
    heads_ref, side_ref = refs[per // 2 - 1 : per // 2 + 1]
    stage, tops, marks, sems = refs[per // 2 + 1 :]
    section, position = place_ref[0], place_ref[1]
    base = section * per
    rows, width = x_hbm.shape[1:]

    copies = []
    loads = [pltpu.make_async_copy(x_hbm.at[base + c], stage.at[c], sems.at[0, c]) for c in range(2, per)]
    pieces = []
    for c in range(per):
        micro = base + c
        top = pl.ds(0, EDGE)
        for i, array in enumerate((x_hbm, out_cot_hbm, skip_cot_hbm)):
            target = tops.at[c, :, pl.ds(i * width, width)]
            pieces.append(pltpu.make_async_copy(array.at[micro, top], target, sems.at[2 + i, c]))
    for copy in loads + pieces:
        copy.start()

    def store(source, target, sem):
        copy = pltpu.make_async_copy(source, target, sem)
        copy.start()
        copies.append(copy)

    for c, copy in enumerate(loads, 2):
        copy.wait()
        store(stage.at[c], sources[c // 2 - 1].at[pl.ds((c % 2) * rows, rows)], sems.at[6, c])

    ids, before, earlier = ids_ref[...], before_ref[...], earlier_ref[...]
    spot = lax.broadcasted_iota(jnp.int32, ids.shape, 1)
    shifted = jnp.where(spot == 0, pltpu.roll(before, 1, 1), pltpu.roll(ids, 1, 1))
    started = position >= 1
    keep0 = jnp.where((ids == before) & started, 1.0, 0.0)
    keep1 = jnp.where((ids == shifted) & (started | (spot > 0)), 1.0, 0.0)
    keep_before = jnp.where((before == earlier) & (position >= 2), 1.0, 0.0)
    valid = valid_ref[...].astype(F32)
    row = lax.broadcasted_iota(jnp.int32, (EDGE, SIDE), 0)
    lane = lax.broadcasted_iota(jnp.int32, (EDGE, SIDE), 1)
    level = lax.broadcasted_iota(jnp.int32, (SIDE - mel_width, rows), 0)

    def pick(values, c):
        low, high = values[c : c + 1], values[per + c : per + c + 1]
        return jnp.where(section == 0, low, high)

    for c in range(per):
        marks[mel_width:, :] = jnp.where(
            level == 0,
            pick(valid, c),
            jnp.where(level == 1, pick(keep0, c), jnp.where(level == 2, pick(keep1, c), 0.0)),
        )
        marks[0:mel_width, :] = mel_ref[c].astype(F32)
        side_ref[c, 0:rows, :] = marks[...].T.astype(BF16)
        kept = jnp.broadcast_to(pick(keep_before, c)[:, rows - 1 : rows], (EDGE, SIDE))
        rim = jnp.where((row == EDGE - 1) & (lane == mel_width + 1), kept, 0.0)
        side_ref[c, rows : rows + EDGE, :] = rim.astype(BF16)
    for copy in pieces:
        copy.wait()
    head_line = lax.broadcasted_iota(jnp.int32, (EDGE, 3 * width), 0)
    heads = jnp.zeros((EDGE, 3 * width), F32)
    sides = jnp.zeros((EDGE, SIDE), F32)
    for c in range(per):
        heads = jnp.where(head_line == c, tops[c].astype(F32)[0:1], heads)
        sides = jnp.where(row == c, side_ref[c, 0:EDGE, :].astype(F32)[0:1], sides)
    heads_ref[:, : 3 * width] = heads.astype(BF16)
    heads_ref[:, 3 * width :] = sides.astype(BF16)
    for copy in copies:
        copy.wait()


def prep(per, place, samples, mel, clip_ids, valid, out_cot, skip_cot, wait):
    count, rows, width = samples.shape
    mel_width = mel.shape[1]
    any_space = pl.BlockSpec(memory_space=pl.ANY)
    whole = lambda a: pl.BlockSpec(a.shape, lambda i, s: (0,) * a.ndim)
    out = lambda *shape: jax.ShapeDtypeStruct(shape, BF16)
    ids = lambda back: pl.BlockSpec((count, rows), lambda i, s: (0, jnp.maximum(s[1] - back, 0)))
    return pl.pallas_call(
        functools.partial(prep_kernel, per, mel_width),
        grid_spec=pltpu.PrefetchScalarGridSpec(
            num_scalar_prefetch=1,
            grid=(1,),
            in_specs=[
                pl.BlockSpec((per, mel_width, rows), lambda i, s: (s[0], 0, 0)),
                whole(valid), ids(0), ids(1), ids(2),
            ]
            + [any_space] * 4,
            out_specs=[any_space] * (per // 2 - 1)
            + [
                pl.BlockSpec((EDGE, 3 * width + SIDE), lambda i, s: (0, 0)),
                pl.BlockSpec((per, rows + EDGE, SIDE), lambda i, s: (0, 0, 0)),
            ],
            scratch_shapes=[
                pltpu.VMEM((per, rows, width), BF16),
                pltpu.VMEM((per, EDGE, 3 * width), BF16),
                pltpu.VMEM((SIDE, rows), F32),
                pltpu.SemaphoreType.DMA((7, per)),
            ],
        ),
        out_shape=[out(2 * rows, width) for _ in range(per // 2 - 1)]
        + [
            out(EDGE, 3 * width + SIDE), out(per, rows + EDGE, SIDE),
        ],
        compiler_params=pltpu.CompilerParams(vmem_limit_bytes=VMEM_LIMIT),
        cost_estimate=LONG,
        name="prep",
    )(
        place, mel, valid, clip_ids, clip_ids, clip_ids, samples, out_cot, skip_cot, wait,
    )


def gate_grads(scaled, th, sg):
    both = scaled * sg
    return both * (1.0 - th * th), both * th * (1.0 - sg)


def fold(blocks, pair, start, top, bottom, group):
    lanes = top.shape[1]
    place = lax.broadcasted_iota(jnp.int32, top.shape, 1)
    low = lax.rem(place, 2 * group) < group
    stop = start + top.shape[0]
    blocks[2 * pair, start:stop, :] = jnp.where(low, top, pltpu.roll(bottom, group, 1))
    blocks[2 * pair + 1, start:stop, :] = jnp.where(low, pltpu.roll(top, lanes - group, 1), bottom)


def beside(res, skip, odd):
    lanes = res.shape[1]
    place = lax.broadcasted_iota(jnp.int32, res.shape, 1)
    if odd:
        return jnp.where(place < lanes // 2, pltpu.roll(res, lanes // 2, 1), skip)
    return jnp.where(place < lanes // 2, res, pltpu.roll(skip, lanes // 2, 1))


def layers_kernel(pair, per, mel_width, waits, reused, place_ref, *refs):
    first_pair = pair == 0
    last_pair = pair == per // 2 - 1
    (
        x_hbm, halo_hbm, tail_hbm, side_hbm, after_hbm, twice_hbm, out_cot_hbm, skip_cot_hbm, pack_own, pack_other,
    ) = refs[:10]
    refs = refs[10 + waits :]
    if not first_pair:
        sums_in, acc_in = refs[:2]
        refs = refs[2:]
    refs = refs[reused:]
    act_hbm, skip_hbm, send_hbm, keep_hbm, back_hbm = refs[:5]
    if last_pair:
        keep_sums_hbm, send_sums_hbm = refs[5:7]
    else:
        sums_ref, acc_hbm = refs[5:7]
    (
        pack, arrived2, joined02, joined12, grads12, grads02, side2, after, twice, tail, tanh0, sig0, tanh1, sig1,
        hidden02, hidden12, act_f, skip_f, act_b, skip_b, dgate12, dgate02, grad_f, lower2, back2, acc, sums, blocks,
        sems, out_sems,
    ) = refs[7:]
    section = place_ref[0]
    other = 1 - section
    rows, width = arrived2.shape[1:]
    wide = 2 * width
    both_rows = slice(0, 2 * rows)
    cond = slice(wide, wide + SIDE)
    outer_rows = wide + SIDE
    outer = slice(outer_rows, outer_rows + width)
    bias_row = outer_rows + width

    def load(source, target, *sem):
        return pltpu.make_async_copy(source, target, sems.at[sem])

    def main(i):
        return slice(i * rows, (i + 1) * rows)

    def rim(i):
        return slice(2 * rows + i * EDGE, 2 * rows + (i + 1) * EDGE)

    def whole(ref, i, span=slice(None)):
        return jnp.concatenate([ref[main(i), span], ref[rim(i), span]], 0)

    def put_whole(ref, i, span, value):
        ref[main(i), span] = value[:rows]
        ref[rim(i), span] = value[rows:]

    first_loads, late_loads = [], []
    for i in range(2):
        chunk = 2 * pair + i
        micro = section * per + chunk
        first_loads.append(
            [
                load(x_hbm.at[micro], joined02.at[main(i), width:], i, 0),
                load(halo_hbm.at[pl.ds(i * rows, rows)], arrived2.at[i], i, 1),
                load(side_hbm.at[chunk, pl.ds(0, rows)], side2.at[main(i)], i, 2),
                load(side_hbm.at[chunk, pl.ds(rows, EDGE)], side2.at[rim(i)], i, 3),
            ]
        )
        late_loads.append(
            [
                load(out_cot_hbm.at[micro], grads12.at[main(i), :width], i, 4),
                load(skip_cot_hbm.at[micro], grads12.at[main(i), width:], i, 5),
            ]
        )
    first_loads[0] += [
        load(after_hbm, after, 2, 0),
        load(twice_hbm, twice, 2, 1),
        load(
            tail_hbm.at[pl.ds(2 * rows, EDGE), pl.ds(2 * pair * SIDE, 2 * SIDE)], tail, 2, 2
        ),
    ]
    def start_pack(layer):
        for which, pack_hbm in ((layer, pack_own), (1 - layer, pack_other)):

            @pl.when(section == which)
            def _():
                load(pack_hbm, pack.at[layer], 2, 3 + layer).start()

    for copy in first_loads[0]:
        copy.start()
    start_pack(0)

    stores = []

    def put(source, target):
        copy = pltpu.make_async_copy(source, target, out_sems.at[len(stores)])
        copy.start()
        stores.append(copy)
        return copy

    columns = tiles(wide)
    spot = lax.broadcasted_iota(jnp.int32, (EDGE, width), 0)
    narrow = lax.broadcasted_iota(jnp.int32, (EDGE, SIDE), 0)
    zero = jnp.zeros((EDGE, width), F32)
    sums[...] = jnp.zeros_like(sums) if first_pair else sums_in[...]

    def bias(layer, which, span):
        both = pack[layer, bias_row : bias_row + CHAIN_SMALL, span].astype(F32)
        return both[2 * which : 2 * which + 1] + both[2 * which + 1 : 2 * which + 2]

    output_stores, finished_stores = [], []
    for i in range(2):
        chunk = 2 * pair + i
        for copy in first_loads[i]:
            copy.wait()
        next_row = after[...].astype(F32)[chunk : chunk + 1]
        next_side = jnp.where(narrow == 0, next_row[:, 3 * width :], 0.0)
        side2[rim(i), :] = side2[rim(i), :] + tail[:, i * SIDE : (i + 1) * SIDE] + next_side.astype(BF16)
        side = whole(side2, i)
        keep0 = side[:, mel_width + 1 : mel_width + 2]
        joined02[main(i), :width] = arrived2[i] * keep0[:rows]
        first = joined02[i * rows : i * rows + EDGE, width:].astype(F32)
        last = arrived2[i, rows - EDGE : rows, :].astype(F32)
        two_back = twice[...].astype(F32)[chunk : chunk + 1]
        early = jnp.where(spot == 0, first, jnp.where(spot == EDGE - 1, two_back, zero))
        joined02[rim(i), :width] = early.astype(BF16) * keep0[rows:]
        here = jnp.where(spot == 0, next_row[:, :width], jnp.where(spot == EDGE - 1, last, zero))
        joined02[rim(i), width:] = here.astype(BF16)
        for n in range(2):
            value = jnp.where(spot == 0, next_row[:, (n + 1) * width : (n + 2) * width], zero)
            grads12[rim(i), n * width : (n + 1) * width] = value.astype(BF16)
        keep0 = keep0[:rows].astype(F32)
        keep1 = side[:, mel_width + 2 : mel_width + 3].astype(F32)
        valid = side[:, mel_width : mel_width + 1].astype(F32)

        def gates(layer, joined, tanh, sig, hidden, kept):
            if i == 0:
                load(pack_own, pack.at[layer], 2, 3 + layer).wait()
                if layer == 0:
                    start_pack(1)
                    for copy in late_loads[0] + first_loads[1] + late_loads[1]:
                        copy.start()
            rows_in = whole(joined, i)
            for part in tiles(width):
                late = slice(part.start + width, part.stop + width)
                left = nn(rows_in, pack[layer, :wide, part]) + nn(side, pack[layer, cond, part])
                right = nn(rows_in, pack[layer, :wide, late]) + nn(side, pack[layer, cond, late])
                th = jnp.tanh(left + bias(layer, 0, part))
                sg = sigmoid(right + bias(layer, 0, late))
                tanh[:, part] = th[:kept]
                sig[:, part] = sg[:kept]
                put_whole(hidden, i, part, (th * sg * valid).astype(BF16))

        gates(0, joined02, tanh0, sig0, hidden02, rows)
        if i == 1 and not first_pair:
            acc_load = load(acc_in, acc, 2, 5)
            acc_load.start()
        for copy in output_stores:
            copy.wait()
            finished_stores.append(copy)
        hidden = whole(hidden02, i)
        for part in tiles(width):
            late = slice(part.start + width, part.stop + width)
            stream = (
                whole(joined02, i, late).astype(F32) + nn(hidden, pack[0, outer, part]) + bias(0, 1, part)
            )
            low = stream.astype(BF16)
            act_f[0, :, part] = stream[:rows]
            act_b[0, :, part] = low[:rows]
            put_whole(joined12, i, late, low)
            put_whole(joined12, i, part, (pltpu.roll(stream, 1, 0) * keep1).astype(BF16))
            skip = nn(hidden[:rows], pack[0, outer, late]) + bias(0, 1, late)
            skip_f[0, :, part] = skip
            skip_b[0, :, part] = skip.astype(BF16)

        gates(1, joined12, tanh1, sig1, hidden12, rows + EDGE)
        hidden = hidden12[main(i), :]
        for part in tiles(width):
            late = slice(part.start + width, part.stop + width)
            stream = act_f[0, :, part] + (nn(hidden, pack[1, outer, part]) + bias(1, 1, part))
            act_f[1, :, part] = stream
            act_b[1, :, part] = stream.astype(BF16)
            skip = skip_f[0, :, part] + (nn(hidden, pack[1, outer, late]) + bias(1, 1, late))
            skip_f[1, :, part] = skip
            skip_b[1, :, part] = skip.astype(BF16)
        output_stores = [
            put(act_b.at[other], send_hbm.at[i, 0]),
            put(skip_b.at[other], send_hbm.at[i, 1]),
            put(act_f.at[section], act_hbm.at[section, chunk]),
            put(skip_f.at[section], skip_hbm.at[section, chunk]),
        ]

        for copy in late_loads[i]:
            copy.wait()
        grads = whole(grads12, i)
        for part in tiles(width):
            late = slice(part.start + width, part.stop + width)
            weight = pack[1, outer_rows + part.start : outer_rows + part.stop, :]
            left, right = gate_grads(nt(grads, weight) * valid, tanh1[:, part], sig1[:, part])
            sums[1, 0:1, part] += jnp.sum(left[:rows], 0, keepdims=True)
            sums[1, 0:1, late] += jnp.sum(right[:rows], 0, keepdims=True)
            put_whole(dgate12, i, part, left.astype(BF16))
            put_whole(dgate12, i, late, right.astype(BF16))
        dgate = whole(dgate12, i)
        for part in tiles(width):
            late = slice(part.start + width, part.stop + width)
            early = nt(dgate, pack[1, part, :]) * keep1
            here = nt(dgate[:rows], pack[1, late, :])
            above = grads12[main(i), part].astype(F32)
            gradient = above + here + pltpu.roll(early, rows + EDGE - 1, 0)[:rows]
            low = gradient.astype(BF16)
            grad_f[:, part] = gradient
            grads02[main(i), part] = low
            grads02[main(i), late] = grads12[main(i), late]
            lower2[i, 1, :, part] = low
            sums[1, 1:2, part] += jnp.sum(above, 0, keepdims=True)
            sums[0, 1:2, part] += jnp.sum(gradient, 0, keepdims=True)
            skip_sum = jnp.sum(grads12[main(i), late].astype(F32), 0, keepdims=True)
            sums[1, 1:2, late] += skip_sum
            sums[0, 1:2, late] += skip_sum

        grads = grads02[main(i), :]
        for part in tiles(width):
            late = slice(part.start + width, part.stop + width)
            weight = pack[0, outer_rows + part.start : outer_rows + part.stop, :]
            left, right = gate_grads(nt(grads, weight) * valid[:rows], tanh0[:, part], sig0[:, part])
            sums[0, 0:1, part] += jnp.sum(left, 0, keepdims=True)
            sums[0, 0:1, late] += jnp.sum(right, 0, keepdims=True)
            dgate02[main(i), part] = left.astype(BF16)
            dgate02[main(i), late] = right.astype(BF16)
        dgate = dgate02[main(i), :]
        for part in tiles(width):
            late = slice(part.start + width, part.stop + width)
            back2[i, :, part] = (nt(dgate, pack[0, part, :]) * keep0).astype(BF16)
            lower2[i, 0, :, part] = (grad_f[:, part] + nt(dgate, pack[0, late, :])).astype(BF16)
        put(back2.at[i], back_hbm.at[i])
        put(lower2.at[i, section], keep_hbm.at[i])
        put(lower2.at[i, other], send_hbm.at[i, 2])

    operands = {
        1: (joined12, dgate12, hidden12, grads12),
        0: (joined02, dgate02, hidden02, grads02),
    }
    def put_half(layer, half):
        copies = [
            pltpu.make_async_copy(blocks.at[layer, half], there.at[layer], out_sems.at[len(stores)])
            for there in (keep_sums_hbm, send_sums_hbm)
        ]
        for mine, copy in zip((section == half, section != half), copies):
            pl.when(mine)(copy.start)
        stores.append(copies[0])

    if not first_pair:
        acc_load.wait()
    quarter, lanes = blocks.shape[-2:]
    turn = lanes // 2
    for layer in (1, 0):
        joined, dgate, hidden, grads = operands[layer]
        outer_sums = []
        for tile in columns:
            conv = tn(joined[both_rows, :], dgate[both_rows, tile])
            conds = tn(side2[both_rows, :], dgate[both_rows, tile])
            if not first_pair:
                conv = conv + acc[layer, :wide, tile].astype(F32)
                conds = conds + acc[layer, wide:outer_rows, tile].astype(F32)
            conv, conds = conv.astype(BF16), conds.astype(BF16)
            if not last_pair:
                acc[layer, :wide, tile] = conv
                acc[layer, wide:outer_rows, tile] = conds
                continue
            for at in range(tile.start, tile.stop, lanes):
                span = slice(at - tile.start, at - tile.start + lanes)
                halves = [blocks.at[layer, half] for half in range(2)]
                value = conv[:, span]
                fold(halves[0], at // lanes, 0, value[:quarter], value[quarter : 2 * quarter], turn)
                value = value[2 * quarter :]
                middle = value.shape[0] // 2
                fold(halves[1], at // lanes, 0, value[:middle], value[middle:], turn)
                value = conds[:, span]
                fold(halves[1], at // lanes, middle, value[: SIDE // 2], value[SIDE // 2 :], turn)
        if last_pair:
            put_half(layer, 0)
        else:
            put(acc.at[layer, :outer_rows], acc_hbm.at[layer, pl.ds(0, outer_rows)])
        for tile in columns:
            outer_sum = tn(hidden[both_rows, :], grads[both_rows, tile])
            if not first_pair:
                outer_sum = outer_sum + acc[layer, outer, tile].astype(F32)
            outer_sum = outer_sum.astype(BF16)
            outer_sums.append(outer_sum)
            if not last_pair:
                acc[layer, outer, tile] = outer_sum
        if not last_pair:
            put(acc.at[layer, outer], acc_hbm.at[layer, pl.ds(outer_rows, width)])
        if last_pair:
            line = lax.broadcasted_iota(jnp.int32, (BIAS_ROWS // 2, lanes), 0)
            total = sums[layer]
            middle = (wide - 2 * quarter + SIDE) // 2
            for zy in range(wide // lanes):
                at = zy // 2 * lanes
                n, span = at // 256, slice(at % 256, at % 256 + lanes)
                value = beside(outer_sums[n][:, span], outer_sums[n + width // 256][:, span], zy % 2)
                fold(blocks.at[layer, 1], zy, middle, value[: width // 2], value[width // 2 :], turn // 2)
                biases = total[0:1, zy * lanes : (zy + 1) * lanes]
                pair_biases = beside(total[:, at : at + lanes], total[:, width + at : width + at + lanes], zy % 2)
                start = middle + width // 2
                for x, (first, second) in enumerate(
                    ((biases, pair_biases[1:2]), (pltpu.roll(total[:, zy * lanes : (zy + 1) * lanes], turn, 1)[0:1], pltpu.roll(pair_biases, lanes - turn // 2, 1)[1:2]))
                ):
                    rows_in = jnp.where(line == 0, first, jnp.where(line == 1, second, 0.0))
                    blocks[layer, 1, 2 * zy + x, start : start + BIAS_ROWS // 2, :] = rows_in.astype(BF16)
            put_half(layer, 1)
    if not last_pair:
        sums_ref[...] = sums[...]
    for store in stores:
        if not any(store is done for done in finished_stores):
            store.wait()


def layers(pair, per, mel_width, place, x, halo, tail, side, after, twice, out_cot, skip_cot, packs, sums, reused, waits):
    count, rows, width = x.shape
    total = rows + EDGE
    wide = 2 * width
    lanes = 128
    any_space = pl.BlockSpec(memory_space=pl.ANY)
    vmem = pl.BlockSpec(memory_space=pltpu.VMEM)
    smem = pl.BlockSpec(memory_space=pltpu.SMEM)
    low = lambda *shape: jax.ShapeDtypeStruct(shape, BF16)
    full = lambda *shape: jax.ShapeDtypeStruct(shape, F32)
    last_pair = pair == per // 2 - 1
    blocks = (wide // (lanes // 2), (3 * width + SIDE + BIAS_ROWS) // 4, lanes)
    first = 11 + len(waits) + len(sums)
    return pl.pallas_call(
        functools.partial(layers_kernel, pair, per, mel_width, len(waits), len(reused)),
        out_shape=[full(2, per, rows, width)] * 2
        + [low(2, 3, rows, width), low(2, rows, width), low(2, rows, width)]
        + ([low(2, *blocks)] * 2 if last_pair else [full(2, 8, wide), low(2, 3 * width + SIDE, wide)]),
        in_specs=[smem]
        + [any_space] * (10 + len(waits))
        + [vmem, any_space][: len(sums)]
        + [any_space] * len(reused),
        out_specs=[any_space] * 5 + ([any_space] * 2 if last_pair else [vmem, any_space]),
        input_output_aliases={first + i: i for i in range(len(reused))},
        scratch_shapes=[
            pltpu.VMEM((2,) + packs[0].shape, BF16),
            pltpu.VMEM((2, rows, width), BF16),
            pltpu.VMEM((2 * total, wide), BF16),
            pltpu.VMEM((2 * total, wide), BF16),
            pltpu.VMEM((2 * total, wide), BF16),
            pltpu.VMEM((2 * rows, wide), BF16),
            pltpu.VMEM((2 * total, SIDE), BF16),
            pltpu.VMEM(after.shape, BF16),
            pltpu.VMEM(twice.shape, BF16),
            pltpu.VMEM((EDGE, 2 * SIDE), BF16),
            pltpu.VMEM((rows, width), F32),
            pltpu.VMEM((rows, width), F32),
            pltpu.VMEM((total, width), F32),
            pltpu.VMEM((total, width), F32),
            pltpu.VMEM((2 * total, width), BF16),
            pltpu.VMEM((2 * total, width), BF16),
            pltpu.VMEM((2, rows, width), F32),
            pltpu.VMEM((2, rows, width), F32),
            pltpu.VMEM((2, rows, width), BF16),
            pltpu.VMEM((2, rows, width), BF16),
            pltpu.VMEM((2 * total, wide), BF16),
            pltpu.VMEM((2 * rows, wide), BF16),
            pltpu.VMEM((rows, width), F32),
            pltpu.VMEM((2, 2, rows, width), BF16),
            pltpu.VMEM((2, rows, width), BF16),
            pltpu.VMEM((2, 3 * width + SIDE, wide), BF16),
            pltpu.VMEM((2, 8, wide), F32),
            pltpu.VMEM((2, 2) + (blocks if last_pair else (1, 16, lanes)), BF16),
            pltpu.SemaphoreType.DMA((3, 6)),
            pltpu.SemaphoreType.DMA((18,)),
        ],
        compiler_params=pltpu.CompilerParams(vmem_limit_bytes=VMEM_LIMIT),
        cost_estimate=LONG,
        name="layers",
    )(place, x, halo, tail, side, after, twice, out_cot, skip_cot, *packs, *waits, *sums, *reused)


def finish_kernel(place_ref, received, kept, near, far, *refs):
    act_ref, skip_ref, grads_ref, token_ref = refs[-4:]
    section = place_ref[0]
    act_ref[0] = received[:, 0].astype(F32)
    skip_ref[0] = received[:, 1].astype(F32)
    first_layer = section == 0
    grads_ref[section] = kept[...].astype(F32) + jnp.where(first_layer, near[...].astype(F32), 0.0)
    grads_ref[1 - section] = received[:, 2].astype(F32) + jnp.where(first_layer, far[...].astype(F32), 0.0)
    token_ref[...] = jnp.zeros_like(token_ref)


def finish(pair, place, received, kept, near, far, act, skip, grads, waits):
    per, rows, width = act.shape[1:]
    step = rows // 4
    any_space = pl.BlockSpec(memory_space=pl.ANY)
    part = pl.BlockSpec((2, step, width), lambda i, s: (0, i, 0))
    away = pl.BlockSpec((1, 2, step, width), lambda i, s: (1 - s[0], pair, i, 0))
    reused = [act, skip] + ([] if grads is None else [grads])
    return pl.pallas_call(
        finish_kernel,
        grid_spec=pltpu.PrefetchScalarGridSpec(
            num_scalar_prefetch=1,
            grid=(rows // step,),
            in_specs=[pl.BlockSpec((2, 3, step, width), lambda i, s: (0, 0, i, 0))]
            + [part] * 3
            + [any_space] * (len(waits) + len(reused)),
            out_specs=[
                away,
                away,
                pl.BlockSpec((2, 2, step, width), lambda i, s: (0, pair, i, 0)),
                pl.BlockSpec((8, 128), lambda i, s: (0, 0)),
            ],
        ),
        out_shape=[jax.ShapeDtypeStruct(act.shape, F32)] * 3 + [jax.ShapeDtypeStruct((8, 128), F32)],
        input_output_aliases={5 + len(waits) + i: i for i in range(len(reused))},
        compiler_params=pltpu.CompilerParams(vmem_limit_bytes=VMEM_LIMIT),
        cost_estimate=LONG,
        name="finish",
    )(place, received, kept, near, far, *waits, *reused)


AXES = {"h": 8, "l": 4, "y": 2, "x": 1}


def bits_of(position):
    return {axis: lax.rem(position // mask, 2) for axis, mask in AXES.items()}


def step_kernel(step, pieces, waits, place_ref, *refs):
    count = 2 + step
    terms = [refs[2 + p * step : 2 + (p + 1) * step] for p in range(len(pieces))]
    aways = refs[2 + len(pieces) * step + waits :][: len(pieces)]
    buffers = refs[2 + len(pieces) * step + waits + len(pieces) :]
    sems = buffers[-1]
    bits = bits_of(place_ref[1])
    copies = []
    for p, (start, rows, order) in enumerate(pieces):
        for k, source in enumerate(refs[:2] + terms[p]):
            gone = order[: max(k - 1, 0)]
            index = []
            for axis in AXES:
                if axis in gone:
                    continue
                if axis == order[step]:
                    index.append(1 - bits[axis])
                elif axis in order[:step]:
                    index.append(bits[axis])
                else:
                    index.append(slice(None))
            at = pl.ds(start, rows) if k < 2 else slice(None)
            copy = pltpu.make_async_copy(
                source.at[(slice(None), *index, at)], buffers[p].at[k], sems.at[p, k]
            )
            copy.start()
            copies.append(copy)
    for p in range(len(pieces)):
        for k in range(count):
            copies[p * count + k].wait()
        total = buffers[p][0].astype(F32)
        for k in range(1, count):
            total = total + buffers[p][k].astype(F32)
        aways[p][...] = total.astype(BF16)


def halving_step(step, pieces, place, sums, terms, waits):
    any_space = pl.BlockSpec(memory_space=pl.ANY)
    lanes = sums[0].shape[-1]
    shapes = [(2,) + (2,) * (len(AXES) - 1 - step) + (rows, lanes) for _, rows, _ in pieces]
    flat = [term for of_piece in terms for term in of_piece]
    return pl.pallas_call(
        functools.partial(step_kernel, step, pieces, len(waits)),
        out_shape=[jax.ShapeDtypeStruct(shape, BF16) for shape in shapes],
        in_specs=[pl.BlockSpec(memory_space=pltpu.SMEM)] + [any_space] * (2 + len(flat) + len(waits)),
        out_specs=[pl.BlockSpec(memory_space=pltpu.VMEM)] * len(pieces),
        scratch_shapes=[pltpu.VMEM((2 + step,) + shape, BF16) for shape in shapes]
        + [pltpu.SemaphoreType.DMA((len(pieces), 2 + step))],
        compiler_params=pltpu.CompilerParams(vmem_limit_bytes=SMALL_VMEM_LIMIT),
        cost_estimate=LONG,
        name="halving_step",
    )(place, *sums, *flat, *waits)


def last_kernel(pieces, place_ref, *refs):
    steps = len(AXES) - 1
    count = 2 + steps
    terms = [refs[2 + p * steps : 2 + (p + 1) * steps] for p in range(len(pieces))]
    near_ref, cross_ref, swap_ref, mine_ref, buffer, sems = refs[2 + len(pieces) * steps :]
    section = place_ref[0]
    bits = bits_of(place_ref[1])
    copies = []
    for p, (start, rows, order) in enumerate(pieces):
        for k, source in enumerate(refs[:2] + terms[p]):
            gone = order[: max(k - 1, 0)]
            for side in range(2):
                index = []
                for axis in AXES:
                    if axis not in gone:
                        index.append(bits[axis] if axis in order[:steps] or side else 1 - bits[axis])
                at = pl.ds(start, rows) if k < 2 else slice(None)
                copy = pltpu.make_async_copy(
                    source.at[(slice(None), *index, at)],
                    buffer.at[k, side, :, pl.ds(start, rows)],
                    sems.at[p, k, side],
                )
                copy.start()
                copies.append(copy)
    for copy in copies:
        copy.wait()

    def total(layer, side):
        return sum(buffer[k, side, layer].astype(F32) for k in range(count))

    near_ref[...] = total(section, 0).astype(BF16)
    cross_ref[...] = total(1 - section, 0).astype(BF16)
    swap_ref[...] = total(1 - section, 1).astype(BF16)
    mine_ref[...] = total(section, 1)


def last_step(pieces, place, sums, terms):
    any_space = pl.BlockSpec(memory_space=pl.ANY)
    vmem = pl.BlockSpec(memory_space=pltpu.VMEM)
    shape = sums[0].shape[-2:]
    flat = [term for of_piece in terms for term in of_piece]
    count = len(AXES) + 1
    return pl.pallas_call(
        functools.partial(last_kernel, pieces),
        out_shape=[jax.ShapeDtypeStruct(shape, BF16)] * 3 + [jax.ShapeDtypeStruct(shape, F32)],
        in_specs=[pl.BlockSpec(memory_space=pltpu.SMEM)] + [any_space] * (2 + len(flat)),
        out_specs=[vmem] * 4,
        scratch_shapes=[
            pltpu.VMEM((count, 2, 2) + shape, BF16),
            pltpu.SemaphoreType.DMA((len(pieces), count, 2)),
        ],
        compiler_params=pltpu.CompilerParams(vmem_limit_bytes=SMALL_VMEM_LIMIT),
        cost_estimate=LONG,
        name="last_step",
    )(place, *sums, *flat)


def shares_kernel(
    width, mel_width, place_ref, mine, near, cross, swap, conv, cond, b_conv, res, b_res, skip, b_skip, tall
):
    quarter, lanes = mine.shape
    share = lanes // 2
    own = mine[...] + near[...].astype(F32)
    got = cross[...].astype(F32) + swap[...].astype(F32)
    is_first = place_ref[0] == 0
    low, high = jnp.where(is_first, own, got), jnp.where(is_first, got, own)
    rest = width - quarter
    tall[0:quarter, :] = low
    tall[quarter : 2 * quarter, :] = pltpu.roll(low, share, 1)
    tall[2 * quarter : 2 * quarter + rest, :] = high[:rest]
    tall[2 * quarter + rest : 2 * width, :] = pltpu.roll(high[:rest], share, 1)
    for tap in range(2):
        conv[tap] = tall[tap * width : (tap + 1) * width, :].T[:share]
    value = high[rest : rest + SIDE // 2]
    cond[...] = jnp.concatenate([value, pltpu.roll(value, share, 1)], 0).T[:share, :mel_width]
    start = rest + SIDE // 2
    value = high[start : start + width // 2]
    value = jnp.concatenate([value, pltpu.roll(value, lanes - share // 2, 1)], 0).T
    res[...] = value[: share // 2]
    skip[...] = value[share : share + share // 2]
    biases = high[start + width // 2 : start + width // 2 + 8]
    b_conv[...] = biases[0:1, :share]
    b_res[...] = biases[1:2, : share // 2]
    b_skip[...] = biases[1:2, share : share + share // 2]


def own_shares(place, width, mel_width, mine, near, cross, swap):
    vmem = pl.BlockSpec(memory_space=pltpu.VMEM)
    share = mine.shape[1] // 2
    full = lambda *shape: jax.ShapeDtypeStruct(shape, F32)
    conv, cond, b_conv, res, b_res, skip, b_skip = pl.pallas_call(
        functools.partial(shares_kernel, width, mel_width),
        out_shape=[
            full(2, share, width), full(share, mel_width), full(1, share), full(share // 2, width),
            full(1, share // 2), full(share // 2, width), full(1, share // 2),
        ],
        in_specs=[pl.BlockSpec(memory_space=pltpu.SMEM)] + [vmem] * 4,
        out_specs=[vmem] * 7,
        scratch_shapes=[pltpu.VMEM((2 * width, mine.shape[1]), F32)],
        compiler_params=pltpu.CompilerParams(vmem_limit_bytes=SMALL_VMEM_LIMIT),
        cost_estimate=LONG,
        name="own_shares",
    )(place, mine, near, cross, swap)
    return jnp.swapaxes(conv, 1, 2), cond.T, b_conv, res.T, b_res, skip.T, b_skip


def unfold(halves, width, mel_width):
    _, devices, quarter, lanes = halves.shape
    share = lanes // 2
    halves = halves.astype(F32)
    rest = width - quarter

    def stacked(block, group):
        split_lanes = block.reshape(block.shape[:2] + (lanes // (2 * group), 2, group))
        return jnp.moveaxis(split_lanes, 3, 1).reshape(devices, -1, lanes // 2)

    flat = lambda block: jnp.moveaxis(block, 0, 1).reshape(block.shape[1], -1)
    low, high = halves
    conv = jnp.concatenate([stacked(low, share), stacked(high[:, :rest], share)], 1)
    cond = stacked(high[:, rest : rest + SIDE // 2], share)[:, :mel_width]
    start = rest + SIDE // 2
    both = stacked(high[:, start : start + width // 2], share // 2)
    start = start + width // 2
    b_conv = high[:, start : start + 1, :share]
    b_res = high[:, start + 1 : start + 2, : share // 2]
    b_skip = high[:, start + 1 : start + 2, share : share + share // 2]
    parts = (conv, cond, b_conv, both[:, :, : share // 2], b_res, both[:, :, share // 2 :], b_skip)
    return [flat(part) for part in parts]


def on_device(
    samples, mel, clip_ids, valid, w_conv, w_cond, b_conv, w_res, b_res, w_skip, b_skip, cot_out, cot_skip
):
    section = lax.axis_index("section")
    position = lax.axis_index("tm")
    parts = lax.axis_size("tm")
    count, rows, width = samples.shape
    mel_width = mel.shape[-1]
    per = count // 2
    place = jnp.stack([section, position]).astype(jnp.int32)
    swap = [(0, 1), (1, 0)]
    swapped = lambda a: lax.ppermute(a, "section", swap)

    mel = jnp.swapaxes(mel, 1, 2)
    block, ends = first_halo(per, place, samples, mel, valid)
    forward = shift("tm", 1)
    halos = [lax.ppermute(block, "tm", forward)]
    twice = lax.ppermute(ends, "tm", shift("tm", 2))
    pack = pack_weights(w_conv[0].reshape(2 * width, 2 * width), w_cond, b_conv, w_res, b_res, w_skip, b_skip)
    packs = (pack, swapped(pack))
    *later, heads, side = prep(per, place, samples, mel, clip_ids, valid, cot_out, cot_skip, block)
    for block in later:
        block = lax.optimization_barrier((block, halos[-1]))[0]
        halos.append(lax.ppermute(block, "tm", forward))
    after = lax.ppermute(heads, "tm", shift("tm", -1))

    near_pairs = [(j + 1, j) for j in range(parts - 1)]
    far_pairs = [(parts + j + 1, j) for j in range(parts - 1)]
    axes = ("section", "tm")
    pairs = range(per // 2)
    outs, received, near, far = [], [], [], []
    for pair in pairs:
        out = layers(
            pair, per, mel_width, place, samples, halos[pair], halos[0], side, after, twice, cot_out, cot_skip,
            packs, outs[-1][5:] if outs else [], outs[-1][:2] if outs else [], [],
        )
        outs.append(out)
        if pair == pairs[-1]:
            came = swapped(out[6])
        else:
            received.append(swapped(out[2]))
        if pair == pairs[-1]:
            near.append(lax.ppermute(out[4], "tm", shift("tm", -1)))
            far.append(swapped(near[-1]))
        else:
            near.append(lax.ppermute(out[4], axes, near_pairs))
            far.append(lax.ppermute(out[4], axes, far_pairs))
    act, skip = outs[-1][:2]
    kept, sent = outs[-1][5:]

    def finished(pair, act, skip, grads, waits):
        return finish(pair, place, received[pair], outs[pair][3], near[pair], far[pair], act, skip, grads, waits)

    if parts == 16 and 2 * width // parts == sent.shape[-1] // 2:
        quarter, lanes = sent.shape[-2:]
        pieces = ((0, 144, "yxlh"), (144, 144, "lyxh"), (288, quarter - 288, "xlyh"))
        flips = lambda mask: [(i, i ^ mask) for i in range(parts)]
        sums = [array.reshape((2,) + (2,) * len(AXES) + (quarter, lanes)) for array in (kept, came)]
        terms = [[] for _ in pieces]
        act, skip, grads, token = finished(0, act, skip, None, [sent])
        for step in range(len(AXES) - 1):
            aways = halving_step(step, pieces, place, sums, terms, [token])
            token = aways[0]
            for (_, _, order), away, of_piece in zip(pieces, aways, terms):
                of_piece.append(lax.ppermute(away, "tm", flips(AXES[order[step]])))
            if step == 0:
                last = lax.optimization_barrier((outs[-1][2], terms[0][0]))[0]
                received.append(swapped(last))
            if step == 1:
                act, skip, grads, token = finished(1, act, skip, grads, [token])
        near_sum, cross_sum, swap_sum, mine = last_step(pieces, place, sums, terms)
        mask = AXES["h"]
        crossed = [(s * parts + i, (1 - s) * parts + (i ^ mask)) for s in range(2) for i in range(parts)]
        shares = own_shares(
            place, width, mel_width, mine, lax.ppermute(near_sum, "tm", flips(mask)),
            lax.ppermute(cross_sum, axes, crossed), swapped(swap_sum),
        )
    else:
        received.append(swapped(outs[-1][2]))
        act, skip, grads, _ = finished(0, act, skip, None, [])
        act, skip, grads, _ = finished(1, act, skip, grads, [])
        total = (kept.astype(F32) + came.astype(F32)).astype(BF16)
        mine = jnp.where(section == 0, total[0], total[1])
        got = swapped(jnp.where(section == 0, total[1], total[0]))
        low = jnp.where(section == 0, mine, got)
        high = jnp.where(section == 0, got, mine)
        shares = [
            lax.psum_scatter(part, "tm", scatter_dimension=1, tiled=True)
            for part in unfold(jnp.stack([low, high]), width, mel_width)
        ]
    conv, cond, g_conv, res, g_res, skip_w, g_skip = shares
    flat = lambda a: a.reshape(1, count, rows, width)
    return (
        flat(act),
        flat(skip),
        flat(grads),
        conv.reshape(1, 2, width, -1),
        cond[None],
        g_conv,
        res[None],
        g_res,
        skip_w[None],
        g_skip,
    )


def solution(mesh):
    placed = (
        P(None, "tm", None),
        P(None, "tm", None),
        P(),
        P(None, "tm"),
        P("section", None, None, None),
        P("section", None, None),
        P("section", None),
        P("section", None, None),
        P("section", None),
        P("section", None, None),
        P("section", None),
        P(None, "tm", None),
        P(None, "tm", None),
    )
    return jax.shard_map(
        on_device,
        mesh=mesh,
        in_specs=placed,
        out_specs=(
            P("section", None, "tm", None),
            P("section", None, "tm", None),
            P("section", None, "tm", None),
            P("section", None, None, "tm"),
            P("section", None, "tm"),
            P("section", "tm"),
            P("section", None, "tm"),
            P("section", "tm"),
            P("section", None, "tm"),
            P("section", "tm"),
        ),
        check_vma=False,
    )
```

```python
import functools

import jax
import jax.numpy as jnp
from jax import lax
from jax.experimental import pallas as pl
from jax.experimental.pallas import tpu as pltpu
from jax.sharding import PartitionSpec as P

BF16 = jnp.bfloat16
F32 = jnp.float32
EDGE = 16
SIDE = 128
BIAS_ROWS = 64
CHAIN_SMALL = 16
VMEM_LIMIT = 53 * 1024 * 1024
SMALL_VMEM_LIMIT = 48 * 1024 * 1024
LONG = pl.CostEstimate(flops=10**12, bytes_accessed=10**9, transcendentals=0)


def shift(axis, by):
    devices = lax.axis_size(axis)
    return [(i, i + by) for i in range(devices) if 0 <= i + by < devices]


def nn(left, right):
    return lax.dot_general(left, right, (((1,), (0,)), ((), ())), preferred_element_type=F32)


def nt(left, right):
    return lax.dot_general(left, right, (((1,), (1,)), ((), ())), preferred_element_type=F32)


def tn(left, right):
    return lax.dot_general(left, right, (((0,), (0,)), ((), ())), preferred_element_type=F32)


def sigmoid(v):
    return 0.5 * jnp.tanh(0.5 * v) + 0.5


def tiles(width, step=256):
    return [slice(n, n + step) for n in range(0, width, step)]


def first_halo_kernel(
    per, mel_width, place_ref, mel_ref, valid_ref, x_hbm, halo_hbm, ends_ref, stage, tail, ends, marks, sems
):
    section = place_ref[0]
    rows, width = stage.shape[1:]
    loads = [
        pltpu.make_async_copy(x_hbm.at[section * per + c], stage.at[c], sems.at[c]) for c in range(2)
    ]
    end = pl.ds(rows - EDGE, EDGE)
    end_loads = [
        pltpu.make_async_copy(x_hbm.at[section * per + c, end], ends.at[c], sems.at[5 + c]) for c in range(per)
    ]
    for copy in end_loads + loads:
        copy.start()
    row = lax.broadcasted_iota(jnp.int32, (EDGE, SIDE), 0)
    level = lax.broadcasted_iota(jnp.int32, (SIDE - mel_width, SIDE), 0)
    valid = valid_ref[...].astype(F32)
    for c in range(per):
        own = jnp.where(section == 0, valid[c : c + 1], valid[per + c : per + c + 1])
        marks[:mel_width, :] = mel_ref[c].astype(F32)
        marks[mel_width:, :] = jnp.where(level == 0, own, 0.0)
        last = marks[...].T[SIDE - EDGE :, :]
        tail[:, c * SIDE : (c + 1) * SIDE] = jnp.where(row == EDGE - 1, last, 0.0).astype(BF16)
    stores = [pltpu.make_async_copy(tail, halo_hbm.at[pl.ds(2 * rows, EDGE)], sems.at[4])]
    stores[0].start()
    for c, copy in enumerate(loads):
        copy.wait()
        stores.append(
            pltpu.make_async_copy(stage.at[c], halo_hbm.at[pl.ds(c * rows, rows)], sems.at[2 + c])
        )
        stores[-1].start()
    for copy in end_loads:
        copy.wait()
    line = lax.broadcasted_iota(jnp.int32, (EDGE, width), 0)
    ended = jnp.zeros((EDGE, width), F32)
    for c in range(per):
        ended = jnp.where(line == c, ends[c].astype(F32)[EDGE - 1 : EDGE], ended)
    ends_ref[...] = ended.astype(BF16)
    for copy in stores:
        copy.wait()


def first_halo(per, place, samples, mel, valid):
    count, rows, width = samples.shape
    mel_width = mel.shape[1]
    last = rows // SIDE - 1
    return pl.pallas_call(
        functools.partial(first_halo_kernel, per, mel_width),
        grid_spec=pltpu.PrefetchScalarGridSpec(
            num_scalar_prefetch=1,
            grid=(1,),
            in_specs=[
                pl.BlockSpec((per, mel_width, SIDE), lambda i, s: (s[0], 0, last)),
                pl.BlockSpec((count, SIDE), lambda i, s: (0, last)),
                pl.BlockSpec(memory_space=pl.ANY),
            ],
            out_specs=[
                pl.BlockSpec(memory_space=pl.ANY),
                pl.BlockSpec((EDGE, width), lambda i, s: (0, 0)),
            ],
            scratch_shapes=[
                pltpu.VMEM((2, rows, width), BF16),
                pltpu.VMEM((EDGE, width), BF16),
                pltpu.VMEM((per, EDGE, width), BF16),
                pltpu.VMEM((SIDE, SIDE), F32),
                pltpu.SemaphoreType.DMA((5 + per,)),
            ],
        ),
        out_shape=[
            jax.ShapeDtypeStruct((2 * rows + EDGE, width), BF16),
            jax.ShapeDtypeStruct((EDGE, width), BF16),
        ],
        compiler_params=pltpu.CompilerParams(vmem_limit_bytes=VMEM_LIMIT),
        cost_estimate=LONG,
        name="first_halo",
    )(place, mel, valid, samples)


def pack_kernel(conv_hbm, cond_ref, res_ref, skip_ref, b_conv_ref, b_res_ref, b_skip_ref, pack_hbm, pack, sems):
    _, mel_width, wide = cond_ref.shape
    width = wide // 2
    cond_rows = SIDE
    conv_load = pltpu.make_async_copy(conv_hbm, pack.at[pl.ds(0, wide)], sems.at[0])
    conv_load.start()
    cond_at = wide
    outer_at = cond_at + cond_rows
    pack[cond_at : cond_at + mel_width, :] = cond_ref[0]
    pack[cond_at + mel_width : outer_at, :] = jnp.zeros((cond_rows - mel_width, 2 * width), BF16)
    pack[outer_at : outer_at + width, :width] = res_ref[0]
    pack[outer_at : outer_at + width, width:] = skip_ref[0]
    line = lax.broadcasted_iota(jnp.int32, (CHAIN_SMALL, width), 0)
    for half, lower in ((0, b_res_ref), (1, b_skip_ref)):
        span = slice(half * width, (half + 1) * width)
        first, second = b_conv_ref[0:1, span], lower[0:1, :]
        first_high = first.astype(BF16).astype(F32)
        second_high = second.astype(BF16).astype(F32)
        packed = jnp.where(
            line == 0,
            first_high,
            jnp.where(
                line == 1,
                first - first_high,
                jnp.where(line == 2, second_high, jnp.where(line == 3, second - second_high, 0.0)),
            ),
        )
        pack[outer_at + width :, span] = packed.astype(BF16)
    below = pl.ds(wide, pack.shape[0] - wide)
    stores = [pltpu.make_async_copy(pack.at[below], pack_hbm.at[below], sems.at[1])]
    stores[0].start()
    conv_load.wait()
    above = pl.ds(0, wide)
    stores.append(pltpu.make_async_copy(pack.at[above], pack_hbm.at[above], sems.at[2]))
    stores[1].start()
    for copy in stores:
        copy.wait()


def pack_weights(w_conv, w_cond, b_conv, w_res, b_res, w_skip, b_skip):
    wide = w_conv.shape[-1]
    packed = wide + SIDE + wide // 2 + CHAIN_SMALL
    vmem = pl.BlockSpec(memory_space=pltpu.VMEM)
    any_space = pl.BlockSpec(memory_space=pl.ANY)
    return pl.pallas_call(
        pack_kernel,
        out_shape=jax.ShapeDtypeStruct((packed, wide), BF16),
        in_specs=[any_space] + [vmem] * 6,
        out_specs=any_space,
        scratch_shapes=[pltpu.VMEM((packed, wide), BF16), pltpu.SemaphoreType.DMA((3,))],
        compiler_params=pltpu.CompilerParams(vmem_limit_bytes=VMEM_LIMIT),
        cost_estimate=LONG,
        name="pack_weights",
    )(w_conv, w_cond, w_res, w_skip, b_conv, b_res, b_skip)


def prep_kernel(
    per, mel_width, place_ref, mel_ref, valid_ref, ids_ref, before_ref, earlier_ref, x_hbm, out_cot_hbm,
    skip_cot_hbm, _, *refs,
):
    sources = refs[: per // 2 - 1]
    heads_ref, side_ref = refs[per // 2 - 1 : per // 2 + 1]
    stage, tops, marks, sems = refs[per // 2 + 1 :]
    section, position = place_ref[0], place_ref[1]
    base = section * per
    rows, width = x_hbm.shape[1:]

    copies = []
    loads = [pltpu.make_async_copy(x_hbm.at[base + c], stage.at[c], sems.at[0, c]) for c in range(2, per)]
    pieces = []
    for c in range(per):
        micro = base + c
        top = pl.ds(0, EDGE)
        for i, array in enumerate((x_hbm, out_cot_hbm, skip_cot_hbm)):
            target = tops.at[c, :, pl.ds(i * width, width)]
            pieces.append(pltpu.make_async_copy(array.at[micro, top], target, sems.at[2 + i, c]))
    for copy in loads + pieces:
        copy.start()

    def store(source, target, sem):
        copy = pltpu.make_async_copy(source, target, sem)
        copy.start()
        copies.append(copy)

    for c, copy in enumerate(loads, 2):
        copy.wait()
        store(stage.at[c], sources[c // 2 - 1].at[pl.ds((c % 2) * rows, rows)], sems.at[6, c])

    ids, before, earlier = ids_ref[...], before_ref[...], earlier_ref[...]
    spot = lax.broadcasted_iota(jnp.int32, ids.shape, 1)
    shifted = jnp.where(spot == 0, pltpu.roll(before, 1, 1), pltpu.roll(ids, 1, 1))
    started = position >= 1
    keep0 = jnp.where((ids == before) & started, 1.0, 0.0)
    keep1 = jnp.where((ids == shifted) & (started | (spot > 0)), 1.0, 0.0)
    keep_before = jnp.where((before == earlier) & (position >= 2), 1.0, 0.0)
    valid = valid_ref[...].astype(F32)
    row = lax.broadcasted_iota(jnp.int32, (EDGE, SIDE), 0)
    lane = lax.broadcasted_iota(jnp.int32, (EDGE, SIDE), 1)
    level = lax.broadcasted_iota(jnp.int32, (SIDE - mel_width, rows), 0)

    def pick(values, c):
        low, high = values[c : c + 1], values[per + c : per + c + 1]
        return jnp.where(section == 0, low, high)

    for c in range(per):
        marks[mel_width:, :] = jnp.where(
            level == 0,
            pick(valid, c),
            jnp.where(level == 1, pick(keep0, c), jnp.where(level == 2, pick(keep1, c), 0.0)),
        )
        marks[0:mel_width, :] = mel_ref[c].astype(F32)
        side_ref[c, 0:rows, :] = marks[...].T.astype(BF16)
        kept = jnp.broadcast_to(pick(keep_before, c)[:, rows - 1 : rows], (EDGE, SIDE))
        rim = jnp.where((row == EDGE - 1) & (lane == mel_width + 1), kept, 0.0)
        side_ref[c, rows : rows + EDGE, :] = rim.astype(BF16)
    for copy in pieces:
        copy.wait()
    head_line = lax.broadcasted_iota(jnp.int32, (EDGE, 3 * width), 0)
    heads = jnp.zeros((EDGE, 3 * width), F32)
    sides = jnp.zeros((EDGE, SIDE), F32)
    for c in range(per):
        heads = jnp.where(head_line == c, tops[c].astype(F32)[0:1], heads)
        sides = jnp.where(row == c, side_ref[c, 0:EDGE, :].astype(F32)[0:1], sides)
    heads_ref[:, : 3 * width] = heads.astype(BF16)
    heads_ref[:, 3 * width :] = sides.astype(BF16)
    for copy in copies:
        copy.wait()


def prep(per, place, samples, mel, clip_ids, valid, out_cot, skip_cot, wait):
    count, rows, width = samples.shape
    mel_width = mel.shape[1]
    any_space = pl.BlockSpec(memory_space=pl.ANY)
    whole = lambda a: pl.BlockSpec(a.shape, lambda i, s: (0,) * a.ndim)
    out = lambda *shape: jax.ShapeDtypeStruct(shape, BF16)
    ids = lambda back: pl.BlockSpec((count, rows), lambda i, s: (0, jnp.maximum(s[1] - back, 0)))
    return pl.pallas_call(
        functools.partial(prep_kernel, per, mel_width),
        grid_spec=pltpu.PrefetchScalarGridSpec(
            num_scalar_prefetch=1,
            grid=(1,),
            in_specs=[
                pl.BlockSpec((per, mel_width, rows), lambda i, s: (s[0], 0, 0)),
                whole(valid), ids(0), ids(1), ids(2),
            ]
            + [any_space] * 4,
            out_specs=[any_space] * (per // 2 - 1)
            + [
                pl.BlockSpec((EDGE, 3 * width + SIDE), lambda i, s: (0, 0)),
                pl.BlockSpec((per, rows + EDGE, SIDE), lambda i, s: (0, 0, 0)),
            ],
            scratch_shapes=[
                pltpu.VMEM((per, rows, width), BF16),
                pltpu.VMEM((per, EDGE, 3 * width), BF16),
                pltpu.VMEM((SIDE, rows), F32),
                pltpu.SemaphoreType.DMA((7, per)),
            ],
        ),
        out_shape=[out(2 * rows, width) for _ in range(per // 2 - 1)]
        + [
            out(EDGE, 3 * width + SIDE), out(per, rows + EDGE, SIDE),
        ],
        compiler_params=pltpu.CompilerParams(vmem_limit_bytes=VMEM_LIMIT),
        cost_estimate=LONG,
        name="prep",
    )(
        place, mel, valid, clip_ids, clip_ids, clip_ids, samples, out_cot, skip_cot, wait,
    )


def gate_grads(scaled, th, sg):
    both = scaled * sg
    return both * (1.0 - th * th), both * th * (1.0 - sg)


def fold(blocks, pair, start, top, bottom, group):
    lanes = top.shape[1]
    place = lax.broadcasted_iota(jnp.int32, top.shape, 1)
    low = lax.rem(place, 2 * group) < group
    stop = start + top.shape[0]
    blocks[2 * pair, start:stop, :] = jnp.where(low, top, pltpu.roll(bottom, group, 1))
    blocks[2 * pair + 1, start:stop, :] = jnp.where(low, pltpu.roll(top, lanes - group, 1), bottom)


def beside(res, skip, odd):
    lanes = res.shape[1]
    place = lax.broadcasted_iota(jnp.int32, res.shape, 1)
    if odd:
        return jnp.where(place < lanes // 2, pltpu.roll(res, lanes // 2, 1), skip)
    return jnp.where(place < lanes // 2, res, pltpu.roll(skip, lanes // 2, 1))


def layers_kernel(pair, per, mel_width, waits, reused, place_ref, *refs):
    first_pair = pair == 0
    last_pair = pair == per // 2 - 1
    (
        x_hbm, halo_hbm, tail_hbm, side_hbm, after_hbm, twice_hbm, out_cot_hbm, skip_cot_hbm, pack_own, pack_other,
    ) = refs[:10]
    refs = refs[10 + waits :]
    if not first_pair:
        sums_in, acc_in = refs[:2]
        refs = refs[2:]
    refs = refs[reused:]
    act_hbm, skip_hbm, send_hbm, keep_hbm, back_hbm = refs[:5]
    if last_pair:
        keep_sums_hbm, send_sums_hbm = refs[5:7]
    else:
        sums_ref, acc_hbm = refs[5:7]
    (
        pack, arrived2, joined02, joined12, grads12, grads02, side2, after, twice, tail, tanh0, sig0, tanh1, sig1,
        hidden02, hidden12, act_f, skip_f, act_b, skip_b, dgate12, dgate02, grad_f, lower2, back2, acc, sums, blocks,
        sems, out_sems,
    ) = refs[7:]
    section = place_ref[0]
    other = 1 - section
    rows, width = arrived2.shape[1:]
    wide = 2 * width
    both_rows = slice(0, 2 * rows)
    cond = slice(wide, wide + SIDE)
    outer_rows = wide + SIDE
    outer = slice(outer_rows, outer_rows + width)
    bias_row = outer_rows + width

    def load(source, target, *sem):
        return pltpu.make_async_copy(source, target, sems.at[sem])

    def main(i):
        return slice(i * rows, (i + 1) * rows)

    def rim(i):
        return slice(2 * rows + i * EDGE, 2 * rows + (i + 1) * EDGE)

    def whole(ref, i, span=slice(None)):
        return jnp.concatenate([ref[main(i), span], ref[rim(i), span]], 0)

    def put_whole(ref, i, span, value):
        ref[main(i), span] = value[:rows]
        ref[rim(i), span] = value[rows:]

    first_loads, late_loads = [], []
    for i in range(2):
        chunk = 2 * pair + i
        micro = section * per + chunk
        first_loads.append(
            [
                load(x_hbm.at[micro], joined02.at[main(i), width:], i, 0),
                load(halo_hbm.at[pl.ds(i * rows, rows)], arrived2.at[i], i, 1),
                load(side_hbm.at[chunk, pl.ds(0, rows)], side2.at[main(i)], i, 2),
                load(side_hbm.at[chunk, pl.ds(rows, EDGE)], side2.at[rim(i)], i, 3),
            ]
        )
        late_loads.append(
            [
                load(out_cot_hbm.at[micro], grads12.at[main(i), :width], i, 4),
                load(skip_cot_hbm.at[micro], grads12.at[main(i), width:], i, 5),
            ]
        )
    first_loads[0] += [
        load(after_hbm, after, 2, 0),
        load(twice_hbm, twice, 2, 1),
        load(
            tail_hbm.at[pl.ds(2 * rows, EDGE), pl.ds(2 * pair * SIDE, 2 * SIDE)], tail, 2, 2
        ),
    ]
    def start_pack(layer):
        for which, pack_hbm in ((layer, pack_own), (1 - layer, pack_other)):

            @pl.when(section == which)
            def _():
                load(pack_hbm, pack.at[layer], 2, 3 + layer).start()

    for copy in first_loads[0]:
        copy.start()
    start_pack(0)

    stores = []

    def put(source, target):
        copy = pltpu.make_async_copy(source, target, out_sems.at[len(stores)])
        copy.start()
        stores.append(copy)
        return copy

    columns = tiles(wide)
    spot = lax.broadcasted_iota(jnp.int32, (EDGE, width), 0)
    narrow = lax.broadcasted_iota(jnp.int32, (EDGE, SIDE), 0)
    zero = jnp.zeros((EDGE, width), F32)
    sums[...] = jnp.zeros_like(sums) if first_pair else sums_in[...]

    def bias(layer, which, span):
        both = pack[layer, bias_row : bias_row + CHAIN_SMALL, span].astype(F32)
        return both[2 * which : 2 * which + 1] + both[2 * which + 1 : 2 * which + 2]

    output_stores, finished_stores = [], []
    for i in range(2):
        chunk = 2 * pair + i
        for copy in first_loads[i]:
            copy.wait()
        next_row = after[...].astype(F32)[chunk : chunk + 1]
        next_side = jnp.where(narrow == 0, next_row[:, 3 * width :], 0.0)
        side2[rim(i), :] = side2[rim(i), :] + tail[:, i * SIDE : (i + 1) * SIDE] + next_side.astype(BF16)
        side = whole(side2, i)
        keep0 = side[:, mel_width + 1 : mel_width + 2]
        joined02[main(i), :width] = arrived2[i] * keep0[:rows]
        first = joined02[i * rows : i * rows + EDGE, width:].astype(F32)
        last = arrived2[i, rows - EDGE : rows, :].astype(F32)
        two_back = twice[...].astype(F32)[chunk : chunk + 1]
        early = jnp.where(spot == 0, first, jnp.where(spot == EDGE - 1, two_back, zero))
        joined02[rim(i), :width] = early.astype(BF16) * keep0[rows:]
        here = jnp.where(spot == 0, next_row[:, :width], jnp.where(spot == EDGE - 1, last, zero))
        joined02[rim(i), width:] = here.astype(BF16)
        for n in range(2):
            value = jnp.where(spot == 0, next_row[:, (n + 1) * width : (n + 2) * width], zero)
            grads12[rim(i), n * width : (n + 1) * width] = value.astype(BF16)
        keep0 = keep0[:rows].astype(F32)
        keep1 = side[:, mel_width + 2 : mel_width + 3].astype(F32)
        valid = side[:, mel_width : mel_width + 1].astype(F32)

        def gates(layer, joined, tanh, sig, hidden, kept):
            if i == 0:
                load(pack_own, pack.at[layer], 2, 3 + layer).wait()
                if layer == 0:
                    start_pack(1)
                    for copy in late_loads[0] + first_loads[1] + late_loads[1]:
                        copy.start()
            rows_in = whole(joined, i)
            for part in tiles(width):
                late = slice(part.start + width, part.stop + width)
                left = nn(rows_in, pack[layer, :wide, part]) + nn(side, pack[layer, cond, part])
                right = nn(rows_in, pack[layer, :wide, late]) + nn(side, pack[layer, cond, late])
                th = jnp.tanh(left + bias(layer, 0, part))
                sg = sigmoid(right + bias(layer, 0, late))
                tanh[:, part] = th[:kept]
                sig[:, part] = sg[:kept]
                put_whole(hidden, i, part, (th * sg * valid).astype(BF16))

        gates(0, joined02, tanh0, sig0, hidden02, rows)
        if i == 1 and not first_pair:
            acc_load = load(acc_in, acc, 2, 5)
            acc_load.start()
        for copy in output_stores:
            copy.wait()
            finished_stores.append(copy)
        hidden = whole(hidden02, i)
        for part in tiles(width):
            late = slice(part.start + width, part.stop + width)
            stream = (
                whole(joined02, i, late).astype(F32) + nn(hidden, pack[0, outer, part]) + bias(0, 1, part)
            )
            low = stream.astype(BF16)
            act_f[0, :, part] = stream[:rows]
            act_b[0, :, part] = low[:rows]
            put_whole(joined12, i, late, low)
            put_whole(joined12, i, part, (pltpu.roll(stream, 1, 0) * keep1).astype(BF16))
            skip = nn(hidden[:rows], pack[0, outer, late]) + bias(0, 1, late)
            skip_f[0, :, part] = skip
            skip_b[0, :, part] = skip.astype(BF16)

        gates(1, joined12, tanh1, sig1, hidden12, rows + EDGE)
        hidden = hidden12[main(i), :]
        for part in tiles(width):
            late = slice(part.start + width, part.stop + width)
            stream = act_f[0, :, part] + (nn(hidden, pack[1, outer, part]) + bias(1, 1, part))
            act_f[1, :, part] = stream
            act_b[1, :, part] = stream.astype(BF16)
            skip = skip_f[0, :, part] + (nn(hidden, pack[1, outer, late]) + bias(1, 1, late))
            skip_f[1, :, part] = skip
            skip_b[1, :, part] = skip.astype(BF16)
        output_stores = [
            put(act_b.at[other], send_hbm.at[i, 0]),
            put(skip_b.at[other], send_hbm.at[i, 1]),
            put(act_f.at[section], act_hbm.at[section, chunk]),
            put(skip_f.at[section], skip_hbm.at[section, chunk]),
        ]

        for copy in late_loads[i]:
            copy.wait()
        grads = whole(grads12, i)
        for part in tiles(width):
            late = slice(part.start + width, part.stop + width)
            weight = pack[1, outer_rows + part.start : outer_rows + part.stop, :]
            left, right = gate_grads(nt(grads, weight) * valid, tanh1[:, part], sig1[:, part])
            sums[1, 0:1, part] += jnp.sum(left[:rows], 0, keepdims=True)
            sums[1, 0:1, late] += jnp.sum(right[:rows], 0, keepdims=True)
            put_whole(dgate12, i, part, left.astype(BF16))
            put_whole(dgate12, i, late, right.astype(BF16))
        dgate = whole(dgate12, i)
        for part in tiles(width):
            late = slice(part.start + width, part.stop + width)
            early = nt(dgate, pack[1, part, :]) * keep1
            here = nt(dgate[:rows], pack[1, late, :])
            above = grads12[main(i), part].astype(F32)
            gradient = above + here + pltpu.roll(early, rows + EDGE - 1, 0)[:rows]
            low = gradient.astype(BF16)
            grad_f[:, part] = gradient
            grads02[main(i), part] = low
            grads02[main(i), late] = grads12[main(i), late]
            lower2[i, 1, :, part] = low
            sums[1, 1:2, part] += jnp.sum(above, 0, keepdims=True)
            sums[0, 1:2, part] += jnp.sum(gradient, 0, keepdims=True)
            skip_sum = jnp.sum(grads12[main(i), late].astype(F32), 0, keepdims=True)
            sums[1, 1:2, late] += skip_sum
            sums[0, 1:2, late] += skip_sum

        grads = grads02[main(i), :]
        for part in tiles(width):
            late = slice(part.start + width, part.stop + width)
            weight = pack[0, outer_rows + part.start : outer_rows + part.stop, :]
            left, right = gate_grads(nt(grads, weight) * valid[:rows], tanh0[:, part], sig0[:, part])
            sums[0, 0:1, part] += jnp.sum(left, 0, keepdims=True)
            sums[0, 0:1, late] += jnp.sum(right, 0, keepdims=True)
            dgate02[main(i), part] = left.astype(BF16)
            dgate02[main(i), late] = right.astype(BF16)
        dgate = dgate02[main(i), :]
        for part in tiles(width):
            late = slice(part.start + width, part.stop + width)
            back2[i, :, part] = (nt(dgate, pack[0, part, :]) * keep0).astype(BF16)
            lower2[i, 0, :, part] = (grad_f[:, part] + nt(dgate, pack[0, late, :])).astype(BF16)
        put(back2.at[i], back_hbm.at[i])
        put(lower2.at[i, section], keep_hbm.at[i])
        put(lower2.at[i, other], send_hbm.at[i, 2])

    operands = {
        1: (joined12, dgate12, hidden12, grads12),
        0: (joined02, dgate02, hidden02, grads02),
    }
    def put_half(layer, half):
        copies = [
            pltpu.make_async_copy(blocks.at[layer, half], there.at[layer], out_sems.at[len(stores)])
            for there in (keep_sums_hbm, send_sums_hbm)
        ]
        for mine, copy in zip((section == half, section != half), copies):
            pl.when(mine)(copy.start)
        stores.append(copies[0])

    if not first_pair:
        acc_load.wait()
    quarter, lanes = blocks.shape[-2:]
    turn = lanes // 2
    for layer in (1, 0):
        joined, dgate, hidden, grads = operands[layer]
        outer_sums = []
        for tile in columns:
            conv = tn(joined[both_rows, :], dgate[both_rows, tile])
            conds = tn(side2[both_rows, :], dgate[both_rows, tile])
            if not first_pair:
                conv = conv + acc[layer, :wide, tile].astype(F32)
                conds = conds + acc[layer, wide:outer_rows, tile].astype(F32)
            conv, conds = conv.astype(BF16), conds.astype(BF16)
            if not last_pair:
                acc[layer, :wide, tile] = conv
                acc[layer, wide:outer_rows, tile] = conds
                continue
            for at in range(tile.start, tile.stop, lanes):
                span = slice(at - tile.start, at - tile.start + lanes)
                halves = [blocks.at[layer, half] for half in range(2)]
                value = conv[:, span]
                fold(halves[0], at // lanes, 0, value[:quarter], value[quarter : 2 * quarter], turn)
                value = value[2 * quarter :]
                middle = value.shape[0] // 2
                fold(halves[1], at // lanes, 0, value[:middle], value[middle:], turn)
                value = conds[:, span]
                fold(halves[1], at // lanes, middle, value[: SIDE // 2], value[SIDE // 2 :], turn)
        if last_pair:
            put_half(layer, 0)
        else:
            put(acc.at[layer, :outer_rows], acc_hbm.at[layer, pl.ds(0, outer_rows)])
        for tile in columns:
            outer_sum = tn(hidden[both_rows, :], grads[both_rows, tile])
            if not first_pair:
                outer_sum = outer_sum + acc[layer, outer, tile].astype(F32)
            outer_sum = outer_sum.astype(BF16)
            outer_sums.append(outer_sum)
            if not last_pair:
                acc[layer, outer, tile] = outer_sum
        if not last_pair:
            put(acc.at[layer, outer], acc_hbm.at[layer, pl.ds(outer_rows, width)])
        if last_pair:
            line = lax.broadcasted_iota(jnp.int32, (BIAS_ROWS // 2, lanes), 0)
            total = sums[layer]
            middle = (wide - 2 * quarter + SIDE) // 2
            for zy in range(wide // lanes):
                at = zy // 2 * lanes
                n, span = at // 256, slice(at % 256, at % 256 + lanes)
                value = beside(outer_sums[n][:, span], outer_sums[n + width // 256][:, span], zy % 2)
                fold(blocks.at[layer, 1], zy, middle, value[: width // 2], value[width // 2 :], turn // 2)
                biases = total[0:1, zy * lanes : (zy + 1) * lanes]
                pair_biases = beside(total[:, at : at + lanes], total[:, width + at : width + at + lanes], zy % 2)
                start = middle + width // 2
                for x, (first, second) in enumerate(
                    ((biases, pair_biases[1:2]), (pltpu.roll(total[:, zy * lanes : (zy + 1) * lanes], turn, 1)[0:1], pltpu.roll(pair_biases, lanes - turn // 2, 1)[1:2]))
                ):
                    rows_in = jnp.where(line == 0, first, jnp.where(line == 1, second, 0.0))
                    blocks[layer, 1, 2 * zy + x, start : start + BIAS_ROWS // 2, :] = rows_in.astype(BF16)
            put_half(layer, 1)
    if not last_pair:
        sums_ref[...] = sums[...]
    for store in stores:
        if not any(store is done for done in finished_stores):
            store.wait()


def layers(pair, per, mel_width, place, x, halo, tail, side, after, twice, out_cot, skip_cot, packs, sums, reused, waits):
    count, rows, width = x.shape
    total = rows + EDGE
    wide = 2 * width
    lanes = 128
    any_space = pl.BlockSpec(memory_space=pl.ANY)
    vmem = pl.BlockSpec(memory_space=pltpu.VMEM)
    smem = pl.BlockSpec(memory_space=pltpu.SMEM)
    low = lambda *shape: jax.ShapeDtypeStruct(shape, BF16)
    full = lambda *shape: jax.ShapeDtypeStruct(shape, F32)
    last_pair = pair == per // 2 - 1
    blocks = (wide // (lanes // 2), (3 * width + SIDE + BIAS_ROWS) // 4, lanes)
    first = 11 + len(waits) + len(sums)
    return pl.pallas_call(
        functools.partial(layers_kernel, pair, per, mel_width, len(waits), len(reused)),
        out_shape=[full(2, per, rows, width)] * 2
        + [low(2, 3, rows, width), low(2, rows, width), low(2, rows, width)]
        + ([low(2, *blocks)] * 2 if last_pair else [full(2, 8, wide), low(2, 3 * width + SIDE, wide)]),
        in_specs=[smem]
        + [any_space] * (10 + len(waits))
        + [vmem, any_space][: len(sums)]
        + [any_space] * len(reused),
        out_specs=[any_space] * 5 + ([any_space] * 2 if last_pair else [vmem, any_space]),
        input_output_aliases={first + i: i for i in range(len(reused))},
        scratch_shapes=[
            pltpu.VMEM((2,) + packs[0].shape, BF16),
            pltpu.VMEM((2, rows, width), BF16),
            pltpu.VMEM((2 * total, wide), BF16),
            pltpu.VMEM((2 * total, wide), BF16),
            pltpu.VMEM((2 * total, wide), BF16),
            pltpu.VMEM((2 * rows, wide), BF16),
            pltpu.VMEM((2 * total, SIDE), BF16),
            pltpu.VMEM(after.shape, BF16),
            pltpu.VMEM(twice.shape, BF16),
            pltpu.VMEM((EDGE, 2 * SIDE), BF16),
            pltpu.VMEM((rows, width), F32),
            pltpu.VMEM((rows, width), F32),
            pltpu.VMEM((total, width), F32),
            pltpu.VMEM((total, width), F32),
            pltpu.VMEM((2 * total, width), BF16),
            pltpu.VMEM((2 * total, width), BF16),
            pltpu.VMEM((2, rows, width), F32),
            pltpu.VMEM((2, rows, width), F32),
            pltpu.VMEM((2, rows, width), BF16),
            pltpu.VMEM((2, rows, width), BF16),
            pltpu.VMEM((2 * total, wide), BF16),
            pltpu.VMEM((2 * rows, wide), BF16),
            pltpu.VMEM((rows, width), F32),
            pltpu.VMEM((2, 2, rows, width), BF16),
            pltpu.VMEM((2, rows, width), BF16),
            pltpu.VMEM((2, 3 * width + SIDE, wide), BF16),
            pltpu.VMEM((2, 8, wide), F32),
            pltpu.VMEM((2, 2) + (blocks if last_pair else (1, 16, lanes)), BF16),
            pltpu.SemaphoreType.DMA((3, 6)),
            pltpu.SemaphoreType.DMA((18,)),
        ],
        compiler_params=pltpu.CompilerParams(vmem_limit_bytes=VMEM_LIMIT),
        cost_estimate=LONG,
        name="layers",
    )(place, x, halo, tail, side, after, twice, out_cot, skip_cot, *packs, *waits, *sums, *reused)


def after_all(*arrays):
    def kernel(*refs):
        refs[-1][...] = jnp.zeros_like(refs[-1])

    return pl.pallas_call(
        kernel,
        out_shape=jax.ShapeDtypeStruct((8, 128), F32),
        in_specs=[pl.BlockSpec(memory_space=pl.ANY)] * len(arrays),
        out_specs=pl.BlockSpec(memory_space=pltpu.VMEM),
        cost_estimate=LONG,
        name="after_all",
    )(*arrays)


def finish_kernel(place_ref, received, kept, near, far, *refs):
    act_ref, skip_ref, grads_ref, token_ref = refs[-4:]
    section = place_ref[0]
    act_ref[0] = received[:, 0].astype(F32)
    skip_ref[0] = received[:, 1].astype(F32)
    first_layer = section == 0
    grads_ref[section] = kept[...].astype(F32) + jnp.where(first_layer, near[...].astype(F32), 0.0)
    grads_ref[1 - section] = received[:, 2].astype(F32) + jnp.where(first_layer, far[...].astype(F32), 0.0)
    token_ref[...] = jnp.zeros_like(token_ref)


def finish(pair, place, received, kept, near, far, act, skip, grads, waits):
    per, rows, width = act.shape[1:]
    step = rows // 2
    any_space = pl.BlockSpec(memory_space=pl.ANY)
    part = pl.BlockSpec((2, step, width), lambda i, s: (0, i, 0))
    away = pl.BlockSpec((1, 2, step, width), lambda i, s: (1 - s[0], pair, i, 0))
    reused = [act, skip] + ([] if grads is None else [grads])
    return pl.pallas_call(
        finish_kernel,
        grid_spec=pltpu.PrefetchScalarGridSpec(
            num_scalar_prefetch=1,
            grid=(rows // step,),
            in_specs=[pl.BlockSpec((2, 3, step, width), lambda i, s: (0, 0, i, 0))]
            + [part] * 3
            + [any_space] * (len(waits) + len(reused)),
            out_specs=[
                away,
                away,
                pl.BlockSpec((2, 2, step, width), lambda i, s: (0, pair, i, 0)),
                pl.BlockSpec((8, 128), lambda i, s: (0, 0)),
            ],
        ),
        out_shape=[jax.ShapeDtypeStruct(act.shape, F32)] * 3 + [jax.ShapeDtypeStruct((8, 128), F32)],
        input_output_aliases={5 + len(waits) + i: i for i in range(len(reused))},
        compiler_params=pltpu.CompilerParams(vmem_limit_bytes=VMEM_LIMIT),
        cost_estimate=LONG,
        name="finish",
    )(place, received, kept, near, far, *waits, *reused)


AXES = {"h": 8, "l": 4, "y": 2, "x": 1}


def bits_of(position):
    return {axis: lax.rem(position // mask, 2) for axis, mask in AXES.items()}


def step_kernel(step, pieces, waits, place_ref, *refs):
    count = 2 + step
    terms = [refs[2 + p * step : 2 + (p + 1) * step] for p in range(len(pieces))]
    aways = refs[2 + len(pieces) * step + waits :][: len(pieces)]
    buffers = refs[2 + len(pieces) * step + waits + len(pieces) :]
    sems = buffers[-1]
    bits = bits_of(place_ref[1])
    copies = []
    for p, (start, rows, order) in enumerate(pieces):
        for k, source in enumerate(refs[:2] + terms[p]):
            gone = order[: max(k - 1, 0)]
            index = []
            for axis in AXES:
                if axis in gone:
                    continue
                if axis == order[step]:
                    index.append(1 - bits[axis])
                elif axis in order[:step]:
                    index.append(bits[axis])
                else:
                    index.append(slice(None))
            at = pl.ds(start, rows) if k < 2 else slice(None)
            copy = pltpu.make_async_copy(
                source.at[(slice(None), *index, at)], buffers[p].at[k], sems.at[p, k]
            )
            copy.start()
            copies.append(copy)
    for p in range(len(pieces)):
        for k in range(count):
            copies[p * count + k].wait()
        total = buffers[p][0].astype(F32)
        for k in range(1, count):
            total = total + buffers[p][k].astype(F32)
        aways[p][...] = total.astype(BF16)


def halving_step(step, pieces, place, sums, terms, waits):
    any_space = pl.BlockSpec(memory_space=pl.ANY)
    lanes = sums[0].shape[-1]
    shapes = [(2,) + (2,) * (len(AXES) - 1 - step) + (rows, lanes) for _, rows, _ in pieces]
    flat = [term for of_piece in terms for term in of_piece]
    return pl.pallas_call(
        functools.partial(step_kernel, step, pieces, len(waits)),
        out_shape=[jax.ShapeDtypeStruct(shape, BF16) for shape in shapes],
        in_specs=[pl.BlockSpec(memory_space=pltpu.SMEM)] + [any_space] * (2 + len(flat) + len(waits)),
        out_specs=[pl.BlockSpec(memory_space=pltpu.VMEM)] * len(pieces),
        scratch_shapes=[pltpu.VMEM((2 + step,) + shape, BF16) for shape in shapes]
        + [pltpu.SemaphoreType.DMA((len(pieces), 2 + step))],
        compiler_params=pltpu.CompilerParams(vmem_limit_bytes=SMALL_VMEM_LIMIT),
        cost_estimate=LONG,
        name="halving_step",
    )(place, *sums, *flat, *waits)


def last_kernel(pieces, place_ref, *refs):
    steps = len(AXES) - 1
    count = 2 + steps
    terms = [refs[2 + p * steps : 2 + (p + 1) * steps] for p in range(len(pieces))]
    near_ref, cross_ref, swap_ref, mine_ref, buffer, sems = refs[2 + len(pieces) * steps :]
    section = place_ref[0]
    bits = bits_of(place_ref[1])
    copies = []
    for p, (start, rows, order) in enumerate(pieces):
        for k, source in enumerate(refs[:2] + terms[p]):
            gone = order[: max(k - 1, 0)]
            for side in range(2):
                index = []
                for axis in AXES:
                    if axis not in gone:
                        index.append(bits[axis] if axis in order[:steps] or side else 1 - bits[axis])
                at = pl.ds(start, rows) if k < 2 else slice(None)
                copy = pltpu.make_async_copy(
                    source.at[(slice(None), *index, at)],
                    buffer.at[k, side, :, pl.ds(start, rows)],
                    sems.at[p, k, side],
                )
                copy.start()
                copies.append(copy)
    for copy in copies:
        copy.wait()

    def total(layer, side):
        return sum(buffer[k, side, layer].astype(F32) for k in range(count))

    near_ref[...] = total(section, 0).astype(BF16)
    cross_ref[...] = total(1 - section, 0).astype(BF16)
    swap_ref[...] = total(1 - section, 1).astype(BF16)
    mine_ref[...] = total(section, 1)


def last_step(pieces, place, sums, terms):
    any_space = pl.BlockSpec(memory_space=pl.ANY)
    vmem = pl.BlockSpec(memory_space=pltpu.VMEM)
    shape = sums[0].shape[-2:]
    flat = [term for of_piece in terms for term in of_piece]
    count = len(AXES) + 1
    return pl.pallas_call(
        functools.partial(last_kernel, pieces),
        out_shape=[jax.ShapeDtypeStruct(shape, BF16)] * 3 + [jax.ShapeDtypeStruct(shape, F32)],
        in_specs=[pl.BlockSpec(memory_space=pltpu.SMEM)] + [any_space] * (2 + len(flat)),
        out_specs=[vmem] * 4,
        scratch_shapes=[
            pltpu.VMEM((count, 2, 2) + shape, BF16),
            pltpu.SemaphoreType.DMA((len(pieces), count, 2)),
        ],
        compiler_params=pltpu.CompilerParams(vmem_limit_bytes=SMALL_VMEM_LIMIT),
        cost_estimate=LONG,
        name="last_step",
    )(place, *sums, *flat)


def shares_kernel(
    width, mel_width, place_ref, mine, near, cross, swap, conv, cond, b_conv, res, b_res, skip, b_skip, tall
):
    quarter, lanes = mine.shape
    share = lanes // 2
    own = mine[...] + near[...].astype(F32)
    got = cross[...].astype(F32) + swap[...].astype(F32)
    is_first = place_ref[0] == 0
    low, high = jnp.where(is_first, own, got), jnp.where(is_first, got, own)
    rest = width - quarter
    tall[0:quarter, :] = low
    tall[quarter : 2 * quarter, :] = pltpu.roll(low, share, 1)
    tall[2 * quarter : 2 * quarter + rest, :] = high[:rest]
    tall[2 * quarter + rest : 2 * width, :] = pltpu.roll(high[:rest], share, 1)
    for tap in range(2):
        conv[tap] = tall[tap * width : (tap + 1) * width, :].T[:share]
    value = high[rest : rest + SIDE // 2]
    cond[...] = jnp.concatenate([value, pltpu.roll(value, share, 1)], 0).T[:share, :mel_width]
    start = rest + SIDE // 2
    value = high[start : start + width // 2]
    value = jnp.concatenate([value, pltpu.roll(value, lanes - share // 2, 1)], 0).T
    res[...] = value[: share // 2]
    skip[...] = value[share : share + share // 2]
    biases = high[start + width // 2 : start + width // 2 + 8]
    b_conv[...] = biases[0:1, :share]
    b_res[...] = biases[1:2, : share // 2]
    b_skip[...] = biases[1:2, share : share + share // 2]


def own_shares(place, width, mel_width, mine, near, cross, swap):
    vmem = pl.BlockSpec(memory_space=pltpu.VMEM)
    share = mine.shape[1] // 2
    full = lambda *shape: jax.ShapeDtypeStruct(shape, F32)
    conv, cond, b_conv, res, b_res, skip, b_skip = pl.pallas_call(
        functools.partial(shares_kernel, width, mel_width),
        out_shape=[
            full(2, share, width), full(share, mel_width), full(1, share), full(share // 2, width),
            full(1, share // 2), full(share // 2, width), full(1, share // 2),
        ],
        in_specs=[pl.BlockSpec(memory_space=pltpu.SMEM)] + [vmem] * 4,
        out_specs=[vmem] * 7,
        scratch_shapes=[pltpu.VMEM((2 * width, mine.shape[1]), F32)],
        compiler_params=pltpu.CompilerParams(vmem_limit_bytes=SMALL_VMEM_LIMIT),
        cost_estimate=LONG,
        name="own_shares",
    )(place, mine, near, cross, swap)
    return jnp.swapaxes(conv, 1, 2), cond.T, b_conv, res.T, b_res, skip.T, b_skip


def unfold(halves, width, mel_width):
    _, devices, quarter, lanes = halves.shape
    share = lanes // 2
    halves = halves.astype(F32)
    rest = width - quarter

    def stacked(block, group):
        split_lanes = block.reshape(block.shape[:2] + (lanes // (2 * group), 2, group))
        return jnp.moveaxis(split_lanes, 3, 1).reshape(devices, -1, lanes // 2)

    flat = lambda block: jnp.moveaxis(block, 0, 1).reshape(block.shape[1], -1)
    low, high = halves
    conv = jnp.concatenate([stacked(low, share), stacked(high[:, :rest], share)], 1)
    cond = stacked(high[:, rest : rest + SIDE // 2], share)[:, :mel_width]
    start = rest + SIDE // 2
    both = stacked(high[:, start : start + width // 2], share // 2)
    start = start + width // 2
    b_conv = high[:, start : start + 1, :share]
    b_res = high[:, start + 1 : start + 2, : share // 2]
    b_skip = high[:, start + 1 : start + 2, share : share + share // 2]
    parts = (conv, cond, b_conv, both[:, :, : share // 2], b_res, both[:, :, share // 2 :], b_skip)
    return [flat(part) for part in parts]


def on_device(
    samples, mel, clip_ids, valid, w_conv, w_cond, b_conv, w_res, b_res, w_skip, b_skip, cot_out, cot_skip
):
    section = lax.axis_index("section")
    position = lax.axis_index("tm")
    parts = lax.axis_size("tm")
    count, rows, width = samples.shape
    mel_width = mel.shape[-1]
    per = count // 2
    place = jnp.stack([section, position]).astype(jnp.int32)
    swap = [(0, 1), (1, 0)]
    swapped = lambda a: lax.ppermute(a, "section", swap)

    mel = jnp.swapaxes(mel, 1, 2)
    block, ends = first_halo(per, place, samples, mel, valid)
    forward = shift("tm", 1)
    halos = [lax.ppermute(block, "tm", forward)]
    twice = lax.ppermute(ends, "tm", shift("tm", 2))
    pack = pack_weights(w_conv[0].reshape(2 * width, 2 * width), w_cond, b_conv, w_res, b_res, w_skip, b_skip)
    packs = (pack, swapped(pack))
    *later, heads, side = prep(per, place, samples, mel, clip_ids, valid, cot_out, cot_skip, block)
    for block in later:
        block = lax.optimization_barrier((block, halos[-1]))[0]
        halos.append(lax.ppermute(block, "tm", forward))
    after = lax.ppermute(heads, "tm", shift("tm", -1))

    axes = ("section", "tm")
    pairs = range(per // 2)
    outs, received, near, far = [], [], [], []
    for pair in pairs:
        out = layers(
            pair, per, mel_width, place, samples, halos[pair], halos[0], side, after, twice, cot_out, cot_skip,
            packs, outs[-1][5:] if outs else [], outs[-1][:2] if outs else [], [],
        )
        outs.append(out)
        if pair == pairs[-1]:
            came = swapped(out[6])
        else:
            received.append(swapped(out[2]))
        near.append(lax.ppermute(out[4], "tm", shift("tm", -1)))
    act, skip = outs[-1][:2]
    kept, sent = outs[-1][5:]

    def finished(pair, act, skip, grads, waits):
        return finish(pair, place, received[pair], outs[pair][3], near[pair], far[pair], act, skip, grads, waits)

    if parts == 16 and 2 * width // parts == sent.shape[-1] // 2:
        quarter, lanes = sent.shape[-2:]
        pieces = ((0, 144, "yxlh"), (144, 144, "lyxh"), (288, quarter - 288, "xlyh"))
        flips = lambda mask: [(i, i ^ mask) for i in range(parts)]
        sums = [array.reshape((2,) + (2,) * len(AXES) + (quarter, lanes)) for array in (kept, came)]
        terms = [[] for _ in pieces]
        token = after_all(sent, near[0], received[0])
        far.append(swapped(lax.optimization_barrier((near[0], token))[0]))
        for step in range(len(AXES) - 1):
            aways = halving_step(step, pieces, place, sums, terms, [token])
            token = aways[0]
            for (_, _, order), away, of_piece in zip(pieces, aways, terms):
                of_piece.append(lax.ppermute(away, "tm", flips(AXES[order[step]])))
            if step == 0:
                act, skip, grads, token = finished(0, act, skip, None, [token])
                forward, back = lax.optimization_barrier((outs[-1][2], near[1], token))[:2]
                received.append(swapped(forward))
                far.append(swapped(back))
            if step == 1:
                act, skip, grads, token = finished(1, act, skip, grads, [token])
        near_sum, cross_sum, swap_sum, mine = last_step(pieces, place, sums, terms)
        mask = AXES["h"]
        crossed = [(s * parts + i, (1 - s) * parts + (i ^ mask)) for s in range(2) for i in range(parts)]
        shares = own_shares(
            place, width, mel_width, mine, lax.ppermute(near_sum, "tm", flips(mask)),
            lax.ppermute(cross_sum, axes, crossed), swapped(swap_sum),
        )
    else:
        received.append(swapped(outs[-1][2]))
        far.extend(swapped(back) for back in near)
        act, skip, grads, _ = finished(0, act, skip, None, [])
        act, skip, grads, _ = finished(1, act, skip, grads, [])
        total = (kept.astype(F32) + came.astype(F32)).astype(BF16)
        mine = jnp.where(section == 0, total[0], total[1])
        got = swapped(jnp.where(section == 0, total[1], total[0]))
        low = jnp.where(section == 0, mine, got)
        high = jnp.where(section == 0, got, mine)
        shares = [
            lax.psum_scatter(part, "tm", scatter_dimension=1, tiled=True)
            for part in unfold(jnp.stack([low, high]), width, mel_width)
        ]
    conv, cond, g_conv, res, g_res, skip_w, g_skip = shares
    flat = lambda a: a.reshape(1, count, rows, width)
    return (
        flat(act),
        flat(skip),
        flat(grads),
        conv.reshape(1, 2, width, -1),
        cond[None],
        g_conv,
        res[None],
        g_res,
        skip_w[None],
        g_skip,
    )


def solution(mesh):
    placed = (
        P(None, "tm", None),
        P(None, "tm", None),
        P(),
        P(None, "tm"),
        P("section", None, None, None),
        P("section", None, None),
        P("section", None),
        P("section", None, None),
        P("section", None),
        P("section", None, None),
        P("section", None),
        P(None, "tm", None),
        P(None, "tm", None),
    )
    return jax.shard_map(
        on_device,
        mesh=mesh,
        in_specs=placed,
        out_specs=(
            P("section", None, "tm", None),
            P("section", None, "tm", None),
            P("section", None, "tm", None),
            P("section", None, None, "tm"),
            P("section", None, "tm"),
            P("section", "tm"),
            P("section", None, "tm"),
            P("section", "tm"),
            P("section", None, "tm"),
            P("section", "tm"),
        ),
        check_vma=False,
    )
```

```python
import functools

import jax
import jax.numpy as jnp
from jax import lax
from jax.experimental import pallas as pl
from jax.experimental.pallas import tpu as pltpu
from jax.sharding import PartitionSpec as P

BF16 = jnp.bfloat16
F32 = jnp.float32
EDGE = 16
SIDE = 128
COND_ROWS = 96
BIAS_ROWS = 32
CHAIN_SMALL = 16
VMEM_LIMIT = 53 * 1024 * 1024
WHOLE_VMEM_LIMIT = 60 * 1024 * 1024
SMALL_VMEM_LIMIT = 48 * 1024 * 1024
LONG = pl.CostEstimate(flops=10**12, bytes_accessed=10**9, transcendentals=0)


def shift(axis, by):
    devices = lax.axis_size(axis)
    return [(i, i + by) for i in range(devices) if 0 <= i + by < devices]


def nn(left, right):
    return lax.dot_general(left, right, (((1,), (0,)), ((), ())), preferred_element_type=F32)


def nt(left, right):
    return lax.dot_general(left, right, (((1,), (1,)), ((), ())), preferred_element_type=F32)


def tn(left, right):
    return lax.dot_general(left, right, (((0,), (0,)), ((), ())), preferred_element_type=F32)


def sigmoid(v):
    return 0.5 * jnp.tanh(0.5 * v) + 0.5


def tiles(width, step=256):
    return [slice(n, n + step) for n in range(0, width, step)]


def first_halo_kernel(
    per, mel_width, place_ref, mel_ref, valid_ref, x_hbm, halo_hbm, ends_ref, stage, tail, ends, marks, sems
):
    section = place_ref[0]
    rows, width = stage.shape[1:]
    loads = [
        pltpu.make_async_copy(x_hbm.at[section * per + c], stage.at[c], sems.at[c]) for c in range(2)
    ]
    end = pl.ds(rows - EDGE, EDGE)
    end_loads = [
        pltpu.make_async_copy(x_hbm.at[section * per + c, end], ends.at[c], sems.at[5 + c]) for c in range(per)
    ]
    for copy in end_loads + loads:
        copy.start()
    row = lax.broadcasted_iota(jnp.int32, (EDGE, SIDE), 0)
    level = lax.broadcasted_iota(jnp.int32, (SIDE - mel_width, SIDE), 0)
    valid = valid_ref[...].astype(F32)
    for c in range(per):
        own = jnp.where(section == 0, valid[c : c + 1], valid[per + c : per + c + 1])
        marks[:mel_width, :] = mel_ref[c].astype(F32)
        marks[mel_width:, :] = jnp.where(level == 0, own, 0.0)
        last = marks[...].T[SIDE - EDGE :, :]
        tail[:, c * SIDE : (c + 1) * SIDE] = jnp.where(row == EDGE - 1, last, 0.0).astype(BF16)
    stores = [pltpu.make_async_copy(tail, halo_hbm.at[pl.ds(2 * rows, EDGE)], sems.at[4])]
    stores[0].start()
    for c, copy in enumerate(loads):
        copy.wait()
        stores.append(
            pltpu.make_async_copy(stage.at[c], halo_hbm.at[pl.ds(c * rows, rows)], sems.at[2 + c])
        )
        stores[-1].start()
    for copy in end_loads:
        copy.wait()
    line = lax.broadcasted_iota(jnp.int32, (EDGE, width), 0)
    ended = jnp.zeros((EDGE, width), F32)
    for c in range(per):
        ended = jnp.where(line == c, ends[c].astype(F32)[EDGE - 1 : EDGE], ended)
    ends_ref[...] = ended.astype(BF16)
    for copy in stores:
        copy.wait()


def first_halo(per, place, samples, mel, valid):
    count, rows, width = samples.shape
    mel_width = mel.shape[1]
    last = rows // SIDE - 1
    return pl.pallas_call(
        functools.partial(first_halo_kernel, per, mel_width),
        grid_spec=pltpu.PrefetchScalarGridSpec(
            num_scalar_prefetch=1,
            grid=(1,),
            in_specs=[
                pl.BlockSpec((per, mel_width, SIDE), lambda i, s: (s[0], 0, last)),
                pl.BlockSpec((count, SIDE), lambda i, s: (0, last)),
                pl.BlockSpec(memory_space=pl.ANY),
            ],
            out_specs=[
                pl.BlockSpec(memory_space=pl.ANY),
                pl.BlockSpec((EDGE, width), lambda i, s: (0, 0)),
            ],
            scratch_shapes=[
                pltpu.VMEM((2, rows, width), BF16),
                pltpu.VMEM((EDGE, width), BF16),
                pltpu.VMEM((per, EDGE, width), BF16),
                pltpu.VMEM((SIDE, SIDE), F32),
                pltpu.SemaphoreType.DMA((5 + per,)),
            ],
        ),
        out_shape=[
            jax.ShapeDtypeStruct((2 * rows + EDGE, width), BF16),
            jax.ShapeDtypeStruct((EDGE, width), BF16),
        ],
        compiler_params=pltpu.CompilerParams(vmem_limit_bytes=VMEM_LIMIT),
        cost_estimate=LONG,
        name="first_halo",
    )(place, mel, valid, samples)


def pack_kernel(conv_hbm, cond_ref, res_ref, skip_ref, b_conv_ref, b_res_ref, b_skip_ref, pack_hbm, pack, sems):
    _, mel_width, wide = cond_ref.shape
    width = wide // 2
    cond_rows = SIDE
    conv_load = pltpu.make_async_copy(conv_hbm, pack.at[pl.ds(0, wide)], sems.at[0])
    conv_load.start()
    cond_at = wide
    outer_at = cond_at + cond_rows
    pack[cond_at : cond_at + mel_width, :] = cond_ref[0]
    pack[cond_at + mel_width : outer_at, :] = jnp.zeros((cond_rows - mel_width, 2 * width), BF16)
    pack[outer_at : outer_at + width, :width] = res_ref[0]
    pack[outer_at : outer_at + width, width:] = skip_ref[0]
    line = lax.broadcasted_iota(jnp.int32, (CHAIN_SMALL, width), 0)
    for half, lower in ((0, b_res_ref), (1, b_skip_ref)):
        span = slice(half * width, (half + 1) * width)
        first, second = b_conv_ref[0:1, span], lower[0:1, :]
        first_high = first.astype(BF16).astype(F32)
        second_high = second.astype(BF16).astype(F32)
        packed = jnp.where(
            line == 0,
            first_high,
            jnp.where(
                line == 1,
                first - first_high,
                jnp.where(line == 2, second_high, jnp.where(line == 3, second - second_high, 0.0)),
            ),
        )
        pack[outer_at + width :, span] = packed.astype(BF16)
    below = pl.ds(wide, pack.shape[0] - wide)
    stores = [pltpu.make_async_copy(pack.at[below], pack_hbm.at[below], sems.at[1])]
    stores[0].start()
    conv_load.wait()
    above = pl.ds(0, wide)
    stores.append(pltpu.make_async_copy(pack.at[above], pack_hbm.at[above], sems.at[2]))
    stores[1].start()
    for copy in stores:
        copy.wait()


def pack_weights(w_conv, w_cond, b_conv, w_res, b_res, w_skip, b_skip):
    wide = w_conv.shape[-1]
    packed = wide + SIDE + wide // 2 + CHAIN_SMALL
    vmem = pl.BlockSpec(memory_space=pltpu.VMEM)
    any_space = pl.BlockSpec(memory_space=pl.ANY)
    return pl.pallas_call(
        pack_kernel,
        out_shape=jax.ShapeDtypeStruct((packed, wide), BF16),
        in_specs=[any_space] + [vmem] * 6,
        out_specs=any_space,
        scratch_shapes=[pltpu.VMEM((packed, wide), BF16), pltpu.SemaphoreType.DMA((3,))],
        compiler_params=pltpu.CompilerParams(vmem_limit_bytes=VMEM_LIMIT),
        cost_estimate=LONG,
        name="pack_weights",
    )(w_conv, w_cond, w_res, w_skip, b_conv, b_res, b_skip)


def prep_kernel(
    per, mel_width, place_ref, mel_ref, valid_ref, ids_ref, before_ref, earlier_ref, x_hbm, out_cot_hbm,
    skip_cot_hbm, _, *refs,
):
    sources = refs[: per // 2 - 1]
    heads_ref, side_ref = refs[per // 2 - 1 : per // 2 + 1]
    stage, tops, marks, sems = refs[per // 2 + 1 :]
    section, position = place_ref[0], place_ref[1]
    base = section * per
    rows, width = x_hbm.shape[1:]

    copies = []
    loads = [pltpu.make_async_copy(x_hbm.at[base + c], stage.at[c], sems.at[0, c]) for c in range(2, per)]
    pieces = []
    for c in range(per):
        micro = base + c
        top = pl.ds(0, EDGE)
        for i, array in enumerate((x_hbm, out_cot_hbm, skip_cot_hbm)):
            target = tops.at[c, :, pl.ds(i * width, width)]
            pieces.append(pltpu.make_async_copy(array.at[micro, top], target, sems.at[2 + i, c]))
    for copy in loads + pieces:
        copy.start()

    def store(source, target, sem):
        copy = pltpu.make_async_copy(source, target, sem)
        copy.start()
        copies.append(copy)

    for c, copy in enumerate(loads, 2):
        copy.wait()
        store(stage.at[c], sources[c // 2 - 1].at[pl.ds((c % 2) * rows, rows)], sems.at[6, c])

    ids, before, earlier = ids_ref[...], before_ref[...], earlier_ref[...]
    spot = lax.broadcasted_iota(jnp.int32, ids.shape, 1)
    shifted = jnp.where(spot == 0, pltpu.roll(before, 1, 1), pltpu.roll(ids, 1, 1))
    started = position >= 1
    keep0 = jnp.where((ids == before) & started, 1.0, 0.0)
    keep1 = jnp.where((ids == shifted) & (started | (spot > 0)), 1.0, 0.0)
    keep_before = jnp.where((before == earlier) & (position >= 2), 1.0, 0.0)
    valid = valid_ref[...].astype(F32)
    row = lax.broadcasted_iota(jnp.int32, (EDGE, SIDE), 0)
    lane = lax.broadcasted_iota(jnp.int32, (EDGE, SIDE), 1)
    level = lax.broadcasted_iota(jnp.int32, (SIDE - mel_width, rows), 0)

    def pick(values, c):
        low, high = values[c : c + 1], values[per + c : per + c + 1]
        return jnp.where(section == 0, low, high)

    for c in range(per):
        marks[mel_width:, :] = jnp.where(
            level == 0,
            pick(valid, c),
            jnp.where(level == 1, pick(keep0, c), jnp.where(level == 2, pick(keep1, c), 0.0)),
        )
        marks[0:mel_width, :] = mel_ref[c].astype(F32)
        side_ref[c, 0:rows, :] = marks[...].T.astype(BF16)
        kept = jnp.broadcast_to(pick(keep_before, c)[:, rows - 1 : rows], (EDGE, SIDE))
        rim = jnp.where((row == EDGE - 1) & (lane == mel_width + 1), kept, 0.0)
        side_ref[c, rows : rows + EDGE, :] = rim.astype(BF16)
    for copy in pieces:
        copy.wait()
    head_line = lax.broadcasted_iota(jnp.int32, (EDGE, 3 * width), 0)
    heads = jnp.zeros((EDGE, 3 * width), F32)
    sides = jnp.zeros((EDGE, SIDE), F32)
    for c in range(per):
        heads = jnp.where(head_line == c, tops[c].astype(F32)[0:1], heads)
        sides = jnp.where(row == c, side_ref[c, 0:EDGE, :].astype(F32)[0:1], sides)
    heads_ref[:, : 3 * width] = heads.astype(BF16)
    heads_ref[:, 3 * width :] = sides.astype(BF16)
    for copy in copies:
        copy.wait()


def prep(per, place, samples, mel, clip_ids, valid, out_cot, skip_cot, wait):
    count, rows, width = samples.shape
    mel_width = mel.shape[1]
    any_space = pl.BlockSpec(memory_space=pl.ANY)
    whole = lambda a: pl.BlockSpec(a.shape, lambda i, s: (0,) * a.ndim)
    out = lambda *shape: jax.ShapeDtypeStruct(shape, BF16)
    ids = lambda back: pl.BlockSpec((count, rows), lambda i, s: (0, jnp.maximum(s[1] - back, 0)))
    return pl.pallas_call(
        functools.partial(prep_kernel, per, mel_width),
        grid_spec=pltpu.PrefetchScalarGridSpec(
            num_scalar_prefetch=1,
            grid=(1,),
            in_specs=[
                pl.BlockSpec((per, mel_width, rows), lambda i, s: (s[0], 0, 0)),
                whole(valid), ids(0), ids(1), ids(2),
            ]
            + [any_space] * 4,
            out_specs=[any_space] * (per // 2 - 1)
            + [
                pl.BlockSpec((EDGE, 3 * width + SIDE), lambda i, s: (0, 0)),
                pl.BlockSpec((per, rows + EDGE, SIDE), lambda i, s: (0, 0, 0)),
            ],
            scratch_shapes=[
                pltpu.VMEM((per, rows, width), BF16),
                pltpu.VMEM((per, EDGE, 3 * width), BF16),
                pltpu.VMEM((SIDE, rows), F32),
                pltpu.SemaphoreType.DMA((7, per)),
            ],
        ),
        out_shape=[out(2 * rows, width) for _ in range(per // 2 - 1)]
        + [
            out(EDGE, 3 * width + SIDE), out(per, rows + EDGE, SIDE),
        ],
        compiler_params=pltpu.CompilerParams(vmem_limit_bytes=VMEM_LIMIT),
        cost_estimate=LONG,
        name="prep",
    )(
        place, mel, valid, clip_ids, clip_ids, clip_ids, samples, out_cot, skip_cot, wait,
    )


def gate_grads(scaled, th, sg):
    both = scaled * sg
    return both * (1.0 - th * th), both * th * (1.0 - sg)


def fold(blocks, pair, start, top, bottom, group):
    lanes = top.shape[1]
    place = lax.broadcasted_iota(jnp.int32, top.shape, 1)
    low = lax.rem(place, 2 * group) < group
    stop = start + top.shape[0]
    blocks[2 * pair, start:stop, :] = jnp.where(low, top, pltpu.roll(bottom, group, 1))
    blocks[2 * pair + 1, start:stop, :] = jnp.where(low, pltpu.roll(top, lanes - group, 1), bottom)


def beside(res, skip, odd):
    lanes = res.shape[1]
    place = lax.broadcasted_iota(jnp.int32, res.shape, 1)
    if odd:
        return jnp.where(place < lanes // 2, pltpu.roll(res, lanes // 2, 1), skip)
    return jnp.where(place < lanes // 2, res, pltpu.roll(skip, lanes // 2, 1))


def add_up(operands, side, acc, sums, blocks, earlier, wait, put_sums, put_half):
    wide = acc.shape[-1]
    width = wide // 2
    outer_rows = wide + SIDE
    outer = slice(outer_rows, outer_rows + width)
    columns = tiles(wide)
    if blocks is not None:
        quarter, lanes = blocks.shape[-2:]
        turn = lanes // 2
    for layer in (1, 0):
        joined, dgate, hidden, grads = operands[layer]
        wait(layer)
        outer_sums = []
        for tile in columns:
            conv = tn(joined[...], dgate[:, tile])
            conds = tn(side[...], dgate[:, tile])
            if earlier:
                conv = conv + acc[layer, :wide, tile].astype(F32)
                conds = conds + acc[layer, wide:outer_rows, tile].astype(F32)
            conv, conds = conv.astype(BF16), conds.astype(BF16)
            if blocks is None:
                acc[layer, :wide, tile] = conv
                acc[layer, wide:outer_rows, tile] = conds
                continue
            for at in range(tile.start, tile.stop, lanes):
                span = slice(at - tile.start, at - tile.start + lanes)
                halves = [blocks.at[layer, half] for half in range(2)]
                value = conv[:, span]
                fold(halves[0], at // lanes, 0, value[:quarter], value[quarter : 2 * quarter], turn)
                value = value[2 * quarter :]
                middle = value.shape[0] // 2
                fold(halves[1], at // lanes, 0, value[:middle], value[middle:], turn)
                value = conds[:, span]
                fold(halves[1], at // lanes, middle, value[: COND_ROWS // 2], value[COND_ROWS // 2 : COND_ROWS], turn)
        if blocks is not None:
            put_half(layer, 0)
        else:
            put_sums(layer, slice(0, outer_rows))
        for tile in columns:
            outer_sum = tn(hidden[...], grads[:, tile])
            if earlier:
                outer_sum = outer_sum + acc[layer, outer, tile].astype(F32)
            outer_sum = outer_sum.astype(BF16)
            outer_sums.append(outer_sum)
            if blocks is None:
                acc[layer, outer, tile] = outer_sum
        if blocks is None:
            put_sums(layer, outer)
        if blocks is not None:
            line = lax.broadcasted_iota(jnp.int32, (BIAS_ROWS // 2, lanes), 0)
            total = sums[layer]
            middle = (wide - 2 * quarter + COND_ROWS) // 2
            for zy in range(wide // lanes):
                at = zy // 2 * lanes
                n, span = at // 256, slice(at % 256, at % 256 + lanes)
                value = beside(outer_sums[n][:, span], outer_sums[n + width // 256][:, span], zy % 2)
                fold(blocks.at[layer, 1], zy, middle, value[: width // 2], value[width // 2 :], turn // 2)
                biases = total[0:1, zy * lanes : (zy + 1) * lanes]
                pair_biases = beside(total[:, at : at + lanes], total[:, width + at : width + at + lanes], zy % 2)
                start = middle + width // 2
                for x, (first, second) in enumerate(
                    ((biases, pair_biases[1:2]), (pltpu.roll(total[:, zy * lanes : (zy + 1) * lanes], turn, 1)[0:1], pltpu.roll(pair_biases, lanes - turn // 2, 1)[1:2]))
                ):
                    rows_in = jnp.where(line == 0, first, jnp.where(line == 1, second, 0.0))
                    blocks[layer, 1, 2 * zy + x, start : start + BIAS_ROWS // 2, :] = rows_in.astype(BF16)
            put_half(layer, 1)


def layers_kernel(pair, per, mel_width, waits, reused, place_ref, *refs):
    first_pair = pair == 0
    last_pair = pair == per // 2 - 1
    (
        x_hbm, halo_hbm, tail_hbm, side_hbm, after_hbm, twice_hbm, out_cot_hbm, skip_cot_hbm, pack_own, pack_other,
    ) = refs[:10]
    refs = refs[10 + waits :]
    if not first_pair:
        sums_in, refs = refs[0], refs[1:]
    refs = refs[reused:]
    act_hbm, skip_hbm, send_hbm, keep_hbm, back_hbm = refs[:5]
    sums_ref, refs = refs[5], refs[6:]
    if last_pair:
        operands_hbm, refs = refs[:7], refs[7:]
    else:
        acc_hbm, refs = refs[0], refs[1:]
    (
        pack, arrived2, joined02, joined12, grads12, grads02, side2, after, twice, tail, tanh0, sig0, tanh1, sig1,
        hidden02, hidden12, act_f, skip_f, act_b, skip_b, dgate12, dgate02, grad_f, lower2, back2, acc, sums,
        sems, out_sems,
    ) = refs
    section = place_ref[0]
    other = 1 - section
    rows, width = arrived2.shape[1:]
    wide = 2 * width
    both_rows = slice(0, 2 * rows)
    cond = slice(wide, wide + SIDE)
    outer_rows = wide + SIDE
    outer = slice(outer_rows, outer_rows + width)
    bias_row = outer_rows + width

    def load(source, target, *sem):
        return pltpu.make_async_copy(source, target, sems.at[sem])

    def main(i):
        return slice(i * rows, (i + 1) * rows)

    def rim(i):
        return slice(2 * rows + i * EDGE, 2 * rows + (i + 1) * EDGE)

    def whole(ref, i, span=slice(None)):
        return jnp.concatenate([ref[main(i), span], ref[rim(i), span]], 0)

    def put_whole(ref, i, span, value):
        ref[main(i), span] = value[:rows]
        ref[rim(i), span] = value[rows:]

    first_loads, late_loads = [], []
    for i in range(2):
        chunk = 2 * pair + i
        micro = section * per + chunk
        first_loads.append(
            [
                load(x_hbm.at[micro], joined02.at[main(i), width:], i, 0),
                load(halo_hbm.at[pl.ds(i * rows, rows)], arrived2.at[i], i, 1),
                load(side_hbm.at[chunk, pl.ds(0, rows)], side2.at[main(i)], i, 2),
                load(side_hbm.at[chunk, pl.ds(rows, EDGE)], side2.at[rim(i)], i, 3),
            ]
        )
        late_loads.append(
            [
                load(out_cot_hbm.at[micro], grads12.at[main(i), :width], i, 4),
                load(skip_cot_hbm.at[micro], grads12.at[main(i), width:], i, 5),
            ]
        )
    first_loads[0] += [
        load(after_hbm, after, 2, 0),
        load(twice_hbm, twice, 2, 1),
        load(
            tail_hbm.at[pl.ds(2 * rows, EDGE), pl.ds(2 * pair * SIDE, 2 * SIDE)], tail, 2, 2
        ),
    ]
    def start_pack(layer):
        for which, pack_hbm in ((layer, pack_own), (1 - layer, pack_other)):

            @pl.when(section == which)
            def _():
                load(pack_hbm, pack.at[layer], 2, 3 + layer).start()

    for copy in first_loads[0]:
        copy.start()
    start_pack(0)

    stores = []

    def put(source, target):
        copy = pltpu.make_async_copy(source, target, out_sems.at[len(stores)])
        copy.start()
        stores.append(copy)
        return copy

    columns = tiles(wide)
    spot = lax.broadcasted_iota(jnp.int32, (EDGE, width), 0)
    narrow = lax.broadcasted_iota(jnp.int32, (EDGE, SIDE), 0)
    zero = jnp.zeros((EDGE, width), F32)
    sums[...] = jnp.zeros_like(sums) if first_pair else sums_in[...]

    def bias(layer, which, span):
        both = pack[layer, bias_row : bias_row + CHAIN_SMALL, span].astype(F32)
        return both[2 * which : 2 * which + 1] + both[2 * which + 1 : 2 * which + 2]

    def hand_on(i, which):
        if last_pair:
            for n, ref in which:
                put(ref.at[main(i)], operands_hbm[n].at[main(i)])

    output_stores, finished_stores = [], []
    for i in range(2):
        chunk = 2 * pair + i
        for copy in first_loads[i]:
            copy.wait()
        next_row = after[...].astype(F32)[chunk : chunk + 1]
        next_side = jnp.where(narrow == 0, next_row[:, 3 * width :], 0.0)
        side2[rim(i), :] = side2[rim(i), :] + tail[:, i * SIDE : (i + 1) * SIDE] + next_side.astype(BF16)
        side = whole(side2, i)
        keep0 = side[:, mel_width + 1 : mel_width + 2]
        joined02[main(i), :width] = arrived2[i] * keep0[:rows]
        first = joined02[i * rows : i * rows + EDGE, width:].astype(F32)
        last = arrived2[i, rows - EDGE : rows, :].astype(F32)
        two_back = twice[...].astype(F32)[chunk : chunk + 1]
        early = jnp.where(spot == 0, first, jnp.where(spot == EDGE - 1, two_back, zero))
        joined02[rim(i), :width] = early.astype(BF16) * keep0[rows:]
        here = jnp.where(spot == 0, next_row[:, :width], jnp.where(spot == EDGE - 1, last, zero))
        joined02[rim(i), width:] = here.astype(BF16)
        for n in range(2):
            value = jnp.where(spot == 0, next_row[:, (n + 1) * width : (n + 2) * width], zero)
            grads12[rim(i), n * width : (n + 1) * width] = value.astype(BF16)
        keep0 = keep0[:rows].astype(F32)
        keep1 = side[:, mel_width + 2 : mel_width + 3].astype(F32)
        valid = side[:, mel_width : mel_width + 1].astype(F32)

        def gates(layer, joined, tanh, sig, hidden, kept):
            if i == 0:
                load(pack_own, pack.at[layer], 2, 3 + layer).wait()
                if layer == 0:
                    start_pack(1)
                    for copy in late_loads[0] + first_loads[1] + late_loads[1]:
                        copy.start()
            rows_in = whole(joined, i)
            for part in tiles(width):
                late = slice(part.start + width, part.stop + width)
                left = nn(rows_in, pack[layer, :wide, part]) + nn(side, pack[layer, cond, part])
                right = nn(rows_in, pack[layer, :wide, late]) + nn(side, pack[layer, cond, late])
                th = jnp.tanh(left + bias(layer, 0, part))
                sg = sigmoid(right + bias(layer, 0, late))
                tanh[:, part] = th[:kept]
                sig[:, part] = sg[:kept]
                put_whole(hidden, i, part, (th * sg * valid).astype(BF16))

        gates(0, joined02, tanh0, sig0, hidden02, rows)
        for copy in output_stores:
            copy.wait()
            finished_stores.append(copy)
        hidden = whole(hidden02, i)
        for part in tiles(width):
            late = slice(part.start + width, part.stop + width)
            stream = (
                whole(joined02, i, late).astype(F32) + nn(hidden, pack[0, outer, part]) + bias(0, 1, part)
            )
            low = stream.astype(BF16)
            act_f[0, :, part] = stream[:rows]
            act_b[0, :, part] = low[:rows]
            put_whole(joined12, i, late, low)
            put_whole(joined12, i, part, (pltpu.roll(stream, 1, 0) * keep1).astype(BF16))
            skip = nn(hidden[:rows], pack[0, outer, late]) + bias(0, 1, late)
            skip_f[0, :, part] = skip
            skip_b[0, :, part] = skip.astype(BF16)

        gates(1, joined12, tanh1, sig1, hidden12, rows + EDGE)
        hidden = hidden12[main(i), :]
        for part in tiles(width):
            late = slice(part.start + width, part.stop + width)
            stream = act_f[0, :, part] + (nn(hidden, pack[1, outer, part]) + bias(1, 1, part))
            act_f[1, :, part] = stream
            act_b[1, :, part] = stream.astype(BF16)
            skip = skip_f[0, :, part] + (nn(hidden, pack[1, outer, late]) + bias(1, 1, late))
            skip_f[1, :, part] = skip
            skip_b[1, :, part] = skip.astype(BF16)
        output_stores = [
            put(act_b.at[other], send_hbm.at[i, 0]),
            put(skip_b.at[other], send_hbm.at[i, 1]),
            put(act_f.at[section], act_hbm.at[section, chunk]),
            put(skip_f.at[section], skip_hbm.at[section, chunk]),
        ]

        hand_on(i, ((0, joined12), (2, hidden12), (3, joined02), (5, hidden02)))
        for copy in late_loads[i]:
            copy.wait()
        grads = whole(grads12, i)
        for part in tiles(width):
            late = slice(part.start + width, part.stop + width)
            weight = pack[1, outer_rows + part.start : outer_rows + part.stop, :]
            left, right = gate_grads(nt(grads, weight) * valid, tanh1[:, part], sig1[:, part])
            sums[1, 0:1, part] += jnp.sum(left[:rows], 0, keepdims=True)
            sums[1, 0:1, late] += jnp.sum(right[:rows], 0, keepdims=True)
            put_whole(dgate12, i, part, left.astype(BF16))
            put_whole(dgate12, i, late, right.astype(BF16))
        dgate = whole(dgate12, i)
        for part in tiles(width):
            late = slice(part.start + width, part.stop + width)
            early = nt(dgate, pack[1, part, :]) * keep1
            here = nt(dgate[:rows], pack[1, late, :])
            above = grads12[main(i), part].astype(F32)
            gradient = above + here + pltpu.roll(early, rows + EDGE - 1, 0)[:rows]
            low = gradient.astype(BF16)
            grad_f[:, part] = gradient
            grads02[main(i), part] = low
            grads02[main(i), late] = grads12[main(i), late]
            lower2[i, 1, :, part] = low
            sums[1, 1:2, part] += jnp.sum(above, 0, keepdims=True)
            sums[0, 1:2, part] += jnp.sum(gradient, 0, keepdims=True)
            skip_sum = jnp.sum(grads12[main(i), late].astype(F32), 0, keepdims=True)
            sums[1, 1:2, late] += skip_sum
            sums[0, 1:2, late] += skip_sum

        grads = grads02[main(i), :]
        for part in tiles(width):
            late = slice(part.start + width, part.stop + width)
            weight = pack[0, outer_rows + part.start : outer_rows + part.stop, :]
            left, right = gate_grads(nt(grads, weight) * valid[:rows], tanh0[:, part], sig0[:, part])
            sums[0, 0:1, part] += jnp.sum(left, 0, keepdims=True)
            sums[0, 0:1, late] += jnp.sum(right, 0, keepdims=True)
            dgate02[main(i), part] = left.astype(BF16)
            dgate02[main(i), late] = right.astype(BF16)
        dgate = dgate02[main(i), :]
        for part in tiles(width):
            late = slice(part.start + width, part.stop + width)
            back2[i, :, part] = (nt(dgate, pack[0, part, :]) * keep0).astype(BF16)
            lower2[i, 0, :, part] = (grad_f[:, part] + nt(dgate, pack[0, late, :])).astype(BF16)
        hand_on(i, ((1, dgate12), (4, dgate02), (6, grads02)))
        put(back2.at[i], back_hbm.at[i])
        put(lower2.at[i, section], keep_hbm.at[i])
        put(lower2.at[i, other], send_hbm.at[i, 2])

    operands = {
        1: (joined12, dgate12, hidden12, grads12),
        0: (joined02, dgate02, hidden02, grads02),
    }
    main_rows = lambda ref: ref.at[both_rows]
    if not last_pair:
        add_up(
            {layer: [main_rows(ref) for ref in refs] for layer, refs in operands.items()},
            main_rows(side2), acc, sums, None, False, lambda layer: None,
            lambda layer, span: put(acc.at[layer, span], acc_hbm.at[layer, span]), None,
        )
    sums_ref[...] = sums[...]
    for store in stores:
        if not any(store is done for done in finished_stores):
            store.wait()


def layers(pair, per, mel_width, place, x, halo, tail, side, after, twice, out_cot, skip_cot, packs, sums, reused, waits):
    count, rows, width = x.shape
    total = rows + EDGE
    wide = 2 * width
    any_space = pl.BlockSpec(memory_space=pl.ANY)
    vmem = pl.BlockSpec(memory_space=pltpu.VMEM)
    smem = pl.BlockSpec(memory_space=pltpu.SMEM)
    low = lambda *shape: jax.ShapeDtypeStruct(shape, BF16)
    full = lambda *shape: jax.ShapeDtypeStruct(shape, F32)
    last_pair = pair == per // 2 - 1
    first = 11 + len(waits) + len(sums)
    return pl.pallas_call(
        functools.partial(layers_kernel, pair, per, mel_width, len(waits), len(reused)),
        out_shape=[full(2, per, rows, width)] * 2
        + [low(2, 3, rows, width), low(2, rows, width), low(2, rows, width)]
        + [full(2, 8, wide)]
        + (
            [low(2 * rows, wide), low(2 * rows, wide), low(2 * rows, width)] * 2 + [low(2 * rows, wide)]
            if last_pair
            else [low(2, 3 * width + SIDE, wide)]
        ),
        in_specs=[smem]
        + [any_space] * (10 + len(waits))
        + [vmem] * len(sums)
        + [any_space] * len(reused),
        out_specs=[any_space] * 5 + [vmem] + [any_space] * (7 if last_pair else 1),
        input_output_aliases={first + i: i for i in range(len(reused))},
        scratch_shapes=[
            pltpu.VMEM((2,) + packs[0].shape, BF16),
            pltpu.VMEM((2, rows, width), BF16),
            pltpu.VMEM((2 * total, wide), BF16),
            pltpu.VMEM((2 * total, wide), BF16),
            pltpu.VMEM((2 * total, wide), BF16),
            pltpu.VMEM((2 * rows, wide), BF16),
            pltpu.VMEM((2 * total, SIDE), BF16),
            pltpu.VMEM(after.shape, BF16),
            pltpu.VMEM(twice.shape, BF16),
            pltpu.VMEM((EDGE, 2 * SIDE), BF16),
            pltpu.VMEM((rows, width), F32),
            pltpu.VMEM((rows, width), F32),
            pltpu.VMEM((total, width), F32),
            pltpu.VMEM((total, width), F32),
            pltpu.VMEM((2 * total, width), BF16),
            pltpu.VMEM((2 * total, width), BF16),
            pltpu.VMEM((2, rows, width), F32),
            pltpu.VMEM((2, rows, width), F32),
            pltpu.VMEM((2, rows, width), BF16),
            pltpu.VMEM((2, rows, width), BF16),
            pltpu.VMEM((2 * total, wide), BF16),
            pltpu.VMEM((2 * rows, wide), BF16),
            pltpu.VMEM((rows, width), F32),
            pltpu.VMEM((2, 2, rows, width), BF16),
            pltpu.VMEM((2, rows, width), BF16),
            pltpu.VMEM((2, 3 * width + SIDE, wide) if not last_pair else (2, 16, wide), BF16),
            pltpu.VMEM((2, 8, wide), F32),
            pltpu.SemaphoreType.DMA((3, 6)),
            pltpu.SemaphoreType.DMA((28,)),
        ],
        compiler_params=pltpu.CompilerParams(vmem_limit_bytes=WHOLE_VMEM_LIMIT if last_pair else VMEM_LIMIT),
        cost_estimate=LONG,
        name="layers",
    )(place, x, halo, tail, side, after, twice, out_cot, skip_cot, *packs, *waits, *sums, *reused)


def weights_kernel(
    pair, per, place_ref, x_hbm, side_hbm, out_cot_hbm, skip_cot_hbm, sums_ref, acc_hbm, *refs
):
    sources, refs = refs[:7], refs[7:]
    keep_hbm, send_hbm = refs[:2]
    joined1, dgate1, hidden1, joined0, dgate0, hidden0, grads0, grads1, side, acc, blocks, sems, out_sems = refs[2:]
    section = place_ref[0]
    rows, width = x_hbm.shape[1:]
    count = [0]

    def load(source, target):
        copy = pltpu.make_async_copy(source, target, sems.at[count[0]])
        count[0] += 1
        return copy

    targets = (joined1, dgate1, hidden1, joined0, dgate0, hidden0, grads0)
    given = [load(source, target) for source, target in zip(sources, targets)]
    rest = []
    for i in range(2):
        chunk = 2 * pair + i
        micro = section * per + chunk
        at = pl.ds(i * rows, rows)
        rest += [
            load(side_hbm.at[chunk, pl.ds(0, rows)], side.at[at]),
            load(out_cot_hbm.at[micro], grads1.at[at, pl.ds(0, width)]),
            load(skip_cot_hbm.at[micro], grads1.at[at, pl.ds(width, width)]),
        ]
    sums_so_far = [load(acc_hbm.at[layer], acc.at[layer]) for layer in range(2)]
    second = given[:3] + rest + [sums_so_far[1]]
    first = given[3:] + [sums_so_far[0]]
    for copy in second:
        copy.start()
    stores = []

    def wait(layer):
        if layer == 1:
            for copy in second:
                copy.wait()
            for copy in first:
                copy.start()
        else:
            for copy in first:
                copy.wait()

    def put_half(layer, half):
        copies = [
            pltpu.make_async_copy(blocks.at[layer, half], there.at[layer], out_sems.at[len(stores)])
            for there in (keep_hbm, send_hbm)
        ]
        for mine, copy in zip((section == half, section != half), copies):
            pl.when(mine)(copy.start)
        stores.append(copies[0])

    operands = {1: (joined1, dgate1, hidden1, grads1), 0: (joined0, dgate0, hidden0, grads0)}
    add_up(operands, side, acc, sums_ref, blocks, True, wait, None, put_half)
    for store in stores:
        store.wait()


def weight_sums(pair, per, place, x, side, out_cot, skip_cot, sums, acc, operands):
    _, rows, width = x.shape
    wide = 2 * width
    lanes = 128
    any_space = pl.BlockSpec(memory_space=pl.ANY)
    vmem = pl.BlockSpec(memory_space=pltpu.VMEM)
    blocks = (wide // (lanes // 2), (3 * width + COND_ROWS + BIAS_ROWS) // 4, lanes)
    shape = jax.ShapeDtypeStruct((2,) + blocks, BF16)
    return pl.pallas_call(
        functools.partial(weights_kernel, pair, per),
        out_shape=[shape, shape],
        in_specs=[pl.BlockSpec(memory_space=pltpu.SMEM)] + [any_space] * 4 + [vmem] + [any_space] * 8,
        out_specs=[any_space] * 2,
        scratch_shapes=[pltpu.VMEM(array.shape, BF16) for array in operands]
        + [
            pltpu.VMEM((2 * rows, wide), BF16),
            pltpu.VMEM((2 * rows, SIDE), BF16),
            pltpu.VMEM(acc.shape, BF16),
            pltpu.VMEM((2, 2) + blocks, BF16),
            pltpu.SemaphoreType.DMA((15,)),
            pltpu.SemaphoreType.DMA((4,)),
        ],
        compiler_params=pltpu.CompilerParams(vmem_limit_bytes=WHOLE_VMEM_LIMIT),
        cost_estimate=LONG,
        name="weight_sums",
    )(place, x, side, out_cot, skip_cot, sums, acc, *operands)


def after_all(*arrays):
    def kernel(*refs):
        refs[-1][...] = jnp.zeros_like(refs[-1])

    return pl.pallas_call(
        kernel,
        out_shape=jax.ShapeDtypeStruct((8, 128), F32),
        in_specs=[pl.BlockSpec(memory_space=pl.ANY)] * len(arrays),
        out_specs=pl.BlockSpec(memory_space=pltpu.VMEM),
        cost_estimate=LONG,
        name="after_all",
    )(*arrays)


def finish_kernel(place_ref, received, kept, near, far, *refs):
    act_ref, skip_ref, grads_ref, token_ref = refs[-4:]
    section = place_ref[0]
    act_ref[0] = received[:, 0].astype(F32)
    skip_ref[0] = received[:, 1].astype(F32)
    first_layer = section == 0
    grads_ref[section] = kept[...].astype(F32) + jnp.where(first_layer, near[...].astype(F32), 0.0)
    grads_ref[1 - section] = received[:, 2].astype(F32) + jnp.where(first_layer, far[...].astype(F32), 0.0)
    token_ref[...] = jnp.zeros_like(token_ref)


def finish(pair, place, received, kept, near, far, act, skip, grads, waits):
    per, rows, width = act.shape[1:]
    step = rows // 2
    any_space = pl.BlockSpec(memory_space=pl.ANY)
    part = pl.BlockSpec((2, step, width), lambda i, s: (0, i, 0))
    away = pl.BlockSpec((1, 2, step, width), lambda i, s: (1 - s[0], pair, i, 0))
    reused = [act, skip] + ([] if grads is None else [grads])
    return pl.pallas_call(
        finish_kernel,
        grid_spec=pltpu.PrefetchScalarGridSpec(
            num_scalar_prefetch=1,
            grid=(rows // step,),
            in_specs=[pl.BlockSpec((2, 3, step, width), lambda i, s: (0, 0, i, 0))]
            + [part] * 3
            + [any_space] * (len(waits) + len(reused)),
            out_specs=[
                away,
                away,
                pl.BlockSpec((2, 2, step, width), lambda i, s: (0, pair, i, 0)),
                pl.BlockSpec((8, 128), lambda i, s: (0, 0)),
            ],
        ),
        out_shape=[jax.ShapeDtypeStruct(act.shape, F32)] * 3 + [jax.ShapeDtypeStruct((8, 128), F32)],
        input_output_aliases={5 + len(waits) + i: i for i in range(len(reused))},
        compiler_params=pltpu.CompilerParams(vmem_limit_bytes=VMEM_LIMIT),
        cost_estimate=LONG,
        name="finish",
    )(place, received, kept, near, far, *waits, *reused)


AXES = {"h": 8, "l": 4, "y": 2, "x": 1}


def bits_of(position):
    return {axis: lax.rem(position // mask, 2) for axis, mask in AXES.items()}


def step_kernel(step, pieces, waits, place_ref, *refs):
    count = 2 + step
    terms = [refs[2 + p * step : 2 + (p + 1) * step] for p in range(len(pieces))]
    aways = refs[2 + len(pieces) * step + waits :][: len(pieces)]
    buffers = refs[2 + len(pieces) * step + waits + len(pieces) :]
    sems = buffers[-1]
    bits = bits_of(place_ref[1])
    copies = []
    for p, (start, rows, order) in enumerate(pieces):
        for k, source in enumerate(refs[:2] + terms[p]):
            gone = order[: max(k - 1, 0)]
            index = []
            for axis in AXES:
                if axis in gone:
                    continue
                if axis == order[step]:
                    index.append(1 - bits[axis])
                elif axis in order[:step]:
                    index.append(bits[axis])
                else:
                    index.append(slice(None))
            at = pl.ds(start, rows) if k < 2 else slice(None)
            copy = pltpu.make_async_copy(
                source.at[(slice(None), *index, at)], buffers[p].at[k], sems.at[p, k]
            )
            copy.start()
            copies.append(copy)
    for p in range(len(pieces)):
        for k in range(count):
            copies[p * count + k].wait()
        total = buffers[p][0].astype(F32)
        for k in range(1, count):
            total = total + buffers[p][k].astype(F32)
        aways[p][...] = total.astype(BF16)


def halving_step(step, pieces, place, sums, terms, waits):
    any_space = pl.BlockSpec(memory_space=pl.ANY)
    lanes = sums[0].shape[-1]
    shapes = [(2,) + (2,) * (len(AXES) - 1 - step) + (rows, lanes) for _, rows, _ in pieces]
    flat = [term for of_piece in terms for term in of_piece]
    return pl.pallas_call(
        functools.partial(step_kernel, step, pieces, len(waits)),
        out_shape=[jax.ShapeDtypeStruct(shape, BF16) for shape in shapes],
        in_specs=[pl.BlockSpec(memory_space=pltpu.SMEM)] + [any_space] * (2 + len(flat) + len(waits)),
        out_specs=[pl.BlockSpec(memory_space=pltpu.VMEM)] * len(pieces),
        scratch_shapes=[pltpu.VMEM((2 + step,) + shape, BF16) for shape in shapes]
        + [pltpu.SemaphoreType.DMA((len(pieces), 2 + step))],
        compiler_params=pltpu.CompilerParams(vmem_limit_bytes=SMALL_VMEM_LIMIT),
        cost_estimate=LONG,
        name="halving_step",
    )(place, *sums, *flat, *waits)


def last_kernel(pieces, place_ref, *refs):
    steps = len(AXES) - 1
    count = 2 + steps
    terms = [refs[2 + p * steps : 2 + (p + 1) * steps] for p in range(len(pieces))]
    near_ref, cross_ref, swap_ref, mine_ref, buffer, sems = refs[2 + len(pieces) * steps :]
    section = place_ref[0]
    bits = bits_of(place_ref[1])
    copies = []
    for p, (start, rows, order) in enumerate(pieces):
        for k, source in enumerate(refs[:2] + terms[p]):
            gone = order[: max(k - 1, 0)]
            for side in range(2):
                index = []
                for axis in AXES:
                    if axis not in gone:
                        index.append(bits[axis] if axis in order[:steps] or side else 1 - bits[axis])
                at = pl.ds(start, rows) if k < 2 else slice(None)
                copy = pltpu.make_async_copy(
                    source.at[(slice(None), *index, at)],
                    buffer.at[k, side, :, pl.ds(start, rows)],
                    sems.at[p, k, side],
                )
                copy.start()
                copies.append(copy)
    for copy in copies:
        copy.wait()

    def total(layer, side):
        return sum(buffer[k, side, layer].astype(F32) for k in range(count))

    near_ref[...] = total(section, 0).astype(BF16)
    cross_ref[...] = total(1 - section, 0).astype(BF16)
    swap_ref[...] = total(1 - section, 1).astype(BF16)
    mine_ref[...] = total(section, 1)


def last_step(pieces, place, sums, terms):
    any_space = pl.BlockSpec(memory_space=pl.ANY)
    vmem = pl.BlockSpec(memory_space=pltpu.VMEM)
    shape = sums[0].shape[-2:]
    flat = [term for of_piece in terms for term in of_piece]
    count = len(AXES) + 1
    return pl.pallas_call(
        functools.partial(last_kernel, pieces),
        out_shape=[jax.ShapeDtypeStruct(shape, BF16)] * 3 + [jax.ShapeDtypeStruct(shape, F32)],
        in_specs=[pl.BlockSpec(memory_space=pltpu.SMEM)] + [any_space] * (2 + len(flat)),
        out_specs=[vmem] * 4,
        scratch_shapes=[
            pltpu.VMEM((count, 2, 2) + shape, BF16),
            pltpu.SemaphoreType.DMA((len(pieces), count, 2)),
        ],
        compiler_params=pltpu.CompilerParams(vmem_limit_bytes=SMALL_VMEM_LIMIT),
        cost_estimate=LONG,
        name="last_step",
    )(place, *sums, *flat)


def shares_kernel(
    width, mel_width, place_ref, mine, near, cross, swap, _, conv, cond, b_conv, res, b_res, skip, b_skip, tall
):
    quarter, lanes = mine.shape
    share = lanes // 2
    own = mine[...] + near[...].astype(F32)
    got = cross[...].astype(F32) + swap[...].astype(F32)
    is_first = place_ref[0] == 0
    low, high = jnp.where(is_first, own, got), jnp.where(is_first, got, own)
    rest = width - quarter
    tall[0:quarter, :] = low
    tall[quarter : 2 * quarter, :] = pltpu.roll(low, share, 1)
    tall[2 * quarter : 2 * quarter + rest, :] = high[:rest]
    tall[2 * quarter + rest : 2 * width, :] = pltpu.roll(high[:rest], share, 1)
    for tap in range(2):
        conv[tap] = tall[tap * width : (tap + 1) * width, :].T[:share]
    value = high[rest : rest + COND_ROWS // 2]
    blank = jnp.zeros((lanes - COND_ROWS, lanes), F32)
    cond[...] = jnp.concatenate([value, pltpu.roll(value, share, 1), blank], 0).T[:share, :mel_width]
    start = rest + COND_ROWS // 2
    value = high[start : start + width // 2]
    value = jnp.concatenate([value, pltpu.roll(value, lanes - share // 2, 1)], 0).T
    res[...] = value[: share // 2]
    skip[...] = value[share : share + share // 2]
    biases = high[start + width // 2 : start + width // 2 + 8]
    b_conv[...] = biases[0:1, :share]
    b_res[...] = biases[1:2, : share // 2]
    b_skip[...] = biases[1:2, share : share + share // 2]


def own_shares(place, width, mel_width, mine, near, cross, swap, waits):
    vmem = pl.BlockSpec(memory_space=pltpu.VMEM)
    share = mine.shape[1] // 2
    full = lambda *shape: jax.ShapeDtypeStruct(shape, F32)
    conv, cond, b_conv, res, b_res, skip, b_skip = pl.pallas_call(
        functools.partial(shares_kernel, width, mel_width),
        out_shape=[
            full(2, share, width), full(share, mel_width), full(1, share), full(share // 2, width),
            full(1, share // 2), full(share // 2, width), full(1, share // 2),
        ],
        in_specs=[pl.BlockSpec(memory_space=pltpu.SMEM)] + [vmem] * 4 + [pl.BlockSpec(memory_space=pl.ANY)],
        out_specs=[vmem] * 7,
        scratch_shapes=[pltpu.VMEM((2 * width, mine.shape[1]), F32)],
        compiler_params=pltpu.CompilerParams(vmem_limit_bytes=SMALL_VMEM_LIMIT),
        cost_estimate=LONG,
        name="own_shares",
    )(place, mine, near, cross, swap, *waits)
    return jnp.swapaxes(conv, 1, 2), cond.T, b_conv, res.T, b_res, skip.T, b_skip


def unfold(halves, width, mel_width):
    _, devices, quarter, lanes = halves.shape
    share = lanes // 2
    halves = halves.astype(F32)
    rest = width - quarter

    def stacked(block, group):
        split_lanes = block.reshape(block.shape[:2] + (lanes // (2 * group), 2, group))
        return jnp.moveaxis(split_lanes, 3, 1).reshape(devices, -1, lanes // 2)

    flat = lambda block: jnp.moveaxis(block, 0, 1).reshape(block.shape[1], -1)
    low, high = halves
    conv = jnp.concatenate([stacked(low, share), stacked(high[:, :rest], share)], 1)
    cond = stacked(high[:, rest : rest + COND_ROWS // 2], share)[:, :mel_width]
    start = rest + COND_ROWS // 2
    both = stacked(high[:, start : start + width // 2], share // 2)
    start = start + width // 2
    b_conv = high[:, start : start + 1, :share]
    b_res = high[:, start + 1 : start + 2, : share // 2]
    b_skip = high[:, start + 1 : start + 2, share : share + share // 2]
    parts = (conv, cond, b_conv, both[:, :, : share // 2], b_res, both[:, :, share // 2 :], b_skip)
    return [flat(part) for part in parts]


def on_device(
    samples, mel, clip_ids, valid, w_conv, w_cond, b_conv, w_res, b_res, w_skip, b_skip, cot_out, cot_skip
):
    section = lax.axis_index("section")
    position = lax.axis_index("tm")
    parts = lax.axis_size("tm")
    count, rows, width = samples.shape
    mel_width = mel.shape[-1]
    per = count // 2
    place = jnp.stack([section, position]).astype(jnp.int32)
    swap = [(0, 1), (1, 0)]
    swapped = lambda a: lax.ppermute(a, "section", swap)

    mel = jnp.swapaxes(mel, 1, 2)
    block, ends = first_halo(per, place, samples, mel, valid)
    forward = shift("tm", 1)
    halos = [lax.ppermute(block, "tm", forward)]
    twice = lax.ppermute(ends, "tm", shift("tm", 2))
    pack = pack_weights(w_conv[0].reshape(2 * width, 2 * width), w_cond, b_conv, w_res, b_res, w_skip, b_skip)
    packs = (pack, swapped(pack))
    *later, heads, side = prep(per, place, samples, mel, clip_ids, valid, cot_out, cot_skip, block)
    for block in later:
        block = lax.optimization_barrier((block, halos[-1]))[0]
        halos.append(lax.ppermute(block, "tm", forward))
    after = lax.ppermute(heads, "tm", shift("tm", -1))

    axes = ("section", "tm")
    pairs = range(per // 2)
    outs, received, near, far = [], [], [], []
    for pair in pairs:
        out = layers(
            pair, per, mel_width, place, samples, halos[pair], halos[0], side, after, twice, cot_out, cot_skip,
            packs, [outs[-1][5]] if outs else [], outs[-1][:2] if outs else [], [],
        )
        outs.append(out)
        near.append(lax.ppermute(out[4], "tm", shift("tm", -1)))
        if pair != pairs[-1]:
            received.append(swapped(out[2]))
    kept, sent = weight_sums(
        pairs[-1], per, place, samples, side, cot_out, cot_skip, outs[1][5], outs[0][6], outs[1][6:]
    )
    came = swapped(sent)
    act, skip = outs[-1][:2]

    def finished(pair, act, skip, grads, waits):
        return finish(pair, place, received[pair], outs[pair][3], near[pair], far[pair], act, skip, grads, waits)

    if parts == 16 and 2 * width // parts == sent.shape[-1] // 2:
        quarter, lanes = sent.shape[-2:]
        pieces = ((0, 144, "yxlh"), (144, 144, "lyxh"), (288, quarter - 288, "xlyh"))
        flips = lambda mask: [(i, i ^ mask) for i in range(parts)]
        sums = [array.reshape((2,) + (2,) * len(AXES) + (quarter, lanes)) for array in (kept, came)]
        terms = [[] for _ in pieces]
        token = after_all(sent, near[0], received[0])
        far.append(swapped(lax.optimization_barrier((near[0], token))[0]))
        for step in range(len(AXES) - 1):
            aways = halving_step(step, pieces, place, sums, terms, [token])
            token = aways[0]
            for (_, _, order), away, of_piece in zip(pieces, aways, terms):
                of_piece.append(lax.ppermute(away, "tm", flips(AXES[order[step]])))
            if step == 0:
                act, skip, grads, token = finished(0, act, skip, None, [token])
                forward, back = lax.optimization_barrier((outs[-1][2], near[1], token))[:2]
                received.append(swapped(forward))
                far.append(swapped(back))
            if step == 1:
                act, skip, grads, token = finished(1, act, skip, grads, [token])
        near_sum, cross_sum, swap_sum, mine = last_step(pieces, place, sums, terms)
        mask = AXES["h"]
        crossed = [(s * parts + i, (1 - s) * parts + (i ^ mask)) for s in range(2) for i in range(parts)]
        near_sum, cross_sum, swap_sum = (
            lax.ppermute(near_sum, "tm", flips(mask)), lax.ppermute(cross_sum, axes, crossed), swapped(swap_sum)
        )
        shares = own_shares(place, width, mel_width, mine, near_sum, cross_sum, swap_sum, [token])
    else:
        received.append(swapped(outs[-1][2]))
        far.extend(swapped(back) for back in near)
        act, skip, grads, _ = finished(0, act, skip, None, [])
        act, skip, grads, _ = finished(1, act, skip, grads, [])
        total = (kept.astype(F32) + came.astype(F32)).astype(BF16)
        mine = jnp.where(section == 0, total[0], total[1])
        got = swapped(jnp.where(section == 0, total[1], total[0]))
        low = jnp.where(section == 0, mine, got)
        high = jnp.where(section == 0, got, mine)
        shares = [
            lax.psum_scatter(part, "tm", scatter_dimension=1, tiled=True)
            for part in unfold(jnp.stack([low, high]), width, mel_width)
        ]
    conv, cond, g_conv, res, g_res, skip_w, g_skip = shares
    flat = lambda a: a.reshape(1, count, rows, width)
    return (
        flat(act),
        flat(skip),
        flat(grads),
        conv.reshape(1, 2, width, -1),
        cond[None],
        g_conv,
        res[None],
        g_res,
        skip_w[None],
        g_skip,
    )


def solution(mesh):
    placed = (
        P(None, "tm", None),
        P(None, "tm", None),
        P(),
        P(None, "tm"),
        P("section", None, None, None),
        P("section", None, None),
        P("section", None),
        P("section", None, None),
        P("section", None),
        P("section", None, None),
        P("section", None),
        P(None, "tm", None),
        P(None, "tm", None),
    )
    return jax.shard_map(
        on_device,
        mesh=mesh,
        in_specs=placed,
        out_specs=(
            P("section", None, "tm", None),
            P("section", None, "tm", None),
            P("section", None, "tm", None),
            P("section", None, None, "tm"),
            P("section", None, "tm"),
            P("section", "tm"),
            P("section", None, "tm"),
            P("section", "tm"),
            P("section", None, "tm"),
            P("section", "tm"),
        ),
        check_vma=False,
    )
```

```python
import functools

import jax
import jax.numpy as jnp
from jax import lax
from jax.experimental import pallas as pl
from jax.experimental.pallas import tpu as pltpu
from jax.sharding import PartitionSpec as P

BF16 = jnp.bfloat16
F32 = jnp.float32
EDGE = 16
SIDE = 128
COND_ROWS = 96
BIAS_ROWS = 32
CHAIN_SMALL = 16
VMEM_LIMIT = 53 * 1024 * 1024
WHOLE_VMEM_LIMIT = 60 * 1024 * 1024
SMALL_VMEM_LIMIT = 48 * 1024 * 1024
LONG = pl.CostEstimate(flops=10**12, bytes_accessed=10**9, transcendentals=0)


def shift(axis, by):
    devices = lax.axis_size(axis)
    return [(i, i + by) for i in range(devices) if 0 <= i + by < devices]


def nn(left, right):
    return lax.dot_general(left, right, (((1,), (0,)), ((), ())), preferred_element_type=F32)


def nt(left, right):
    return lax.dot_general(left, right, (((1,), (1,)), ((), ())), preferred_element_type=F32)


def tn(left, right):
    return lax.dot_general(left, right, (((0,), (0,)), ((), ())), preferred_element_type=F32)


def sigmoid(v):
    return 0.5 * jnp.tanh(0.5 * v) + 0.5


def tiles(width, step=256):
    return [slice(n, n + step) for n in range(0, width, step)]


def first_halo_kernel(
    per, mel_width, place_ref, mel_ref, valid_ref, x_hbm, halo_hbm, ends_ref, stage, tail, ends, marks, sems
):
    section = place_ref[0]
    rows, width = stage.shape[1:]
    loads = [
        pltpu.make_async_copy(x_hbm.at[section * per + c], stage.at[c], sems.at[c]) for c in range(2)
    ]
    end = pl.ds(rows - EDGE, EDGE)
    end_loads = [
        pltpu.make_async_copy(x_hbm.at[section * per + c, end], ends.at[c], sems.at[5 + c]) for c in range(per)
    ]
    for copy in end_loads + loads:
        copy.start()
    row = lax.broadcasted_iota(jnp.int32, (EDGE, SIDE), 0)
    level = lax.broadcasted_iota(jnp.int32, (SIDE - mel_width, SIDE), 0)
    valid = valid_ref[...].astype(F32)
    for c in range(per):
        own = jnp.where(section == 0, valid[c : c + 1], valid[per + c : per + c + 1])
        marks[:mel_width, :] = mel_ref[c].astype(F32)
        marks[mel_width:, :] = jnp.where(level == 0, own, 0.0)
        last = marks[...].T[SIDE - EDGE :, :]
        tail[:, c * SIDE : (c + 1) * SIDE] = jnp.where(row == EDGE - 1, last, 0.0).astype(BF16)
    stores = [pltpu.make_async_copy(tail, halo_hbm.at[pl.ds(2 * rows, EDGE)], sems.at[4])]
    stores[0].start()
    for c, copy in enumerate(loads):
        copy.wait()
        stores.append(
            pltpu.make_async_copy(stage.at[c], halo_hbm.at[pl.ds(c * rows, rows)], sems.at[2 + c])
        )
        stores[-1].start()
    for copy in end_loads:
        copy.wait()
    line = lax.broadcasted_iota(jnp.int32, (EDGE, width), 0)
    ended = jnp.zeros((EDGE, width), F32)
    for c in range(per):
        ended = jnp.where(line == c, ends[c].astype(F32)[EDGE - 1 : EDGE], ended)
    ends_ref[...] = ended.astype(BF16)
    for copy in stores:
        copy.wait()


def first_halo(per, place, samples, mel, valid):
    count, rows, width = samples.shape
    mel_width = mel.shape[1]
    last = rows // SIDE - 1
    return pl.pallas_call(
        functools.partial(first_halo_kernel, per, mel_width),
        grid_spec=pltpu.PrefetchScalarGridSpec(
            num_scalar_prefetch=1,
            grid=(1,),
            in_specs=[
                pl.BlockSpec((per, mel_width, SIDE), lambda i, s: (s[0], 0, last)),
                pl.BlockSpec((count, SIDE), lambda i, s: (0, last)),
                pl.BlockSpec(memory_space=pl.ANY),
            ],
            out_specs=[
                pl.BlockSpec(memory_space=pl.ANY),
                pl.BlockSpec((EDGE, width), lambda i, s: (0, 0)),
            ],
            scratch_shapes=[
                pltpu.VMEM((2, rows, width), BF16),
                pltpu.VMEM((EDGE, width), BF16),
                pltpu.VMEM((per, EDGE, width), BF16),
                pltpu.VMEM((SIDE, SIDE), F32),
                pltpu.SemaphoreType.DMA((5 + per,)),
            ],
        ),
        out_shape=[
            jax.ShapeDtypeStruct((2 * rows + EDGE, width), BF16),
            jax.ShapeDtypeStruct((EDGE, width), BF16),
        ],
        compiler_params=pltpu.CompilerParams(vmem_limit_bytes=VMEM_LIMIT),
        cost_estimate=LONG,
        name="first_halo",
    )(place, mel, valid, samples)


def pack_kernel(conv_hbm, cond_ref, res_ref, skip_ref, b_conv_ref, b_res_ref, b_skip_ref, pack_hbm, pack, sems):
    _, mel_width, wide = cond_ref.shape
    width = wide // 2
    cond_rows = SIDE
    conv_load = pltpu.make_async_copy(conv_hbm, pack.at[pl.ds(0, wide)], sems.at[0])
    conv_load.start()
    cond_at = wide
    outer_at = cond_at + cond_rows
    pack[cond_at : cond_at + mel_width, :] = cond_ref[0]
    pack[cond_at + mel_width : outer_at, :] = jnp.zeros((cond_rows - mel_width, 2 * width), BF16)
    pack[outer_at : outer_at + width, :width] = res_ref[0]
    pack[outer_at : outer_at + width, width:] = skip_ref[0]
    line = lax.broadcasted_iota(jnp.int32, (CHAIN_SMALL, width), 0)
    for half, lower in ((0, b_res_ref), (1, b_skip_ref)):
        span = slice(half * width, (half + 1) * width)
        first, second = b_conv_ref[0:1, span], lower[0:1, :]
        first_high = first.astype(BF16).astype(F32)
        second_high = second.astype(BF16).astype(F32)
        packed = jnp.where(
            line == 0,
            first_high,
            jnp.where(
                line == 1,
                first - first_high,
                jnp.where(line == 2, second_high, jnp.where(line == 3, second - second_high, 0.0)),
            ),
        )
        pack[outer_at + width :, span] = packed.astype(BF16)
    below = pl.ds(wide, pack.shape[0] - wide)
    stores = [pltpu.make_async_copy(pack.at[below], pack_hbm.at[below], sems.at[1])]
    stores[0].start()
    conv_load.wait()
    above = pl.ds(0, wide)
    stores.append(pltpu.make_async_copy(pack.at[above], pack_hbm.at[above], sems.at[2]))
    stores[1].start()
    for copy in stores:
        copy.wait()


def pack_weights(w_conv, w_cond, b_conv, w_res, b_res, w_skip, b_skip):
    wide = w_conv.shape[-1]
    packed = wide + SIDE + wide // 2 + CHAIN_SMALL
    vmem = pl.BlockSpec(memory_space=pltpu.VMEM)
    any_space = pl.BlockSpec(memory_space=pl.ANY)
    return pl.pallas_call(
        pack_kernel,
        out_shape=jax.ShapeDtypeStruct((packed, wide), BF16),
        in_specs=[any_space] + [vmem] * 6,
        out_specs=any_space,
        scratch_shapes=[pltpu.VMEM((packed, wide), BF16), pltpu.SemaphoreType.DMA((3,))],
        compiler_params=pltpu.CompilerParams(vmem_limit_bytes=VMEM_LIMIT),
        cost_estimate=LONG,
        name="pack_weights",
    )(w_conv, w_cond, w_res, w_skip, b_conv, b_res, b_skip)


def prep_kernel(
    per, mel_width, place_ref, mel_ref, valid_ref, ids_ref, before_ref, earlier_ref, x_hbm, out_cot_hbm,
    skip_cot_hbm, _, *refs,
):
    sources = refs[: per // 2 - 1]
    heads_ref, side_ref = refs[per // 2 - 1 : per // 2 + 1]
    stage, tops, marks, sems = refs[per // 2 + 1 :]
    section, position = place_ref[0], place_ref[1]
    base = section * per
    rows, width = x_hbm.shape[1:]

    copies = []
    loads = [pltpu.make_async_copy(x_hbm.at[base + c], stage.at[c], sems.at[0, c]) for c in range(2, per)]
    pieces = []
    for c in range(per):
        micro = base + c
        top = pl.ds(0, EDGE)
        for i, array in enumerate((x_hbm, out_cot_hbm, skip_cot_hbm)):
            target = tops.at[c, :, pl.ds(i * width, width)]
            pieces.append(pltpu.make_async_copy(array.at[micro, top], target, sems.at[2 + i, c]))
    for copy in loads + pieces:
        copy.start()

    def store(source, target, sem):
        copy = pltpu.make_async_copy(source, target, sem)
        copy.start()
        copies.append(copy)

    for c, copy in enumerate(loads, 2):
        copy.wait()
        store(stage.at[c], sources[c // 2 - 1].at[pl.ds((c % 2) * rows, rows)], sems.at[6, c])

    ids, before, earlier = ids_ref[...], before_ref[...], earlier_ref[...]
    spot = lax.broadcasted_iota(jnp.int32, ids.shape, 1)
    shifted = jnp.where(spot == 0, pltpu.roll(before, 1, 1), pltpu.roll(ids, 1, 1))
    started = position >= 1
    keep0 = jnp.where((ids == before) & started, 1.0, 0.0)
    keep1 = jnp.where((ids == shifted) & (started | (spot > 0)), 1.0, 0.0)
    keep_before = jnp.where((before == earlier) & (position >= 2), 1.0, 0.0)
    valid = valid_ref[...].astype(F32)
    row = lax.broadcasted_iota(jnp.int32, (EDGE, SIDE), 0)
    lane = lax.broadcasted_iota(jnp.int32, (EDGE, SIDE), 1)
    level = lax.broadcasted_iota(jnp.int32, (SIDE - mel_width, rows), 0)

    def pick(values, c):
        low, high = values[c : c + 1], values[per + c : per + c + 1]
        return jnp.where(section == 0, low, high)

    for c in range(per):
        marks[mel_width:, :] = jnp.where(
            level == 0,
            pick(valid, c),
            jnp.where(level == 1, pick(keep0, c), jnp.where(level == 2, pick(keep1, c), 0.0)),
        )
        marks[0:mel_width, :] = mel_ref[c].astype(F32)
        side_ref[c, 0:rows, :] = marks[...].T.astype(BF16)
        kept = jnp.broadcast_to(pick(keep_before, c)[:, rows - 1 : rows], (EDGE, SIDE))
        rim = jnp.where((row == EDGE - 1) & (lane == mel_width + 1), kept, 0.0)
        side_ref[c, rows : rows + EDGE, :] = rim.astype(BF16)
    for copy in pieces:
        copy.wait()
    head_line = lax.broadcasted_iota(jnp.int32, (EDGE, 3 * width), 0)
    heads = jnp.zeros((EDGE, 3 * width), F32)
    sides = jnp.zeros((EDGE, SIDE), F32)
    for c in range(per):
        heads = jnp.where(head_line == c, tops[c].astype(F32)[0:1], heads)
        sides = jnp.where(row == c, side_ref[c, 0:EDGE, :].astype(F32)[0:1], sides)
    heads_ref[:, : 3 * width] = heads.astype(BF16)
    heads_ref[:, 3 * width :] = sides.astype(BF16)
    for copy in copies:
        copy.wait()


def prep(per, place, samples, mel, clip_ids, valid, out_cot, skip_cot, wait):
    count, rows, width = samples.shape
    mel_width = mel.shape[1]
    any_space = pl.BlockSpec(memory_space=pl.ANY)
    whole = lambda a: pl.BlockSpec(a.shape, lambda i, s: (0,) * a.ndim)
    out = lambda *shape: jax.ShapeDtypeStruct(shape, BF16)
    ids = lambda back: pl.BlockSpec((count, rows), lambda i, s: (0, jnp.maximum(s[1] - back, 0)))
    return pl.pallas_call(
        functools.partial(prep_kernel, per, mel_width),
        grid_spec=pltpu.PrefetchScalarGridSpec(
            num_scalar_prefetch=1,
            grid=(1,),
            in_specs=[
                pl.BlockSpec((per, mel_width, rows), lambda i, s: (s[0], 0, 0)),
                whole(valid), ids(0), ids(1), ids(2),
            ]
            + [any_space] * 4,
            out_specs=[any_space] * (per // 2 - 1)
            + [
                pl.BlockSpec((EDGE, 3 * width + SIDE), lambda i, s: (0, 0)),
                pl.BlockSpec((per, rows + EDGE, SIDE), lambda i, s: (0, 0, 0)),
            ],
            scratch_shapes=[
                pltpu.VMEM((per, rows, width), BF16),
                pltpu.VMEM((per, EDGE, 3 * width), BF16),
                pltpu.VMEM((SIDE, rows), F32),
                pltpu.SemaphoreType.DMA((7, per)),
            ],
        ),
        out_shape=[out(2 * rows, width) for _ in range(per // 2 - 1)]
        + [
            out(EDGE, 3 * width + SIDE), out(per, rows + EDGE, SIDE),
        ],
        compiler_params=pltpu.CompilerParams(vmem_limit_bytes=VMEM_LIMIT),
        cost_estimate=LONG,
        name="prep",
    )(
        place, mel, valid, clip_ids, clip_ids, clip_ids, samples, out_cot, skip_cot, wait,
    )


def gate_grads(scaled, th, sg):
    both = scaled * sg
    return both * (1.0 - th * th), both * th * (1.0 - sg)


def fold(blocks, pair, start, top, bottom, group):
    lanes = top.shape[1]
    place = lax.broadcasted_iota(jnp.int32, top.shape, 1)
    low = lax.rem(place, 2 * group) < group
    stop = start + top.shape[0]
    blocks[2 * pair, start:stop, :] = jnp.where(low, top, pltpu.roll(bottom, group, 1))
    blocks[2 * pair + 1, start:stop, :] = jnp.where(low, pltpu.roll(top, lanes - group, 1), bottom)


def beside(res, skip, odd):
    lanes = res.shape[1]
    place = lax.broadcasted_iota(jnp.int32, res.shape, 1)
    if odd:
        return jnp.where(place < lanes // 2, pltpu.roll(res, lanes // 2, 1), skip)
    return jnp.where(place < lanes // 2, res, pltpu.roll(skip, lanes // 2, 1))


def add_up(operands, side, acc, sums, blocks, earlier, wait, put_sums, put_half):
    wide = acc.shape[-1]
    width = wide // 2
    outer_rows = wide + SIDE
    outer = slice(outer_rows, outer_rows + width)
    columns = tiles(wide)
    if blocks is not None:
        quarter, lanes = blocks.shape[-2:]
        turn = lanes // 2
    for layer in (1, 0):
        joined, dgate, hidden, grads = operands[layer]
        wait(layer)
        outer_sums = []
        for tile in columns:
            conv = tn(joined[...], dgate[:, tile])
            conds = tn(side[...], dgate[:, tile])
            if earlier:
                conv = conv + acc[layer, :wide, tile].astype(F32)
                conds = conds + acc[layer, wide:outer_rows, tile].astype(F32)
            conv, conds = conv.astype(BF16), conds.astype(BF16)
            if blocks is None:
                acc[layer, :wide, tile] = conv
                acc[layer, wide:outer_rows, tile] = conds
                continue
            for at in range(tile.start, tile.stop, lanes):
                span = slice(at - tile.start, at - tile.start + lanes)
                halves = [blocks.at[layer, half] for half in range(2)]
                value = conv[:, span]
                fold(halves[0], at // lanes, 0, value[:quarter], value[quarter : 2 * quarter], turn)
                value = value[2 * quarter :]
                middle = value.shape[0] // 2
                fold(halves[1], at // lanes, 0, value[:middle], value[middle:], turn)
                value = conds[:, span]
                fold(halves[1], at // lanes, middle, value[: COND_ROWS // 2], value[COND_ROWS // 2 : COND_ROWS], turn)
        if blocks is not None:
            put_half(layer, 0)
        else:
            put_sums(layer, slice(0, outer_rows))
        for tile in columns:
            outer_sum = tn(hidden[...], grads[:, tile])
            if earlier:
                outer_sum = outer_sum + acc[layer, outer, tile].astype(F32)
            outer_sum = outer_sum.astype(BF16)
            outer_sums.append(outer_sum)
            if blocks is None:
                acc[layer, outer, tile] = outer_sum
        if blocks is None:
            put_sums(layer, outer)
        if blocks is not None:
            line = lax.broadcasted_iota(jnp.int32, (BIAS_ROWS // 2, lanes), 0)
            total = sums[layer]
            middle = (wide - 2 * quarter + COND_ROWS) // 2
            for zy in range(wide // lanes):
                at = zy // 2 * lanes
                n, span = at // 256, slice(at % 256, at % 256 + lanes)
                value = beside(outer_sums[n][:, span], outer_sums[n + width // 256][:, span], zy % 2)
                fold(blocks.at[layer, 1], zy, middle, value[: width // 2], value[width // 2 :], turn // 2)
                biases = total[0:1, zy * lanes : (zy + 1) * lanes]
                pair_biases = beside(total[:, at : at + lanes], total[:, width + at : width + at + lanes], zy % 2)
                start = middle + width // 2
                for x, (first, second) in enumerate(
                    ((biases, pair_biases[1:2]), (pltpu.roll(total[:, zy * lanes : (zy + 1) * lanes], turn, 1)[0:1], pltpu.roll(pair_biases, lanes - turn // 2, 1)[1:2]))
                ):
                    rows_in = jnp.where(line == 0, first, jnp.where(line == 1, second, 0.0))
                    blocks[layer, 1, 2 * zy + x, start : start + BIAS_ROWS // 2, :] = rows_in.astype(BF16)
            put_half(layer, 1)


def layers_kernel(pair, per, mel_width, waits, reused, place_ref, *refs):
    first_pair = pair == 0
    last_pair = pair == per // 2 - 1
    (
        x_hbm, halo_hbm, tail_hbm, side_hbm, after_hbm, twice_hbm, out_cot_hbm, skip_cot_hbm, pack_own, pack_other,
    ) = refs[:10]
    refs = refs[10 + waits :]
    if not first_pair:
        sums_in, refs = refs[0], refs[1:]
    refs = refs[reused:]
    act_hbm, skip_hbm, send_hbm, keep_hbm, back_hbm = refs[:5]
    sums_ref, refs = refs[5], refs[6:]
    if last_pair:
        operands_hbm, refs = refs[:7], refs[7:]
    else:
        acc_hbm, refs = refs[0], refs[1:]
    (
        pack, arrived2, joined02, joined12, grads12, grads02, side2, after, twice, tail, tanh0, sig0, tanh1, sig1,
        hidden02, hidden12, act_f, skip_f, act_b, skip_b, dgate12, dgate02, grad_f, lower2, back2, acc, sums,
        sems, out_sems,
    ) = refs
    section = place_ref[0]
    other = 1 - section
    rows, width = arrived2.shape[1:]
    wide = 2 * width
    both_rows = slice(0, 2 * rows)
    cond = slice(wide, wide + SIDE)
    outer_rows = wide + SIDE
    outer = slice(outer_rows, outer_rows + width)
    bias_row = outer_rows + width

    def load(source, target, *sem):
        return pltpu.make_async_copy(source, target, sems.at[sem])

    def main(i):
        return slice(i * rows, (i + 1) * rows)

    def rim(i):
        return slice(2 * rows + i * EDGE, 2 * rows + (i + 1) * EDGE)

    def whole(ref, i, span=slice(None)):
        return jnp.concatenate([ref[main(i), span], ref[rim(i), span]], 0)

    def put_whole(ref, i, span, value):
        ref[main(i), span] = value[:rows]
        ref[rim(i), span] = value[rows:]

    first_loads, late_loads = [], []
    for i in range(2):
        chunk = 2 * pair + i
        micro = section * per + chunk
        first_loads.append(
            [
                load(x_hbm.at[micro], joined02.at[main(i), width:], i, 0),
                load(halo_hbm.at[pl.ds(i * rows, rows)], arrived2.at[i], i, 1),
                load(side_hbm.at[chunk, pl.ds(0, rows)], side2.at[main(i)], i, 2),
                load(side_hbm.at[chunk, pl.ds(rows, EDGE)], side2.at[rim(i)], i, 3),
            ]
        )
        late_loads.append(
            [
                load(out_cot_hbm.at[micro], grads12.at[main(i), :width], i, 4),
                load(skip_cot_hbm.at[micro], grads12.at[main(i), width:], i, 5),
            ]
        )
    first_loads[0] += [
        load(after_hbm, after, 2, 0),
        load(twice_hbm, twice, 2, 1),
        load(
            tail_hbm.at[pl.ds(2 * rows, EDGE), pl.ds(2 * pair * SIDE, 2 * SIDE)], tail, 2, 2
        ),
    ]
    def start_pack(layer):
        for which, pack_hbm in ((layer, pack_own), (1 - layer, pack_other)):

            @pl.when(section == which)
            def _():
                load(pack_hbm, pack.at[layer], 2, 3 + layer).start()

    for copy in first_loads[0]:
        copy.start()
    start_pack(0)

    stores = []

    def put(source, target):
        copy = pltpu.make_async_copy(source, target, out_sems.at[len(stores)])
        copy.start()
        stores.append(copy)
        return copy

    columns = tiles(wide)
    spot = lax.broadcasted_iota(jnp.int32, (EDGE, width), 0)
    narrow = lax.broadcasted_iota(jnp.int32, (EDGE, SIDE), 0)
    zero = jnp.zeros((EDGE, width), F32)
    sums[...] = jnp.zeros_like(sums) if first_pair else sums_in[...]

    def bias(layer, which, span):
        both = pack[layer, bias_row : bias_row + CHAIN_SMALL, span].astype(F32)
        return both[2 * which : 2 * which + 1] + both[2 * which + 1 : 2 * which + 2]

    def hand_on(i, which):
        if last_pair:
            for n, ref in which:
                put(ref.at[main(i)], operands_hbm[n].at[main(i)])

    output_stores, finished_stores = [], []
    for i in range(2):
        chunk = 2 * pair + i
        for copy in first_loads[i]:
            copy.wait()
        next_row = after[...].astype(F32)[chunk : chunk + 1]
        next_side = jnp.where(narrow == 0, next_row[:, 3 * width :], 0.0)
        side2[rim(i), :] = side2[rim(i), :] + tail[:, i * SIDE : (i + 1) * SIDE] + next_side.astype(BF16)
        side = whole(side2, i)
        keep0 = side[:, mel_width + 1 : mel_width + 2]
        joined02[main(i), :width] = arrived2[i] * keep0[:rows]
        first = joined02[i * rows : i * rows + EDGE, width:].astype(F32)
        last = arrived2[i, rows - EDGE : rows, :].astype(F32)
        two_back = twice[...].astype(F32)[chunk : chunk + 1]
        early = jnp.where(spot == 0, first, jnp.where(spot == EDGE - 1, two_back, zero))
        joined02[rim(i), :width] = early.astype(BF16) * keep0[rows:]
        here = jnp.where(spot == 0, next_row[:, :width], jnp.where(spot == EDGE - 1, last, zero))
        joined02[rim(i), width:] = here.astype(BF16)
        for n in range(2):
            value = jnp.where(spot == 0, next_row[:, (n + 1) * width : (n + 2) * width], zero)
            grads12[rim(i), n * width : (n + 1) * width] = value.astype(BF16)
        keep0 = keep0[:rows].astype(F32)
        keep1 = side[:, mel_width + 2 : mel_width + 3].astype(F32)
        valid = side[:, mel_width : mel_width + 1].astype(F32)

        def gates(layer, joined, tanh, sig, hidden, kept):
            if i == 0:
                load(pack_own, pack.at[layer], 2, 3 + layer).wait()
                if layer == 0:
                    start_pack(1)
                    for copy in late_loads[0] + first_loads[1] + late_loads[1]:
                        copy.start()
            rows_in = whole(joined, i)
            for part in tiles(width):
                late = slice(part.start + width, part.stop + width)
                left = nn(rows_in, pack[layer, :wide, part]) + nn(side, pack[layer, cond, part])
                right = nn(rows_in, pack[layer, :wide, late]) + nn(side, pack[layer, cond, late])
                th = jnp.tanh(left + bias(layer, 0, part))
                sg = sigmoid(right + bias(layer, 0, late))
                tanh[:, part] = th[:kept]
                sig[:, part] = sg[:kept]
                put_whole(hidden, i, part, (th * sg * valid).astype(BF16))

        gates(0, joined02, tanh0, sig0, hidden02, rows)
        for copy in output_stores:
            copy.wait()
            finished_stores.append(copy)
        hidden = whole(hidden02, i)
        for part in tiles(width):
            late = slice(part.start + width, part.stop + width)
            stream = (
                whole(joined02, i, late).astype(F32) + nn(hidden, pack[0, outer, part]) + bias(0, 1, part)
            )
            low = stream.astype(BF16)
            act_f[0, :, part] = stream[:rows]
            act_b[0, :, part] = low[:rows]
            put_whole(joined12, i, late, low)
            put_whole(joined12, i, part, (pltpu.roll(stream, 1, 0) * keep1).astype(BF16))
            skip = nn(hidden[:rows], pack[0, outer, late]) + bias(0, 1, late)
            skip_f[0, :, part] = skip
            skip_b[0, :, part] = skip.astype(BF16)

        gates(1, joined12, tanh1, sig1, hidden12, rows + EDGE)
        hidden = hidden12[main(i), :]
        for part in tiles(width):
            late = slice(part.start + width, part.stop + width)
            stream = act_f[0, :, part] + (nn(hidden, pack[1, outer, part]) + bias(1, 1, part))
            act_f[1, :, part] = stream
            act_b[1, :, part] = stream.astype(BF16)
            skip = skip_f[0, :, part] + (nn(hidden, pack[1, outer, late]) + bias(1, 1, late))
            skip_f[1, :, part] = skip
            skip_b[1, :, part] = skip.astype(BF16)
        output_stores = [
            put(act_b.at[other], send_hbm.at[i, 0]),
            put(skip_b.at[other], send_hbm.at[i, 1]),
            put(act_f.at[section], act_hbm.at[section, chunk]),
            put(skip_f.at[section], skip_hbm.at[section, chunk]),
        ]

        hand_on(i, ((0, joined12), (2, hidden12), (3, joined02), (5, hidden02)))
        for copy in late_loads[i]:
            copy.wait()
        grads = whole(grads12, i)
        for part in tiles(width):
            late = slice(part.start + width, part.stop + width)
            weight = pack[1, outer_rows + part.start : outer_rows + part.stop, :]
            left, right = gate_grads(nt(grads, weight) * valid, tanh1[:, part], sig1[:, part])
            sums[1, 0:1, part] += jnp.sum(left[:rows], 0, keepdims=True)
            sums[1, 0:1, late] += jnp.sum(right[:rows], 0, keepdims=True)
            put_whole(dgate12, i, part, left.astype(BF16))
            put_whole(dgate12, i, late, right.astype(BF16))
        dgate = whole(dgate12, i)
        for part in tiles(width):
            late = slice(part.start + width, part.stop + width)
            early = nt(dgate, pack[1, part, :]) * keep1
            here = nt(dgate[:rows], pack[1, late, :])
            above = grads12[main(i), part].astype(F32)
            gradient = above + here + pltpu.roll(early, rows + EDGE - 1, 0)[:rows]
            low = gradient.astype(BF16)
            grad_f[:, part] = gradient
            grads02[main(i), part] = low
            grads02[main(i), late] = grads12[main(i), late]
            lower2[i, 1, :, part] = low
            sums[1, 1:2, part] += jnp.sum(above, 0, keepdims=True)
            sums[0, 1:2, part] += jnp.sum(gradient, 0, keepdims=True)
            skip_sum = jnp.sum(grads12[main(i), late].astype(F32), 0, keepdims=True)
            sums[1, 1:2, late] += skip_sum
            sums[0, 1:2, late] += skip_sum

        grads = grads02[main(i), :]
        for part in tiles(width):
            late = slice(part.start + width, part.stop + width)
            weight = pack[0, outer_rows + part.start : outer_rows + part.stop, :]
            left, right = gate_grads(nt(grads, weight) * valid[:rows], tanh0[:, part], sig0[:, part])
            sums[0, 0:1, part] += jnp.sum(left, 0, keepdims=True)
            sums[0, 0:1, late] += jnp.sum(right, 0, keepdims=True)
            dgate02[main(i), part] = left.astype(BF16)
            dgate02[main(i), late] = right.astype(BF16)
        dgate = dgate02[main(i), :]
        for part in tiles(width):
            late = slice(part.start + width, part.stop + width)
            back2[i, :, part] = (nt(dgate, pack[0, part, :]) * keep0).astype(BF16)
            lower2[i, 0, :, part] = (grad_f[:, part] + nt(dgate, pack[0, late, :])).astype(BF16)
        hand_on(i, ((1, dgate12), (4, dgate02), (6, grads02)))
        put(back2.at[i], back_hbm.at[i])
        put(lower2.at[i, section], keep_hbm.at[i])
        put(lower2.at[i, other], send_hbm.at[i, 2])

    operands = {
        1: (joined12, dgate12, hidden12, grads12),
        0: (joined02, dgate02, hidden02, grads02),
    }
    main_rows = lambda ref: ref.at[both_rows]
    if not last_pair:
        add_up(
            {layer: [main_rows(ref) for ref in refs] for layer, refs in operands.items()},
            main_rows(side2), acc, sums, None, False, lambda layer: None,
            lambda layer, span: put(acc.at[layer, span], acc_hbm.at[layer, span]), None,
        )
    sums_ref[...] = sums[...]
    for store in stores:
        if not any(store is done for done in finished_stores):
            store.wait()


def layers(pair, per, mel_width, place, x, halo, tail, side, after, twice, out_cot, skip_cot, packs, sums, reused, waits):
    count, rows, width = x.shape
    total = rows + EDGE
    wide = 2 * width
    any_space = pl.BlockSpec(memory_space=pl.ANY)
    vmem = pl.BlockSpec(memory_space=pltpu.VMEM)
    smem = pl.BlockSpec(memory_space=pltpu.SMEM)
    low = lambda *shape: jax.ShapeDtypeStruct(shape, BF16)
    full = lambda *shape: jax.ShapeDtypeStruct(shape, F32)
    last_pair = pair == per // 2 - 1
    first = 11 + len(waits) + len(sums)
    return pl.pallas_call(
        functools.partial(layers_kernel, pair, per, mel_width, len(waits), len(reused)),
        out_shape=[full(2, per, rows, width)] * 2
        + [low(2, 3, rows, width), low(2, rows, width), low(2, rows, width)]
        + [full(2, 8, wide)]
        + (
            [low(2 * rows, wide), low(2 * rows, wide), low(2 * rows, width)] * 2 + [low(2 * rows, wide)]
            if last_pair
            else [low(2, 3 * width + SIDE, wide)]
        ),
        in_specs=[smem]
        + [any_space] * (10 + len(waits))
        + [vmem] * len(sums)
        + [any_space] * len(reused),
        out_specs=[any_space] * 5 + [vmem] + [any_space] * (7 if last_pair else 1),
        input_output_aliases={first + i: i for i in range(len(reused))},
        scratch_shapes=[
            pltpu.VMEM((2,) + packs[0].shape, BF16),
            pltpu.VMEM((2, rows, width), BF16),
            pltpu.VMEM((2 * total, wide), BF16),
            pltpu.VMEM((2 * total, wide), BF16),
            pltpu.VMEM((2 * total, wide), BF16),
            pltpu.VMEM((2 * rows, wide), BF16),
            pltpu.VMEM((2 * total, SIDE), BF16),
            pltpu.VMEM(after.shape, BF16),
            pltpu.VMEM(twice.shape, BF16),
            pltpu.VMEM((EDGE, 2 * SIDE), BF16),
            pltpu.VMEM((rows, width), F32),
            pltpu.VMEM((rows, width), F32),
            pltpu.VMEM((total, width), F32),
            pltpu.VMEM((total, width), F32),
            pltpu.VMEM((2 * total, width), BF16),
            pltpu.VMEM((2 * total, width), BF16),
            pltpu.VMEM((2, rows, width), F32),
            pltpu.VMEM((2, rows, width), F32),
            pltpu.VMEM((2, rows, width), BF16),
            pltpu.VMEM((2, rows, width), BF16),
            pltpu.VMEM((2 * total, wide), BF16),
            pltpu.VMEM((2 * rows, wide), BF16),
            pltpu.VMEM((rows, width), F32),
            pltpu.VMEM((2, 2, rows, width), BF16),
            pltpu.VMEM((2, rows, width), BF16),
            pltpu.VMEM((2, 3 * width + SIDE, wide) if not last_pair else (2, 16, wide), BF16),
            pltpu.VMEM((2, 8, wide), F32),
            pltpu.SemaphoreType.DMA((3, 6)),
            pltpu.SemaphoreType.DMA((28,)),
        ],
        compiler_params=pltpu.CompilerParams(vmem_limit_bytes=WHOLE_VMEM_LIMIT if last_pair else VMEM_LIMIT),
        cost_estimate=LONG,
        name="layers",
    )(place, x, halo, tail, side, after, twice, out_cot, skip_cot, *packs, *waits, *sums, *reused)


def weights_kernel(
    pair, per, place_ref, x_hbm, side_hbm, out_cot_hbm, skip_cot_hbm, sums_ref, acc_hbm, *refs
):
    sources, refs = refs[:7], refs[7:]
    keep_hbm, send_hbm = refs[:2]
    joined1, dgate1, hidden1, joined0, dgate0, hidden0, grads0, grads1, side, acc, blocks, sems, out_sems = refs[2:]
    section = place_ref[0]
    rows, width = x_hbm.shape[1:]
    count = [0]

    def load(source, target):
        copy = pltpu.make_async_copy(source, target, sems.at[count[0]])
        count[0] += 1
        return copy

    targets = (joined1, dgate1, hidden1, joined0, dgate0, hidden0, grads0)
    given = [load(source, target) for source, target in zip(sources, targets)]
    rest = []
    for i in range(2):
        chunk = 2 * pair + i
        micro = section * per + chunk
        at = pl.ds(i * rows, rows)
        rest += [
            load(side_hbm.at[chunk, pl.ds(0, rows)], side.at[at]),
            load(out_cot_hbm.at[micro], grads1.at[at, pl.ds(0, width)]),
            load(skip_cot_hbm.at[micro], grads1.at[at, pl.ds(width, width)]),
        ]
    sums_so_far = [load(acc_hbm.at[layer], acc.at[layer]) for layer in range(2)]
    second = given[:3] + rest + [sums_so_far[1]]
    first = given[3:] + [sums_so_far[0]]
    for copy in second:
        copy.start()
    stores = []

    def wait(layer):
        if layer == 1:
            for copy in second:
                copy.wait()
            for copy in first:
                copy.start()
        else:
            for copy in first:
                copy.wait()

    def put_half(layer, half):
        copies = [
            pltpu.make_async_copy(blocks.at[layer, half], there.at[layer], out_sems.at[len(stores)])
            for there in (keep_hbm, send_hbm)
        ]
        for mine, copy in zip((section == half, section != half), copies):
            pl.when(mine)(copy.start)
        stores.append(copies[0])

    operands = {1: (joined1, dgate1, hidden1, grads1), 0: (joined0, dgate0, hidden0, grads0)}
    add_up(operands, side, acc, sums_ref, blocks, True, wait, None, put_half)
    for store in stores:
        store.wait()


def weight_sums(pair, per, place, x, side, out_cot, skip_cot, sums, acc, operands):
    _, rows, width = x.shape
    wide = 2 * width
    lanes = 128
    any_space = pl.BlockSpec(memory_space=pl.ANY)
    vmem = pl.BlockSpec(memory_space=pltpu.VMEM)
    blocks = (wide // (lanes // 2), (3 * width + COND_ROWS + BIAS_ROWS) // 4, lanes)
    shape = jax.ShapeDtypeStruct((2,) + blocks, BF16)
    return pl.pallas_call(
        functools.partial(weights_kernel, pair, per),
        out_shape=[shape, shape],
        in_specs=[pl.BlockSpec(memory_space=pltpu.SMEM)] + [any_space] * 4 + [vmem] + [any_space] * 8,
        out_specs=[any_space] * 2,
        scratch_shapes=[pltpu.VMEM(array.shape, BF16) for array in operands]
        + [
            pltpu.VMEM((2 * rows, wide), BF16),
            pltpu.VMEM((2 * rows, SIDE), BF16),
            pltpu.VMEM(acc.shape, BF16),
            pltpu.VMEM((2, 2) + blocks, BF16),
            pltpu.SemaphoreType.DMA((15,)),
            pltpu.SemaphoreType.DMA((4,)),
        ],
        compiler_params=pltpu.CompilerParams(vmem_limit_bytes=WHOLE_VMEM_LIMIT),
        cost_estimate=LONG,
        name="weight_sums",
    )(place, x, side, out_cot, skip_cot, sums, acc, *operands)


def after_all(*arrays):
    def kernel(*refs):
        refs[-1][...] = jnp.zeros_like(refs[-1])

    return pl.pallas_call(
        kernel,
        out_shape=jax.ShapeDtypeStruct((8, 128), F32),
        in_specs=[pl.BlockSpec(memory_space=pl.ANY)] * len(arrays),
        out_specs=pl.BlockSpec(memory_space=pltpu.VMEM),
        cost_estimate=LONG,
        name="after_all",
    )(*arrays)


def finish_kernel(place_ref, received, kept, near, far, *refs):
    act_ref, skip_ref, grads_ref, token_ref = refs[-4:]
    section = place_ref[0]
    act_ref[0] = received[:, 0].astype(F32)
    skip_ref[0] = received[:, 1].astype(F32)
    first_layer = section == 0
    grads_ref[section] = kept[...].astype(F32) + jnp.where(first_layer, near[...].astype(F32), 0.0)
    grads_ref[1 - section] = received[:, 2].astype(F32) + jnp.where(first_layer, far[...].astype(F32), 0.0)
    token_ref[...] = jnp.zeros_like(token_ref)


def finish(pair, place, received, kept, near, far, act, skip, grads, waits):
    per, rows, width = act.shape[1:]
    step = rows // 2
    any_space = pl.BlockSpec(memory_space=pl.ANY)
    part = pl.BlockSpec((2, step, width), lambda i, s: (0, i, 0))
    away = pl.BlockSpec((1, 2, step, width), lambda i, s: (1 - s[0], pair, i, 0))
    reused = [act, skip] + ([] if grads is None else [grads])
    return pl.pallas_call(
        finish_kernel,
        grid_spec=pltpu.PrefetchScalarGridSpec(
            num_scalar_prefetch=1,
            grid=(rows // step,),
            in_specs=[pl.BlockSpec((2, 3, step, width), lambda i, s: (0, 0, i, 0))]
            + [part] * 3
            + [any_space] * (len(waits) + len(reused)),
            out_specs=[
                away,
                away,
                pl.BlockSpec((2, 2, step, width), lambda i, s: (0, pair, i, 0)),
                pl.BlockSpec((8, 128), lambda i, s: (0, 0)),
            ],
        ),
        out_shape=[jax.ShapeDtypeStruct(act.shape, F32)] * 3 + [jax.ShapeDtypeStruct((8, 128), F32)],
        input_output_aliases={5 + len(waits) + i: i for i in range(len(reused))},
        compiler_params=pltpu.CompilerParams(vmem_limit_bytes=VMEM_LIMIT),
        cost_estimate=LONG,
        name="finish",
    )(place, received, kept, near, far, *waits, *reused)


AXES = {"h": 8, "l": 4, "y": 2, "x": 1}


def bits_of(position):
    return {axis: lax.rem(position // mask, 2) for axis, mask in AXES.items()}


def step_kernel(step, pieces, waits, place_ref, *refs):
    count = 2 + step
    terms = [refs[2 + p * step : 2 + (p + 1) * step] for p in range(len(pieces))]
    aways = refs[2 + len(pieces) * step + waits :][: len(pieces)]
    buffers = refs[2 + len(pieces) * step + waits + len(pieces) :]
    sems = buffers[-1]
    bits = bits_of(place_ref[1])
    copies = []
    for p, (start, rows, order) in enumerate(pieces):
        for k, source in enumerate(refs[:2] + terms[p]):
            gone = order[: max(k - 1, 0)]
            index = []
            for axis in AXES:
                if axis in gone:
                    continue
                if axis == order[step]:
                    index.append(1 - bits[axis])
                elif axis in order[:step]:
                    index.append(bits[axis])
                else:
                    index.append(slice(None))
            at = pl.ds(start, rows) if k < 2 else slice(None)
            copy = pltpu.make_async_copy(
                source.at[(slice(None), *index, at)], buffers[p].at[k], sems.at[p, k]
            )
            copy.start()
            copies.append(copy)
    for p in range(len(pieces)):
        for k in range(count):
            copies[p * count + k].wait()
        total = buffers[p][0].astype(F32)
        for k in range(1, count):
            total = total + buffers[p][k].astype(F32)
        aways[p][...] = total.astype(BF16)


def halving_step(step, pieces, place, sums, terms, waits):
    any_space = pl.BlockSpec(memory_space=pl.ANY)
    lanes = sums[0].shape[-1]
    shapes = [(2,) + (2,) * (len(AXES) - 1 - step) + (rows, lanes) for _, rows, _ in pieces]
    flat = [term for of_piece in terms for term in of_piece]
    return pl.pallas_call(
        functools.partial(step_kernel, step, pieces, len(waits)),
        out_shape=[jax.ShapeDtypeStruct(shape, BF16) for shape in shapes],
        in_specs=[pl.BlockSpec(memory_space=pltpu.SMEM)] + [any_space] * (2 + len(flat) + len(waits)),
        out_specs=[pl.BlockSpec(memory_space=pltpu.VMEM)] * len(pieces),
        scratch_shapes=[pltpu.VMEM((2 + step,) + shape, BF16) for shape in shapes]
        + [pltpu.SemaphoreType.DMA((len(pieces), 2 + step))],
        compiler_params=pltpu.CompilerParams(vmem_limit_bytes=SMALL_VMEM_LIMIT),
        cost_estimate=LONG,
        name="halving_step",
    )(place, *sums, *flat, *waits)


def last_kernel(pieces, place_ref, *refs):
    steps = len(AXES) - 1
    count = 2 + steps
    terms = [refs[2 + p * steps : 2 + (p + 1) * steps] for p in range(len(pieces))]
    near_ref, cross_ref, swap_ref, mine_ref, buffer, sems = refs[2 + len(pieces) * steps :]
    section = place_ref[0]
    bits = bits_of(place_ref[1])
    copies = []
    for p, (start, rows, order) in enumerate(pieces):
        for k, source in enumerate(refs[:2] + terms[p]):
            gone = order[: max(k - 1, 0)]
            for side in range(2):
                index = []
                for axis in AXES:
                    if axis not in gone:
                        index.append(bits[axis] if axis in order[:steps] or side else 1 - bits[axis])
                at = pl.ds(start, rows) if k < 2 else slice(None)
                copy = pltpu.make_async_copy(
                    source.at[(slice(None), *index, at)],
                    buffer.at[k, side, :, pl.ds(start, rows)],
                    sems.at[p, k, side],
                )
                copy.start()
                copies.append(copy)
    for copy in copies:
        copy.wait()

    def total(layer, side):
        return sum(buffer[k, side, layer].astype(F32) for k in range(count))

    near_ref[...] = total(section, 0).astype(BF16)
    cross_ref[...] = total(1 - section, 0).astype(BF16)
    swap_ref[...] = total(1 - section, 1).astype(BF16)
    mine_ref[...] = total(section, 1)


def last_step(pieces, place, sums, terms):
    any_space = pl.BlockSpec(memory_space=pl.ANY)
    vmem = pl.BlockSpec(memory_space=pltpu.VMEM)
    shape = sums[0].shape[-2:]
    flat = [term for of_piece in terms for term in of_piece]
    count = len(AXES) + 1
    return pl.pallas_call(
        functools.partial(last_kernel, pieces),
        out_shape=[jax.ShapeDtypeStruct(shape, BF16)] * 3 + [jax.ShapeDtypeStruct(shape, F32)],
        in_specs=[pl.BlockSpec(memory_space=pltpu.SMEM)] + [any_space] * (2 + len(flat)),
        out_specs=[vmem] * 4,
        scratch_shapes=[
            pltpu.VMEM((count, 2, 2) + shape, BF16),
            pltpu.SemaphoreType.DMA((len(pieces), count, 2)),
        ],
        compiler_params=pltpu.CompilerParams(vmem_limit_bytes=SMALL_VMEM_LIMIT),
        cost_estimate=LONG,
        name="last_step",
    )(place, *sums, *flat)


def shares_kernel(
    width, mel_width, place_ref, mine, near, cross, swap, _, conv, cond, b_conv, res, b_res, skip, b_skip, tall
):
    quarter, lanes = mine.shape
    share = lanes // 2
    own = mine[...] + near[...].astype(F32)
    got = cross[...].astype(F32) + swap[...].astype(F32)
    is_first = place_ref[0] == 0
    low, high = jnp.where(is_first, own, got), jnp.where(is_first, got, own)
    rest = width - quarter
    tall[0:quarter, :] = low
    tall[quarter : 2 * quarter, :] = pltpu.roll(low, share, 1)
    tall[2 * quarter : 2 * quarter + rest, :] = high[:rest]
    tall[2 * quarter + rest : 2 * width, :] = pltpu.roll(high[:rest], share, 1)
    for tap in range(2):
        conv[tap] = tall[tap * width : (tap + 1) * width, :].T[:share]
    value = high[rest : rest + COND_ROWS // 2]
    blank = jnp.zeros((lanes - COND_ROWS, lanes), F32)
    cond[...] = jnp.concatenate([value, pltpu.roll(value, share, 1), blank], 0).T[:share, :mel_width]
    start = rest + COND_ROWS // 2
    value = high[start : start + width // 2]
    value = jnp.concatenate([value, pltpu.roll(value, lanes - share // 2, 1)], 0).T
    res[...] = value[: share // 2]
    skip[...] = value[share : share + share // 2]
    biases = high[start + width // 2 : start + width // 2 + 8]
    b_conv[...] = biases[0:1, :share]
    b_res[...] = biases[1:2, : share // 2]
    b_skip[...] = biases[1:2, share : share + share // 2]


def own_shares(place, width, mel_width, mine, near, cross, swap, waits):
    vmem = pl.BlockSpec(memory_space=pltpu.VMEM)
    share = mine.shape[1] // 2
    full = lambda *shape: jax.ShapeDtypeStruct(shape, F32)
    conv, cond, b_conv, res, b_res, skip, b_skip = pl.pallas_call(
        functools.partial(shares_kernel, width, mel_width),
        out_shape=[
            full(2, share, width), full(share, mel_width), full(1, share), full(share // 2, width),
            full(1, share // 2), full(share // 2, width), full(1, share // 2),
        ],
        in_specs=[pl.BlockSpec(memory_space=pltpu.SMEM)] + [vmem] * 4 + [pl.BlockSpec(memory_space=pl.ANY)],
        out_specs=[vmem] * 7,
        scratch_shapes=[pltpu.VMEM((2 * width, mine.shape[1]), F32)],
        compiler_params=pltpu.CompilerParams(vmem_limit_bytes=SMALL_VMEM_LIMIT),
        cost_estimate=LONG,
        name="own_shares",
    )(place, mine, near, cross, swap, *waits)
    return jnp.swapaxes(conv, 1, 2), cond.T, b_conv, res.T, b_res, skip.T, b_skip


def unfold(halves, width, mel_width):
    _, devices, quarter, lanes = halves.shape
    share = lanes // 2
    halves = halves.astype(F32)
    rest = width - quarter

    def stacked(block, group):
        split_lanes = block.reshape(block.shape[:2] + (lanes // (2 * group), 2, group))
        return jnp.moveaxis(split_lanes, 3, 1).reshape(devices, -1, lanes // 2)

    flat = lambda block: jnp.moveaxis(block, 0, 1).reshape(block.shape[1], -1)
    low, high = halves
    conv = jnp.concatenate([stacked(low, share), stacked(high[:, :rest], share)], 1)
    cond = stacked(high[:, rest : rest + COND_ROWS // 2], share)[:, :mel_width]
    start = rest + COND_ROWS // 2
    both = stacked(high[:, start : start + width // 2], share // 2)
    start = start + width // 2
    b_conv = high[:, start : start + 1, :share]
    b_res = high[:, start + 1 : start + 2, : share // 2]
    b_skip = high[:, start + 1 : start + 2, share : share + share // 2]
    parts = (conv, cond, b_conv, both[:, :, : share // 2], b_res, both[:, :, share // 2 :], b_skip)
    return [flat(part) for part in parts]


def on_device(
    samples, mel, clip_ids, valid, w_conv, w_cond, b_conv, w_res, b_res, w_skip, b_skip, cot_out, cot_skip
):
    section = lax.axis_index("section")
    position = lax.axis_index("tm")
    parts = lax.axis_size("tm")
    count, rows, width = samples.shape
    mel_width = mel.shape[-1]
    per = count // 2
    place = jnp.stack([section, position]).astype(jnp.int32)
    swap = [(0, 1), (1, 0)]
    swapped = lambda a: lax.ppermute(a, "section", swap)

    mel = jnp.swapaxes(mel, 1, 2)
    block, ends = first_halo(per, place, samples, mel, valid)
    forward = shift("tm", 1)
    halos = [lax.ppermute(block, "tm", forward)]
    twice = lax.ppermute(ends, "tm", shift("tm", 2))
    pack = pack_weights(w_conv[0].reshape(2 * width, 2 * width), w_cond, b_conv, w_res, b_res, w_skip, b_skip)
    packs = (pack, swapped(pack))
    *later, heads, side = prep(per, place, samples, mel, clip_ids, valid, cot_out, cot_skip, block)
    for block in later:
        block = lax.optimization_barrier((block, halos[-1]))[0]
        halos.append(lax.ppermute(block, "tm", forward))
    after = lax.ppermute(heads, "tm", shift("tm", -1))

    axes = ("section", "tm")
    pairs = range(per // 2)
    outs, received, near, far = [], [], [], []
    for pair in pairs:
        out = layers(
            pair, per, mel_width, place, samples, halos[pair], halos[0], side, after, twice, cot_out, cot_skip,
            packs, [outs[-1][5]] if outs else [], outs[-1][:2] if outs else [], [],
        )
        outs.append(out)
        near.append(lax.ppermute(out[4], "tm", shift("tm", -1)))
        if pair != pairs[-1]:
            received.append(swapped(out[2]))
    kept, sent = weight_sums(
        pairs[-1], per, place, samples, side, cot_out, cot_skip, outs[1][5], outs[0][6], outs[1][6:]
    )
    came = swapped(sent)
    act, skip = outs[-1][:2]

    def finished(pair, act, skip, grads, waits):
        return finish(pair, place, received[pair], outs[pair][3], near[pair], far[pair], act, skip, grads, waits)

    if parts == 16 and 2 * width // parts == sent.shape[-1] // 2:
        quarter, lanes = sent.shape[-2:]
        pieces = ((0, 144, "yxlh"), (144, 128, "lyxh"), (272, quarter - 272, "xlyh"))
        flips = lambda mask: [(i, i ^ mask) for i in range(parts)]
        sums = [array.reshape((2,) + (2,) * len(AXES) + (quarter, lanes)) for array in (kept, came)]
        terms = [[] for _ in pieces]
        token = after_all(sent, near[0], received[0])
        far.append(swapped(lax.optimization_barrier((near[0], token))[0]))
        for step in range(len(AXES) - 1):
            aways = halving_step(step, pieces, place, sums, terms, [token])
            token = aways[0]
            for (_, _, order), away, of_piece in zip(pieces, aways, terms):
                of_piece.append(lax.ppermute(away, "tm", flips(AXES[order[step]])))
            if step == 0:
                act, skip, grads, token = finished(0, act, skip, None, [token])
                forward, back = lax.optimization_barrier((outs[-1][2], near[1], token))[:2]
                received.append(swapped(forward))
                far.append(swapped(back))
            if step == 1:
                act, skip, grads, token = finished(1, act, skip, grads, [token])
        near_sum, cross_sum, swap_sum, mine = last_step(pieces, place, sums, terms)
        mask = AXES["h"]
        crossed = [(s * parts + i, (1 - s) * parts + (i ^ mask)) for s in range(2) for i in range(parts)]
        near_sum, cross_sum, swap_sum = (
            lax.ppermute(near_sum, "tm", flips(mask)), lax.ppermute(cross_sum, axes, crossed), swapped(swap_sum)
        )
        shares = own_shares(place, width, mel_width, mine, near_sum, cross_sum, swap_sum, [token])
    else:
        received.append(swapped(outs[-1][2]))
        far.extend(swapped(back) for back in near)
        act, skip, grads, _ = finished(0, act, skip, None, [])
        act, skip, grads, _ = finished(1, act, skip, grads, [])
        total = (kept.astype(F32) + came.astype(F32)).astype(BF16)
        mine = jnp.where(section == 0, total[0], total[1])
        got = swapped(jnp.where(section == 0, total[1], total[0]))
        low = jnp.where(section == 0, mine, got)
        high = jnp.where(section == 0, got, mine)
        shares = [
            lax.psum_scatter(part, "tm", scatter_dimension=1, tiled=True)
            for part in unfold(jnp.stack([low, high]), width, mel_width)
        ]
    conv, cond, g_conv, res, g_res, skip_w, g_skip = shares
    flat = lambda a: a.reshape(1, count, rows, width)
    return (
        flat(act),
        flat(skip),
        flat(grads),
        conv.reshape(1, 2, width, -1),
        cond[None],
        g_conv,
        res[None],
        g_res,
        skip_w[None],
        g_skip,
    )


def solution(mesh):
    placed = (
        P(None, "tm", None),
        P(None, "tm", None),
        P(),
        P(None, "tm"),
        P("section", None, None, None),
        P("section", None, None),
        P("section", None),
        P("section", None, None),
        P("section", None),
        P("section", None, None),
        P("section", None),
        P(None, "tm", None),
        P(None, "tm", None),
    )
    return jax.shard_map(
        on_device,
        mesh=mesh,
        in_specs=placed,
        out_specs=(
            P("section", None, "tm", None),
            P("section", None, "tm", None),
            P("section", None, "tm", None),
            P("section", None, None, "tm"),
            P("section", None, "tm"),
            P("section", "tm"),
            P("section", None, "tm"),
            P("section", "tm"),
            P("section", None, "tm"),
            P("section", "tm"),
        ),
        check_vma=False,
    )
```
